256 devices in a mesh: lon: 16 (over y_hi, z), lat: 16 (over x, y_lo, core).
Axes of the slice: x: 4, y: 4 (y_hi: 2, y_lo: 2; y = y_hi * 2 + y_lo), z: 8, core: 2. Of those that a mesh axis runs over, the one named last changes fastest.
Arguments:
- inputs: bfloat16 [4, 96, 192, 192], P(None, 'lat', 'lon'), may hold values from -36 to 36
- grad_out: bfloat16 [4, 96, 192, 192], P(None, 'lat', 'lon'), may hold values from -6 to 6
- region: int32 [4, 96, 192], P(None, 'lat', 'lon'), may hold values from 0 to 2
- bias_level: int32 [2, 16], P(None, 'lat'), may hold values from 0 to 1
- norm_gains: float32 [2, 2, 192], replicated, may hold values from 0.1 to 1.9
- in_weight: bfloat16 [2, 192, 576], replicated, may hold values from -0.4375 to 0.4375
- out_weight: bfloat16 [2, 192, 192], replicated, may hold values from -0.4375 to 0.4375
- up_weight: bfloat16 [2, 192, 768], replicated, may hold values from -0.4375 to 0.4375
- down_weight: bfloat16 [2, 768, 192], replicated, may hold values from -0.21875 to 0.21875
- bias_tables: bfloat16 [2, 16, 2, 6, 3312], P(None, 'lat'), may hold values from -2.5 to 301
Outputs:
- blocks_out: bfloat16 [4, 96, 192, 192], P(None, 'lat', 'lon')
- grad_inputs: bfloat16 [4, 96, 192, 192], P(None, 'lat', 'lon')
- grad_gains: float32 [2, 2, 192], replicated
- grad_in_weight: float32 [2, 192, 576], replicated
- grad_out_weight: float32 [2, 192, 192], replicated
- grad_up_weight: float32 [2, 192, 768], replicated
- grad_down_weight: float32 [2, 768, 192], replicated
- grad_tables: float32 [2, 16, 2, 6, 3312], P(None, 'lat')
The draws below stay inside these ranges and needn't reach their ends.
Inputs may be any that keep to these rules, and one draw needn't show every extreme that they name: A token of the shifted block attends only to tokens of its window with the same region id.
All inputs are finite; a program needn't handle non-finite values.
Results may differ from the reference program's by a relative error of at most 0.028.
Values may be sent and summed in bfloat16 or wider, within the bound.
No kernel may reach another device: no remote copies, remote signals or barrier semaphores. Data moves between devices by JAX's collectives and lax.ppermute only.
A program may use at most 64 MiB of HBM per device.

```python
import math
import jax
import jax.numpy as jnp
from jax import lax

C = 192
HEADS = 6
HEAD = 32
FFN = 768
WIN_Z = 2
WIN_LAT = 6
WIN_LON = 12
WIN = 144
RELPOS = 3312
LEVELS = 4
LAT = 96
LON = 192
LATW = 16
LEVW = 2


def draw_inputs(key, part):
    key = jax.random.fold_in(key, 11)
    key_base, key_rows, key_cols = jax.random.split(key, 3)
    full_shape = (LEVELS, LAT, LON, C)
    row_scale = jnp.exp(jax.random.uniform(key_rows, (LEVELS, LAT, LON, 1), jnp.float32, -1.2, 1.09))
    col_scale = jnp.exp(jax.random.uniform(key_cols, (C,), jnp.float32, -1.2, 1.09))
    drawn = jax.random.truncated_normal(key_base, -4.0, 4.0, full_shape, jnp.float32)
    return jnp.clip(drawn * row_scale * col_scale, -36.0, 36.0).astype(jnp.bfloat16)


def draw_bias_tables(key, part):
    key = jax.random.fold_in(key, 23)
    key_base = jax.random.fold_in(key, 0)
    full_shape = (2, LATW, LEVW, HEADS, RELPOS)
    drawn = 0.5 * jax.random.truncated_normal(key_base, -5.0, 5.0, full_shape, jnp.float32)
    return drawn.astype(jnp.bfloat16)


def plant(values, stream_key, low, largest):
    longest = values.shape.index(max(values.shape))
    spots = []
    for shift in (0, 1):
        where = [jax.random.randint(jax.random.fold_in(stream_key, axis), (), 0, length) for axis, length in enumerate(values.shape)]
        where[longest] = (where[longest] + shift) % values.shape[longest]
        spots.append(tuple(where))
    return values.at[spots[0]].set(low).at[spots[1]].set(largest)


def block_levels(own_key, shape, cuts, low, high):
    level = 1.0
    for position, parts in cuts:
        draws = jax.random.uniform(jax.random.fold_in(jax.random.fold_in(own_key, 6), position), (parts,), jnp.float32, low / len(cuts), high / len(cuts))
        level = level * jnp.repeat(jnp.exp(draws), shape[position] // parts).reshape((-1,) + (1,) * (len(shape) - 1 - position))
    return level


def gaussian(stream_key, shape, deviation, bound, shards=(), kind=jnp.bfloat16):
    factor_of = block_levels(stream_key, shape, shards, -0.22, 0.18) if shards else 1.0
    result = jax.random.normal(stream_key, shape, jnp.float32) * deviation * factor_of
    return jnp.minimum(jnp.maximum(result, -bound), bound).astype(kind)


def setup_inputs(seed: int = 0) -> dict:
    key_of = jax.random.split(jax.random.key(seed), 11)
    inputs = draw_inputs(jax.random.fold_in(key_of[10], 71), 0)
    grad_out = gaussian(key_of[1], (LEVELS, LAT, LON, C), 1.0, 6.0, ((1, 16), (2, 16)))
    region = plant(jax.random.randint(key_of[2], (LEVELS, LAT, LON), 0, 3), jax.random.fold_in(key_of[2], 1), 0, 2).astype(jnp.int32)
    bias_level = plant(jax.random.randint(key_of[3], (LEVW, LATW), 0, LEVW), jax.random.fold_in(key_of[3], 1), 0, LEVW - 1).astype(jnp.int32)
    norm_gains = jnp.clip(1.0 + 0.18 * jax.random.normal(key_of[4], (2, 2, C), jnp.float32), 0.1, 1.9)
    in_weight = gaussian(key_of[5], (2, C, 3 * C), C ** -0.5, 0.4375)
    out_weight = gaussian(key_of[6], (2, C, C), C ** -0.5, 0.4375)
    up_weight = gaussian(key_of[7], (2, C, FFN), C ** -0.5, 0.4375)
    down_weight = gaussian(key_of[8], (2, FFN, C), FFN ** -0.5, 0.21875)
    bias_tables = draw_bias_tables(jax.random.fold_in(key_of[10], 71), 0)
    return {"inputs": inputs, "grad_out": grad_out, "region": region, "bias_level": bias_level, "norm_gains": norm_gains, "in_weight": in_weight, "out_weight": out_weight, "up_weight": up_weight, "down_weight": down_weight, "bias_tables": bias_tables}


EPSILON = 1e-05
NEGATIVE = -1000000000.0

def to_windows(grid_in):
    level_count, lat_count, lon_count = (grid_in.shape[0], grid_in.shape[1], grid_in.shape[2])
    trailing = tuple(grid_in.shape[3:])
    shaped = grid_in.reshape((level_count // WIN_Z, WIN_Z, lat_count // WIN_LAT, WIN_LAT, lon_count // WIN_LON, WIN_LON) + trailing)
    layout = (0, 2, 4, 1, 3, 5) + tuple(range(6, 6 + len(trailing)))
    return shaped.transpose(layout).reshape((-1, WIN) + trailing)

def from_windows(windows, level_count, lat_count, lon_count):
    trailing = tuple(windows.shape[2:])
    shaped = windows.reshape((level_count // WIN_Z, lat_count // WIN_LAT, lon_count // WIN_LON, WIN_Z, WIN_LAT, WIN_LON) + trailing)
    layout = (0, 3, 1, 4, 2, 5) + tuple(range(6, 6 + len(trailing)))
    return shaped.transpose(layout).reshape((level_count, lat_count, lon_count) + trailing)

def relative_index():
    window_slot = jnp.arange(WIN, dtype=jnp.int32)
    level_pos = window_slot // (WIN_LAT * WIN_LON)
    row_pos = window_slot // WIN_LON % WIN_LAT
    col_pos = window_slot % WIN_LON
    rel_index = ((level_pos[:, None] * WIN_Z + level_pos[None, :]) * WIN_LAT + row_pos[:, None]) * WIN_LAT + row_pos[None, :]
    rel_index = rel_index * (2 * WIN_LON - 1) + col_pos[:, None] - col_pos[None, :] + WIN_LON - 1
    return rel_index.reshape(-1).astype(jnp.int32)

def selector(bias_level, window_count, latitude_window_count, lon_windows):
    level_windows = bias_level.shape[0]
    window_ids = jnp.arange(window_count, dtype=jnp.int32)
    level_win = window_ids // (latitude_window_count * lon_windows)
    lat_win = window_ids // lon_windows % latitude_window_count
    flat_key = level_win * latitude_window_count + lat_win
    table_keys = jnp.arange(level_windows * latitude_window_count, dtype=jnp.int32)
    chosen = lax.optimization_barrier(jnp.sum(jnp.where(table_keys[None, :] == flat_key[:, None], bias_level.reshape(-1)[None, :], 0), axis=1)).astype(jnp.int32)
    target = lat_win * level_windows + chosen
    row_keys = jnp.arange(latitude_window_count * level_windows, dtype=jnp.int32)
    return (row_keys[None, :] == target[:, None]).astype(jnp.float32)

def layer_norm(flat_values, gain):
    centre = flat_values - lax.optimization_barrier(jnp.mean(flat_values, axis=-1, keepdims=True))
    inverse = lax.rsqrt(lax.optimization_barrier(jnp.mean(centre * centre, axis=-1, keepdims=True)) + EPSILON)
    normal_hat = centre * inverse
    return (normal_hat * gain, normal_hat, inverse)

def norm_backward(upstream, normal_hat, inverse):
    upstream_mean = lax.optimization_barrier(jnp.mean(upstream, axis=-1, keepdims=True))
    cross_mean = lax.optimization_barrier(jnp.mean(upstream * normal_hat, axis=-1, keepdims=True))
    return inverse * (upstream - upstream_mean - normal_hat * cross_mean)

def gelu_exact(expanded):
    return expanded * 0.5 * (1.0 + jax.scipy.special.erf(expanded / math.sqrt(2.0)))

def gelu_slope(expanded):
    cumulative = 0.5 * (1.0 + jax.scipy.special.erf(expanded / math.sqrt(2.0)))
    return cumulative + expanded * jnp.exp(-0.5 * expanded * expanded) / math.sqrt(2.0 * math.pi)

def window_forward(block_in, gain_pair, in_w, out_w, up_w, down_w, bias_rows, region_win):
    window_count = block_in.shape[0]
    flat_in = block_in.astype(jnp.float32).reshape(-1, C)
    normed, first_hat, first_inv = layer_norm(flat_in, gain_pair[0].astype(jnp.float32))
    first_norm = normed.astype(jnp.bfloat16)
    projected = jnp.dot(first_norm, in_w, preferred_element_type=jnp.float32).astype(jnp.bfloat16)
    projected = projected.reshape(window_count, WIN, 3, HEADS, HEAD)
    queries, key_vecs, values = (projected[:, :, 0], projected[:, :, 1], projected[:, :, 2])
    score_scale = 1.0 / math.sqrt(HEAD)
    bias_full = jnp.take(bias_rows.astype(jnp.float32), relative_index(), axis=2).reshape(window_count, HEADS, WIN, WIN)
    scores = jnp.einsum('nahd,nbhd->nhab', queries.astype(jnp.float32), key_vecs.astype(jnp.float32)) * score_scale + bias_full
    if region_win is not None:
        same_region = region_win[:, None, :, None] == region_win[:, None, None, :]
        scores = jnp.where(same_region, scores, NEGATIVE)
    top_score = lax.optimization_barrier(jnp.max(scores, axis=-1, keepdims=True))
    exp_scores = jnp.exp(scores - top_score)
    attend = exp_scores / lax.optimization_barrier(jnp.sum(exp_scores, axis=-1, keepdims=True))
    attend_half = attend.astype(jnp.bfloat16)
    mixed_heads = jnp.einsum('nhab,nbhd->nahd', attend_half.astype(jnp.float32), values.astype(jnp.float32)).astype(jnp.bfloat16)
    mixed_heads = mixed_heads.reshape(-1, C)
    hidden_one = (flat_in + jnp.dot(mixed_heads, out_w, preferred_element_type=jnp.float32)).astype(jnp.bfloat16)
    normed_two, second_hat, second_inv = layer_norm(hidden_one.astype(jnp.float32), gain_pair[1].astype(jnp.float32))
    second_norm = normed_two.astype(jnp.bfloat16)
    expanded = jnp.dot(second_norm, up_w, preferred_element_type=jnp.float32)
    activated = gelu_exact(expanded).astype(jnp.bfloat16)
    block_out = (hidden_one.astype(jnp.float32) + jnp.dot(activated, down_w, preferred_element_type=jnp.float32)).astype(jnp.bfloat16)
    stored = (first_hat, first_inv, first_norm, queries, key_vecs, values, attend, attend_half, mixed_heads, hidden_one, second_hat, second_inv, second_norm, expanded, activated)
    return (block_out.reshape(window_count, WIN, C), stored)

def window_backward(stored, grad_windows, gain_pair, in_w, out_w, up_w, down_w):
    first_hat, first_inv, first_norm, queries, key_vecs, values, attend, attend_half, mixed_heads, hidden_one, second_hat, second_inv, second_norm, expanded, activated = stored
    window_count = queries.shape[0]
    score_scale = 1.0 / math.sqrt(HEAD)
    contract_rows = (((0,), (0,)), ((), ()))
    contract_cols = (((1,), (1,)), ((), ()))
    grad_flat = grad_windows.reshape(-1, C)
    grad_down = lax.dot_general(activated, grad_flat, contract_rows, preferred_element_type=jnp.float32)
    grad_act = lax.dot_general(grad_flat, down_w, contract_cols, preferred_element_type=jnp.float32)
    grad_expanded = (grad_act * gelu_slope(expanded)).astype(jnp.bfloat16)
    grad_up = lax.dot_general(second_norm, grad_expanded, contract_rows, preferred_element_type=jnp.float32)
    grad_second = lax.dot_general(grad_expanded, up_w, contract_cols, preferred_element_type=jnp.float32)
    gain_two = lax.optimization_barrier(jnp.sum(grad_second * second_hat, axis=0))
    grad_hidden = (grad_flat.astype(jnp.float32) + norm_backward(grad_second * gain_pair[1].astype(jnp.float32), second_hat, second_inv)).astype(jnp.bfloat16)
    grad_out_w = lax.dot_general(mixed_heads, grad_hidden, contract_rows, preferred_element_type=jnp.float32)
    grad_mixed = lax.dot_general(grad_hidden, out_w, contract_cols, preferred_element_type=jnp.float32).astype(jnp.bfloat16)
    grad_mixed = grad_mixed.reshape(window_count, WIN, HEADS, HEAD)
    grad_attend = jnp.einsum('nahd,nbhd->nhab', grad_mixed.astype(jnp.float32), values.astype(jnp.float32))
    grad_values = jnp.einsum('nhab,nahd->nbhd', attend_half.astype(jnp.float32), grad_mixed.astype(jnp.float32)).astype(jnp.bfloat16)
    grad_scores = attend * (grad_attend - lax.optimization_barrier(jnp.sum(grad_attend * attend, axis=-1, keepdims=True)))
    flat_scores = grad_scores.reshape(window_count * HEADS, WIN * WIN).T
    grad_rows = jax.ops.segment_sum(flat_scores, relative_index(), num_segments=RELPOS).T.reshape(window_count, HEADS, RELPOS)
    grad_scaled = (grad_scores * score_scale).astype(jnp.bfloat16)
    grad_queries = jnp.einsum('nhab,nbhd->nahd', grad_scaled.astype(jnp.float32), key_vecs.astype(jnp.float32)).astype(jnp.bfloat16)
    grad_keys = jnp.einsum('nhab,nahd->nbhd', grad_scaled.astype(jnp.float32), queries.astype(jnp.float32)).astype(jnp.bfloat16)
    grad_projected = jnp.stack([grad_queries, grad_keys, grad_values], axis=2).reshape(-1, 3 * C)
    grad_in_w = lax.dot_general(first_norm, grad_projected, contract_rows, preferred_element_type=jnp.float32)
    grad_first = lax.dot_general(grad_projected, in_w, contract_cols, preferred_element_type=jnp.float32)
    gain_one = lax.optimization_barrier(jnp.sum(grad_first * first_hat, axis=0))
    grad_block_in = (grad_hidden.astype(jnp.float32) + norm_backward(grad_first * gain_pair[0].astype(jnp.float32), first_hat, first_inv)).astype(jnp.bfloat16)
    weight_gradients = (jnp.stack([gain_one, gain_two]), grad_in_w, grad_out_w, grad_up, grad_down)
    return (grad_block_in.reshape(window_count, WIN, C), weight_gradients, grad_rows)

def block_setup(grid_in, bias_level, table, region):
    windows = to_windows(grid_in)
    window_count = windows.shape[0]
    picker = selector(bias_level, window_count, grid_in.shape[1] // WIN_LAT, grid_in.shape[2] // WIN_LON)
    bias_rows = jnp.dot(picker.astype(jnp.bfloat16), table.reshape(-1, HEADS * RELPOS), preferred_element_type=jnp.float32)
    bias_rows = bias_rows.astype(jnp.bfloat16).reshape(window_count, HEADS, RELPOS)
    if region is None:
        region_win = jnp.zeros((window_count, WIN), jnp.int32)
    else:
        region_win = to_windows(region)
    return (windows, picker, bias_rows, region_win)

def grouped(array_in, group_size):
    return array_in.reshape((-1, group_size) + tuple(array_in.shape[1:]))

def block_forward(grid_in, params, bias_level, table):
    windows, picker, bias_rows, region_win = block_setup(grid_in, bias_level, table, None)
    group_size = math.gcd(windows.shape[0], 16)

    def window_step(pieces):
        return window_forward(pieces[0], *params, pieces[1], None)[0]
    outputs = lax.map(window_step, (grouped(windows, group_size), grouped(bias_rows, group_size)))
    return from_windows(outputs.reshape(-1, WIN, C), grid_in.shape[0], grid_in.shape[1], grid_in.shape[2])

def block_train(grid_in, grad_grid, params, bias_level, table, region):
    windows, picker, bias_rows, region_win = block_setup(grid_in, bias_level, table, region)
    grad_windows = to_windows(grad_grid)
    group_size = math.gcd(windows.shape[0], 16)
    masked = region is not None

    def window_step(grand_totals, pieces):
        win_in, grad_win, rows_in, region_in, picker_in = pieces
        outputs, stored = window_forward(win_in, *params, rows_in, region_in if masked else None)
        grad_in, weight_gradients, grad_rows = window_backward(stored, grad_win, *params)
        table_contribution = lax.dot_general(picker_in, grad_rows.reshape(grad_rows.shape[0], -1), (((0,), (0,)), ((), ())), precision=lax.Precision.HIGHEST, preferred_element_type=jnp.float32)
        summand_terms = weight_gradients + (table_contribution,)
        grand_totals = tuple((running_total + summand_term for running_total, summand_term in zip(grand_totals, summand_terms)))
        return (grand_totals, (outputs, grad_in))
    init = (jnp.zeros((2, C), jnp.float32), jnp.zeros((C, 3 * C), jnp.float32), jnp.zeros((C, C), jnp.float32), jnp.zeros((C, FFN), jnp.float32), jnp.zeros((FFN, C), jnp.float32), jnp.zeros((picker.shape[1], HEADS * RELPOS), jnp.float32))
    pieces = (grouped(windows, group_size), grouped(grad_windows, group_size), grouped(bias_rows, group_size), grouped(region_win, group_size), grouped(picker, group_size))
    grand_totals, (outputs, grad_ins) = lax.scan(window_step, init, pieces)
    level_count, lat_count, lon_count = (grid_in.shape[0], grid_in.shape[1], grid_in.shape[2])
    grid_out = from_windows(outputs.reshape(-1, WIN, C), level_count, lat_count, lon_count)
    grid_grad = from_windows(grad_ins.reshape(-1, WIN, C), level_count, lat_count, lon_count)
    return (grid_out, grid_grad, grand_totals[:5], grand_totals[5].reshape(table.shape))

def reference(inputs, grad_out, region, bias_level, norm_gains, in_weight, out_weight, up_weight, down_weight, bias_tables):
    shifts = (WIN_Z // 2, WIN_LAT // 2, WIN_LON // 2)
    ahead = (-(WIN_Z // 2), -(WIN_LAT // 2), -(WIN_LON // 2))
    params_first = (norm_gains[0], in_weight[0], out_weight[0], up_weight[0], down_weight[0])
    params_second = (norm_gains[1], in_weight[1], out_weight[1], up_weight[1], down_weight[1])
    first_out = block_forward(inputs, params_first, bias_level, bias_tables[0])
    rolled = jnp.roll(first_out, ahead, axis=(0, 1, 2))
    rolled_grad = jnp.roll(grad_out, ahead, axis=(0, 1, 2))
    second_out, second_grad, second_totals, second_table = block_train(rolled, rolled_grad, params_second, bias_level, bias_tables[1], region)
    blocks_out = jnp.roll(second_out, shifts, axis=(0, 1, 2))
    first_grad = jnp.roll(second_grad, shifts, axis=(0, 1, 2))
    unused_out, grad_inputs, first_totals, first_table = block_train(inputs, first_grad, params_first, bias_level, bias_tables[0], None)
    stacked = [jnp.stack([first_totals[index_b], second_totals[index_b]]) for index_b in range(5)]
    grad_tables = jnp.stack([first_table, second_table])
    return (blocks_out, grad_inputs, stacked[0], stacked[1], stacked[2], stacked[3], stacked[4], grad_tables)
```

```python
import functools
import math

import jax
import jax.numpy as jnp
import numpy as np
from jax import lax
from jax.experimental import pallas as pl
from jax.experimental.pallas import tpu as pltpu
from jax.sharding import PartitionSpec as P

C = 192
HEADS = 6
HEAD = 32
FFN = 768
WIN_Z = 2
WIN_LAT = 6
WIN_LON = 12
WIN = 144
TOKENS = 2 * WIN
QUAD = 72
RELPOS = 3312
SPAN = 2 * WIN_LON - 1
ROWS = 3584
GAIN_ROWS = 3456
TABLE_ROWS = 320

EPSILON = 1e-05
NEGATIVE = -1000000000.0
SCALE = 1.0 / math.sqrt(HEAD)

F32 = jnp.float32
BF16 = jnp.bfloat16


def quadrant_rows():
    rows = np.zeros(TOKENS, np.int64)
    at = 0
    for lat_half in range(2):
        for lon_half in range(2):
            for level in range(4):
                for row in range(3):
                    for col in range(6):
                        rows[at] = (level * 6 + lat_half * 3 + row) * 12 + lon_half * 6 + col
                        at += 1
    return rows


def rolled_rows():
    rows = quadrant_rows()
    level, rest = rows // 72, rows % 72
    return ((level + 3) % 4) * 72 + rest


def one_hot(rows):
    picked = np.zeros((TOKENS, TOKENS), np.float32)
    picked[np.arange(TOKENS), rows] = 1.0
    return picked


def pair_keys():
    keys = np.full((512, 256), -1.0, np.float32)
    for level in range(2):
        for row in range(6):
            for offset in range(SPAN):
                for col in range(12):
                    key = col + 11 - offset
                    if 0 <= key < 12:
                        keys[level * 256 + row // 3 * 128 + row % 3 * SPAN + offset, level * 72 + row * 12 + col] = key
    return keys


def mm(left, right):
    return lax.dot_general(left, right, (((1,), (0,)), ((), ())), preferred_element_type=F32)


def mm_nt(left, right):
    return lax.dot_general(left, right, (((1,), (1,)), ((), ())), preferred_element_type=F32)


def eye(size):
    return (
        lax.broadcasted_iota(jnp.int32, (size, size), 0) == lax.broadcasted_iota(jnp.int32, (size, size), 1)
    ).astype(F32).astype(BF16)


def turned(value):
    return mm_nt(eye(value.shape[1]), value).astype(BF16)


def norm_stats(values):
    centre = values - jnp.mean(values, axis=-1, keepdims=True)
    inverse = lax.rsqrt(jnp.mean(centre * centre, axis=-1, keepdims=True) + EPSILON)
    return centre * inverse, inverse


def norm_backward(upstream, normal_hat, inverse):
    upstream_mean = jnp.mean(upstream, axis=-1, keepdims=True)
    cross_mean = jnp.mean(upstream * normal_hat, axis=-1, keepdims=True)
    return inverse * (upstream - upstream_mean - normal_hat * cross_mean)


def head_lanes(head):
    lane = lax.broadcasted_iota(jnp.int32, (1, C), 1)
    return (lane >= head * HEAD) & (lane < (head + 1) * HEAD)


def make_pairs(keys_ref, pairs_ref):
    keys = keys_ref[...]
    for col in range(WIN_LON):
        pairs_ref[col] = jnp.where(keys == float(col), 1.0, 0.0).astype(BF16)


def table_start(zs, zt, hs, ht):
    return (((zs * 2 + zt) * 6 + hs) * 6 + ht) * SPAN


def spread_bias(table_ref, pairs_ref, row_ref, shaped_ref, bias_ref):
    for head in range(HEADS):
        row_ref[head * 2 : head * 2 + 2, :RELPOS] = table_ref[head].astype(F32)
    row = row_ref[: 2 * HEADS]
    for zs in range(2):
        for zt in range(2):
            for group in range(2):
                for ht in range(6):
                    pieces = []
                    for hs in range(group * 3, group * 3 + 3):
                        start = table_start(zs, zt, hs, ht)
                        pieces.append(row[:, start : start + SPAN])
                    pieces.append(jnp.zeros((2 * HEADS, 128 - 3 * SPAN), F32))
                    target = pl.ds(zt * 6 + ht, 2 * HEADS, stride=12)
                    shaped_ref[zs * 2 + group, target, :] = jnp.concatenate(pieces, axis=1)
    shaped = jnp.concatenate([shaped_ref[part, :WIN].astype(BF16) for part in range(4)], axis=1)
    for col in range(WIN_LON):
        spread = mm(shaped, pairs_ref[col])
        bias_ref[0, pl.ds(col, WIN, stride=12), :] = spread[:, :128]
        bias_ref[1, pl.ds(col, WIN, stride=12), :] = spread[:, 128:]


def collect_bias(grads_ref, pairs_ref, levels, row_ref, shaped_ref, out_ref):
    for window in range(2):
        total = jnp.zeros((72, 512), F32)
        for col in range(WIN_LON):
            left = grads_ref[window, 0, pl.ds(col, 72, stride=12), :]
            right = grads_ref[window, 1, pl.ds(col, 72, stride=12), :]
            piece = jnp.concatenate([left, right], axis=1).astype(BF16)
            total = total + mm_nt(piece, pairs_ref[col])
        for part in range(4):
            shaped_ref[part, window * 72 : (window + 1) * 72] = total[:, part * 128 : (part + 1) * 128]
    row_ref[...] = jnp.zeros_like(row_ref)
    for zs in range(2):
        for zt in range(2):
            for group in range(2):
                for ht in range(6):
                    pieces = [
                        shaped_ref[zs * 2 + group, pl.ds(window * 72 + zt * 6 + ht, HEADS, stride=12), :]
                        for window in range(2)
                    ]
                    for level in range(2):
                        chosen = jnp.zeros((HEADS, 128), F32)
                        for window in range(2):
                            chosen = chosen + jnp.where(levels[window] == level, pieces[window], 0.0)
                        for index in range(3):
                            start = table_start(zs, zt, group * 3 + index, ht)
                            row_ref[level * 8 : level * 8 + HEADS, start : start + SPAN] = chosen[
                                :, index * SPAN : (index + 1) * SPAN
                            ]
    for slab in range(26):
        lanes = slice(slab * 128, (slab + 1) * 128)
        rows = jnp.concatenate([row_ref[:HEADS, lanes], row_ref[8 : 8 + HEADS, lanes]], axis=0)
        shaped_ref[slab // 13, slab % 13 * 12 : slab % 13 * 12 + 12] = rows
    out_ref[...] = jnp.concatenate(
        [shaped_ref[0, :156], shaped_ref[1, :156], jnp.zeros((TABLE_ROWS - 312, 128), F32)], axis=0
    ).astype(BF16)


def load_tiles(bias_ref, level, head):
    rows = pl.ds(pl.multiple_of((head * 2 + level) * WIN, 8), WIN)
    return jnp.concatenate([bias_ref[0, rows, :], bias_ref[1, rows, : WIN - 128]], axis=1)


def attention(normed, in_weight, bias_ref, levels, same_region, weights_ref):
    eye_c = eye(C)
    weight_q, weight_k, weight_v = in_weight[:, :C], in_weight[:, C : 2 * C], in_weight[:, 2 * C :]
    kept = []
    mixed = []
    for window in range(2):
        rows = normed[window * WIN : (window + 1) * WIN]
        keys = mm(rows, weight_k).astype(BF16)
        values = mm(rows, weight_v).astype(BF16)
        queries = mm(rows, weight_q).astype(BF16)
        queries_t = mm_nt(eye_c, queries).astype(BF16)
        keys_t = mm_nt(eye_c, keys).astype(BF16)
        values_t = mm_nt(eye_c, values).astype(BF16)
        parts = []
        for head in range(HEADS):
            own = jnp.where(head_lanes(head), keys.astype(F32), 0.0).astype(BF16)
            scores = mm(own, queries_t) * SCALE + load_tiles(bias_ref, levels[window], head)
            if same_region is not None:
                scores = jnp.where(same_region[window], scores, NEGATIVE)
            weights = jnp.exp(scores - jnp.max(scores, axis=0, keepdims=True))
            weights = weights * (1.0 / jnp.sum(weights, axis=0, keepdims=True))
            weights = weights.astype(BF16)
            weights_ref[window * HEADS + head] = weights
            parts.append(mm(values_t[head * HEAD : (head + 1) * HEAD], weights))
        mixed.append(jnp.concatenate(parts, axis=0).astype(BF16))
        kept.append((queries_t, keys_t, values))
    return kept, mixed


def feed_forward(hidden, gain, up_weight):
    hat, inverse = norm_stats(hidden)
    normed = (hat * gain).astype(BF16)
    return hat, inverse, normed, mm(normed, up_weight)


def gelu_parts(expanded):
    cumulative = 0.5 * (1.0 + lax.erf(expanded * (1.0 / math.sqrt(2.0))))
    slope = cumulative + expanded * jnp.exp(-0.5 * expanded * expanded) * (1.0 / math.sqrt(2.0 * math.pi))
    return (expanded * cumulative).astype(BF16), slope


def natural_mixed(mixed):
    eye_w = eye(WIN)
    return jnp.concatenate([mm_nt(eye_w, part) for part in mixed], axis=0).astype(BF16)


def pack(packed_ref, start, value):
    height = value.shape[0]
    for part in range(value.shape[1] // 128):
        rows = slice(start + part * height, start + (part + 1) * height)
        packed_ref[rows] = value[:, part * 128 : (part + 1) * 128].astype(BF16)


def backward(
    grad,
    active,
    slope,
    second_hat,
    second_inverse,
    second_norm,
    mixed,
    attended,
    weights_ref,
    first_hat,
    first_inverse,
    first_norm,
    gain_one,
    gain_two,
    in_weight,
    out_weight,
    up_weight,
    down_weight,
    grads_ref,
    packed_ref,
):
    eye_c = eye(C)
    grad_half = grad.astype(BF16)
    pack(packed_ref, 2304, mm(turned(grad_half), active))
    grad_expanded = (mm(grad_half, down_weight) * slope).astype(BF16)
    normed_t = turned(second_norm)
    pack(packed_ref, 1152, mm(normed_t, grad_expanded))
    grad_second = mm_nt(grad_expanded, up_weight)
    gain_two_grad = jnp.sum(grad_second * second_hat, axis=0, keepdims=True)
    grad_hidden = (grad + norm_backward(grad_second * gain_two, second_hat, second_inverse)).astype(BF16)
    grad_out = mm(mixed[0], grad_hidden[:WIN]) + mm(mixed[1], grad_hidden[WIN:])
    packed_ref[960:1152] = grad_out[:, :128].astype(BF16)
    grad_mixed = mm_nt(grad_hidden, out_weight).astype(BF16)
    projected = []
    for window in range(2):
        queries_t, keys_t, values = attended[window]
        upstream_t = mm_nt(eye_c, grad_mixed[window * WIN : (window + 1) * WIN]).astype(BF16)
        grad_q, grad_k, grad_v = [], [], []
        for head in range(HEADS):
            lanes = slice(head * HEAD, (head + 1) * HEAD)
            half = weights_ref[window * HEADS + head]
            weights = half.astype(F32)
            own = jnp.where(head_lanes(head), values.astype(F32), 0.0).astype(BF16)
            grad_weights = mm(own, upstream_t)
            inner = jnp.sum(grad_weights * weights, axis=0, keepdims=True)
            grad_scores = weights * (grad_weights - inner)
            rows = slice(head * WIN, (head + 1) * WIN)
            grads_ref[window, 0, rows, :] = grad_scores[:, :128]
            grads_ref[window, 1, rows, :] = jnp.concatenate(
                [grad_scores[:, 128:], jnp.zeros((WIN, 256 - WIN), F32)], axis=1
            )
            scaled = (grad_scores * SCALE).astype(BF16)
            grad_v.append(mm_nt(upstream_t[lanes], half))
            grad_q.append(mm(keys_t[lanes], scaled))
            grad_k.append(mm_nt(queries_t[lanes], scaled))
        projected_t = jnp.concatenate(grad_q + grad_k + grad_v, axis=0).astype(BF16)
        projected.append(mm_nt(eye(WIN), projected_t))
    projected = jnp.concatenate(projected, axis=0).astype(BF16)
    first_t = turned(first_norm)
    grad_in = mm(first_t, projected)
    pack(packed_ref, 0, grad_in[:, :512])
    packed_ref[768:960] = jnp.concatenate([grad_in[:, 512:], grad_out[:, 128:]], axis=1).astype(BF16)
    grad_first = mm_nt(projected, in_weight)
    gain_one_grad = jnp.sum(grad_first * first_hat, axis=0, keepdims=True)
    gain_rows = jnp.concatenate(
        [
            gain_one_grad[:, :128],
            jnp.concatenate([gain_one_grad[:, 128:], gain_two_grad[:, 128:]], axis=1),
            gain_two_grad[:, :128],
            jnp.zeros((ROWS - GAIN_ROWS - 3, 128), F32),
        ],
        axis=0,
    )
    packed_ref[GAIN_ROWS:ROWS] = gain_rows.astype(BF16)
    return (
        grad_hidden.astype(F32) + norm_backward(grad_first * gain_one, first_hat, first_inverse)
    ).astype(BF16)


def load_grid(grid_ref, rows_ref):
    for row in range(6):
        for col in range(12):
            piece = grid_ref[row, col].astype(F32)
            target = pl.ds(row * 12 + col, 4, stride=72)
            rows_ref[0, target, :] = piece[:, :128]
            rows_ref[1, target, :] = jnp.concatenate([piece[:, 128:], jnp.zeros((4, 64), F32)], axis=1)
    return jnp.concatenate([rows_ref[0], rows_ref[1][:, :64]], axis=1)


def store_grid(rows, rows_ref, grid_ref):
    rows_ref[0] = rows[:, :128]
    rows_ref[1] = jnp.concatenate([rows[:, 128:], jnp.zeros((TOKENS, 64), F32)], axis=1)
    for row in range(6):
        for col in range(12):
            source = pl.ds(row * 12 + col, 4, stride=72)
            piece = jnp.concatenate([rows_ref[0, source, :], rows_ref[1, source, :][:, :64]], axis=1)
            grid_ref[row, col] = piece.astype(BF16)


def first_kernel(
    levels_ref,
    inputs_ref,
    grad_ref,
    gains_ref,
    in_ref,
    out_ref,
    up_ref,
    down_ref,
    table_ref,
    keys_ref,
    order_ref,
    quad_0,
    quad_1,
    quad_2,
    quad_3,
    weights_out,
    qkt_out,
    values_out,
    mixed_out,
    hidden_out,
    rows_ref,
    pairs_ref,
    row_ref,
    shaped_ref,
    bias_ref,
):
    levels = [levels_ref[0, 0], levels_ref[0, 1]]
    order = order_ref[...]
    grad_quads = mm(order, load_grid(grad_ref, rows_ref).astype(BF16))
    flat = load_grid(inputs_ref, rows_ref)
    make_pairs(keys_ref, pairs_ref)
    spread_bias(table_ref, pairs_ref, row_ref, shaped_ref, bias_ref)
    hat, _ = norm_stats(flat)
    normed = (hat * gains_ref[0:1]).astype(BF16)
    attended, mixed = attention(normed, in_ref[...], bias_ref, levels, None, weights_out)
    for window in range(2):
        qkt_out[window, 0] = attended[window][0]
        qkt_out[window, 1] = attended[window][1]
        values_out[window] = attended[window][2]
        mixed_out[window] = mixed[window]
    hidden = (flat + mm(natural_mixed(mixed), out_ref[...])).astype(BF16)
    hidden_out[...] = hidden
    hidden = hidden.astype(F32)
    _, _, _, expanded = feed_forward(hidden, gains_ref[1:2], up_ref[...])
    active = (expanded * 0.5 * (1.0 + lax.erf(expanded * (1.0 / math.sqrt(2.0))))).astype(BF16)
    result = (hidden + mm_nt(active, down_ref[...])).astype(BF16)
    result_quads = mm(order, result)
    for index, quad in enumerate((quad_0, quad_1, quad_2, quad_3)):
        rows = slice(index * QUAD, (index + 1) * QUAD)
        quad[...] = jnp.concatenate([result_quads[rows], grad_quads[rows]], axis=0).astype(BF16)


def second_kernel(
    levels_ref,
    quad_0,
    quad_1,
    quad_2,
    quad_3,
    region_col_ref,
    region_row_ref,
    gains_ref,
    in_ref,
    out_ref,
    up_ref,
    down_ref,
    table_ref,
    keys_ref,
    ahead_ref,
    back_ref,
    back_0,
    back_1,
    back_2,
    back_3,
    packed_ref,
    tables_out,
    pairs_ref,
    row_ref,
    shaped_ref,
    bias_ref,
    weights_ref,
    grads_ref,
):
    levels = [levels_ref[0, 0], levels_ref[0, 1]]
    quads = [quad[...].astype(F32) for quad in (quad_0, quad_1, quad_2, quad_3)]
    ahead = ahead_ref[...]
    flat = mm(ahead, jnp.concatenate([quad[:QUAD] for quad in quads], axis=0).astype(BF16))
    grad = mm(ahead, jnp.concatenate([quad[QUAD:] for quad in quads], axis=0).astype(BF16))
    make_pairs(keys_ref, pairs_ref)
    spread_bias(table_ref, pairs_ref, row_ref, shaped_ref, bias_ref)
    same = [region_col_ref[window] == region_row_ref[window] for window in range(2)]
    first_hat, first_inverse = norm_stats(flat)
    gain_one, gain_two = gains_ref[0:1], gains_ref[1:2]
    first_norm = (first_hat * gain_one).astype(BF16)
    in_weight, out_weight, up_weight, down_weight = in_ref[...], out_ref[...], up_ref[...], down_ref[...]
    attended, mixed = attention(first_norm, in_weight, bias_ref, levels, same, weights_ref)
    hidden = (flat + mm(natural_mixed(mixed), out_weight)).astype(BF16).astype(F32)
    second_hat, second_inverse, second_norm, expanded = feed_forward(hidden, gain_two, up_weight)
    active, slope = gelu_parts(expanded)
    result = (hidden + mm_nt(active, down_weight)).astype(BF16)
    grad_in = backward(
        grad, active, slope, second_hat, second_inverse, second_norm, mixed, attended, weights_ref,
        first_hat, first_inverse, first_norm, gain_one, gain_two, in_weight, out_weight, up_weight,
        down_weight, grads_ref, packed_ref,
    )
    back = back_ref[...]
    result_quads, grad_quads = mm(back, result), mm(back, grad_in)
    for index, quad in enumerate((back_0, back_1, back_2, back_3)):
        rows = slice(index * QUAD, (index + 1) * QUAD)
        quad[...] = jnp.concatenate([result_quads[rows], grad_quads[rows]], axis=0).astype(BF16)
    collect_bias(grads_ref, pairs_ref, levels, row_ref, shaped_ref, tables_out)


def third_kernel(
    levels_ref,
    quad_0,
    quad_1,
    quad_2,
    quad_3,
    inputs_ref,
    weights_ref,
    qkt_ref,
    values_ref,
    mixed_ref,
    hidden_ref,
    gains_ref,
    in_ref,
    out_ref,
    up_ref,
    down_ref,
    keys_ref,
    natural_ref,
    second_packed_ref,
    blocks_out,
    grad_out,
    packed_ref,
    tables_out,
    rows_ref,
    pairs_ref,
    row_ref,
    shaped_ref,
    grads_ref,
):
    levels = [levels_ref[0, 0], levels_ref[0, 1]]
    quads = [quad[...].astype(F32) for quad in (quad_0, quad_1, quad_2, quad_3)]
    natural = natural_ref[...]
    blocks = mm(natural, jnp.concatenate([quad[:QUAD] for quad in quads], axis=0).astype(BF16))
    store_grid(blocks, rows_ref, blocks_out)
    grad = mm(natural, jnp.concatenate([quad[QUAD:] for quad in quads], axis=0).astype(BF16))
    flat = load_grid(inputs_ref, rows_ref)
    first_hat, first_inverse = norm_stats(flat)
    gain_one, gain_two = gains_ref[0:1], gains_ref[1:2]
    first_norm = (first_hat * gain_one).astype(BF16)
    in_weight, out_weight, up_weight, down_weight = in_ref[...], out_ref[...], up_ref[...], down_ref[...]
    hidden = hidden_ref[...].astype(F32)
    second_hat, second_inverse, second_norm, expanded = feed_forward(hidden, gain_two, up_weight)
    active, slope = gelu_parts(expanded)
    attended = [(qkt_ref[window, 0], qkt_ref[window, 1], values_ref[window]) for window in range(2)]
    mixed = [mixed_ref[0], mixed_ref[1]]
    grad_in = backward(
        grad, active, slope, second_hat, second_inverse, second_norm, mixed, attended, weights_ref,
        first_hat, first_inverse, first_norm, gain_one, gain_two, in_weight, out_weight, up_weight,
        down_weight, grads_ref, packed_ref,
    )
    store_grid(grad_in.astype(F32), rows_ref, grad_out)
    make_pairs(keys_ref, pairs_ref)
    collect_bias(grads_ref, pairs_ref, levels, row_ref, shaped_ref, tables_out)


def whole(*shape):
    return pl.BlockSpec(shape, lambda *_: (0,) * len(shape))


def of_block(block, *shape):
    return pl.BlockSpec((None,) + shape, lambda *_: (block,) + (0,) * len(shape))


def weight_specs(block):
    return [
        of_block(block, 2, C),
        of_block(block, C, 3 * C),
        of_block(block, C, C),
        of_block(block, C, FFN),
        of_block(block, C, FFN),
    ]


def table_spec(block):
    return pl.BlockSpec((None, None, HEADS, 2, RELPOS), lambda *_: (block, 0, 0, 0, 0))


SMEM_WHOLE = pl.BlockSpec(memory_space=pltpu.SMEM)
VMEM_LIMIT = 56 * 1024 * 1024


def call(kernel, in_specs, out_specs, out_shapes, scratch, operands, flops, aliases=None):
    return pl.pallas_call(
        kernel,
        grid=(1,),
        in_specs=in_specs,
        out_specs=out_specs,
        out_shape=out_shapes,
        scratch_shapes=scratch,
        input_output_aliases=aliases or {},
        compiler_params=pltpu.CompilerParams(vmem_limit_bytes=VMEM_LIMIT),
        cost_estimate=pl.CostEstimate(flops=flops, bytes_accessed=4_000_000, transcendentals=1_000_000),
    )(*operands)


def shape_of(shape, dtype):
    return jax.ShapeDtypeStruct(shape, dtype)


def shifted(value, lat_steps, lon_steps):
    lon_count, lat_count = lax.axis_size("lon"), lax.axis_size("lat")
    pairs = []
    for lon in range(lon_count):
        for lat in range(lat_count):
            source = ((lon + lon_steps) % lon_count) * lat_count + (lat + lat_steps) % lat_count
            pairs.append((source, lon * lat_count + lat))
    return lax.ppermute(value, ("lon", "lat"), pairs)


def per_device(
    inputs,
    grad_out,
    region,
    bias_level,
    norm_gains,
    in_weight,
    out_weight,
    up_weight,
    down_weight,
    bias_tables,
):
    weights = (norm_gains, in_weight, out_weight, up_weight, down_weight.transpose(0, 2, 1))
    inputs, grad_out = inputs.transpose(1, 2, 0, 3), grad_out.transpose(1, 2, 0, 3)
    bias_tables = bias_tables.transpose(0, 1, 3, 2, 4)
    bias_level = bias_level.T
    quadrant = one_hot(quadrant_rows())
    rolled = one_hot(rolled_rows())
    keys = jnp.asarray(pair_keys())
    half = [jnp.asarray(array, BF16) for array in (quadrant, quadrant.T, rolled, rolled.T)]
    to_quads, from_quads, rolled_back, rolled_ahead = half
    grid_spec = whole(6, 12, 4, C)
    square = whole(TOKENS, TOKENS)
    keys_spec = whole(512, 256)
    quad_shape = shape_of((2 * QUAD, C), BF16)
    quad_spec = whole(2 * QUAD, C)
    grid_shape = shape_of((6, 12, 4, C), BF16)
    pairs_scratch = pltpu.VMEM((WIN_LON, 512, 256), BF16)
    row_scratch = pltpu.VMEM((16, 26 * 128), F32)
    shaped_scratch = pltpu.VMEM((4, 2 * 72 + 16, 128), F32)
    bias_scratch = pltpu.VMEM((2, 2 * HEADS * WIN, 128), F32)
    rows_scratch = pltpu.VMEM((2, TOKENS, 128), F32)
    grads_scratch = pltpu.VMEM((2, 2, HEADS * WIN, 128), F32)
    stored_shapes = [
        shape_of((2 * HEADS, WIN, WIN), BF16),
        shape_of((2, 2, C, WIN), BF16),
        shape_of((2, WIN, C), BF16),
        shape_of((2, C, WIN), BF16),
        shape_of((TOKENS, C), BF16),
    ]
    stored_specs = [whole(*shape.shape) for shape in stored_shapes]
    packed_shape = shape_of((2, ROWS, 128), BF16)
    table_shape = shape_of((TABLE_ROWS, 128), BF16)
    table_out = whole(TABLE_ROWS, 128)

    quads = call(
        first_kernel,
        [SMEM_WHOLE, grid_spec, grid_spec] + weight_specs(0) + [table_spec(0), keys_spec, square],
        [quad_spec] * 4 + stored_specs,
        [quad_shape] * 4 + stored_shapes,
        [rows_scratch, pairs_scratch, row_scratch, shaped_scratch, bias_scratch],
        (bias_level, inputs, grad_out, *weights, bias_tables, keys, to_quads),
        1_000_000_000,
    )
    stored = quads[4:]
    ahead = (
        quads[3],
        shifted(quads[2], 0, 1),
        shifted(quads[1], 1, 0),
        shifted(quads[0], 1, 1),
    )
    region_col, region_row = region.reshape(2, WIN, 1), region.reshape(2, 1, WIN)
    back = call(
        second_kernel,
        [SMEM_WHOLE] + [quad_spec] * 4 + [whole(2, WIN, 1), whole(2, 1, WIN)] + weight_specs(1)
        + [table_spec(1), keys_spec, square, square],
        [quad_spec] * 4 + [of_block(1, ROWS, 128), table_out],
        [quad_shape] * 4 + [packed_shape, table_shape],
        [pairs_scratch, row_scratch, shaped_scratch, bias_scratch, pltpu.VMEM((2 * HEADS, WIN, WIN), BF16),
         grads_scratch],
        (bias_level, *ahead, region_col, region_row, *weights, bias_tables, keys, rolled_ahead, rolled_back),
        3_000_000_000,
    )
    second_packed, second_tables = back[4:]
    home = (
        shifted(back[3], -1, -1),
        shifted(back[2], -1, 0),
        shifted(back[1], 0, -1),
        back[0],
    )
    blocks_out, grad_inputs, packed, first_tables = call(
        third_kernel,
        [SMEM_WHOLE] + [quad_spec] * 4 + [grid_spec] + stored_specs + weight_specs(0)
        + [keys_spec, square, pl.BlockSpec(memory_space=pl.ANY)],
        [grid_spec, grid_spec, of_block(0, ROWS, 128), table_out],
        [grid_shape, grid_shape, packed_shape, table_shape],
        [rows_scratch, pairs_scratch, row_scratch, shaped_scratch, grads_scratch],
        (bias_level, *home, inputs, *stored, *weights, keys, from_quads, second_packed),
        2_000_000_000,
        {18: 2},
    )
    packed, tables = sum_over_devices(packed.reshape(2 * ROWS, 128), first_tables, second_tables)
    totals = unpack(packed.reshape(2, ROWS, 128), tables.reshape(2, TABLE_ROWS, 128))
    gains, grad_in, grad_out_weight, grad_up, grad_down, grad_tables = totals
    return (
        blocks_out.transpose(2, 0, 1, 3),
        grad_inputs.transpose(2, 0, 1, 3),
        gains,
        grad_in,
        grad_out_weight,
        grad_up,
        grad_down.transpose(0, 2, 1),
        grad_tables.transpose(0, 1, 3, 2, 4),
    )


def exchanged(value, axis, bit):
    count = lax.axis_size(axis)
    return lax.ppermute(value, axis, [(place, place ^ bit) for place in range(count)])


def added(left, right):
    return (left.astype(F32) + right.astype(F32)).astype(BF16)


def upper(axis, bit):
    return (lax.axis_index(axis) & bit) != 0


def halve(value, axis, bit):
    half = value.shape[0] // 2
    up = upper(axis, bit)
    keep = jnp.where(up, value[half:], value[:half])
    send = jnp.where(up, value[:half], value[half:])
    return added(keep, exchanged(send, axis, bit))


def double(value, axis, bit):
    other = exchanged(value, axis, bit)
    up = upper(axis, bit)
    return jnp.concatenate([jnp.where(up, other, value), jnp.where(up, value, other)], axis=0)


def bits(axis):
    count = lax.axis_size(axis)
    return [1 << place for place in range(count.bit_length() - 1)]


def sum_over_devices(packed, first_tables, second_tables):
    for bit in bits("lat"):
        packed = halve(packed, "lat", bit)
    rows = packed.shape[0]
    joined = jnp.concatenate([packed, first_tables, second_tables], axis=0)
    for bit in bits("lon")[:2]:
        joined = halve(joined, "lon", bit)
    for bit in bits("lon")[2:]:
        joined = added(joined, exchanged(joined, "lon", bit))
    for bit in reversed(bits("lon")[:2]):
        joined = double(joined, "lon", bit)
    packed, tables = joined[:rows], joined[rows:]
    for bit in reversed(bits("lat")):
        packed = double(packed, "lat", bit)
    return packed, tables


def unpack_kernel(packed_ref, tables_ref, gains_ref, in_ref, out_ref, up_ref, down_ref, grads_ref, rows_ref):
    rows_ref[...] = tables_ref[...].astype(F32)
    for part in range(4):
        in_ref[:, part * 128 : (part + 1) * 128] = packed_ref[part * C : (part + 1) * C].astype(F32)
    shared = packed_ref[768:960].astype(F32)
    in_ref[:, 512:] = shared[:, :64]
    out_ref[:, :128] = packed_ref[960:1152].astype(F32)
    out_ref[:, 128:] = shared[:, 64:]
    for part in range(6):
        lanes = slice(part * 128, (part + 1) * 128)
        up_ref[:, lanes] = packed_ref[1152 + part * C : 1152 + (part + 1) * C].astype(F32)
        down_ref[:, lanes] = packed_ref[2304 + part * C : 2304 + (part + 1) * C].astype(F32)
    gains = packed_ref[GAIN_ROWS : GAIN_ROWS + 16].astype(F32)
    gains_ref[0:1, :128] = gains[0:1]
    gains_ref[0:1, 128:] = gains[1:2, :64]
    gains_ref[1:2, :128] = gains[2:3]
    gains_ref[1:2, 128:] = gains[1:2, 64:]
    for slab in range(26):
        width = min(128, RELPOS - slab * 128)
        for level in range(2):
            start = slab * 12 + level * HEADS
            grads_ref[:, level, slab * 128 : slab * 128 + width] = rows_ref[start : start + HEADS, :width]


def unpack(packed, tables):
    def block(*shape):
        return pl.BlockSpec((None,) + shape, lambda index: (index,) + (0,) * len(shape))

    return pl.pallas_call(
        unpack_kernel,
        grid=(2,),
        in_specs=[block(ROWS, 128), block(TABLE_ROWS, 128)],
        out_specs=[
            block(2, C),
            block(C, 3 * C),
            block(C, C),
            block(C, FFN),
            block(C, FFN),
            pl.BlockSpec((None, None, HEADS, 2, RELPOS), lambda index: (index, 0, 0, 0, 0)),
        ],
        out_shape=[
            shape_of((2, 2, C), F32),
            shape_of((2, C, 3 * C), F32),
            shape_of((2, C, C), F32),
            shape_of((2, C, FFN), F32),
            shape_of((2, C, FFN), F32),
            shape_of((2, 1, HEADS, 2, RELPOS), F32),
        ],
        scratch_shapes=[pltpu.VMEM((TABLE_ROWS, 128), F32)],
        compiler_params=pltpu.CompilerParams(vmem_limit_bytes=VMEM_LIMIT),
    )(packed, tables)


def solution(mesh):
    placed = (
        P(None, "lat", "lon", None),
        P(None, "lat", "lon", None),
        P(None, "lat", "lon"),
        P(None, "lat"),
        P(),
        P(),
        P(),
        P(),
        P(),
        P(None, "lat", None, None, None),
    )
    return jax.shard_map(
        per_device,
        mesh=mesh,
        in_specs=placed,
        out_specs=(
            P(None, "lat", "lon", None),
            P(None, "lat", "lon", None),
            P(),
            P(),
            P(),
            P(),
            P(),
            P(None, "lat", None, None, None),
        ),
        check_vma=False,
    )
```

```python
import functools
import math

import jax
import jax.numpy as jnp
import numpy as np
from jax import lax
from jax.experimental import pallas as pl
from jax.experimental.pallas import tpu as pltpu
from jax.sharding import PartitionSpec as P

C = 192
HEADS = 6
HEAD = 32
FFN = 768
WIN_Z = 2
WIN_LAT = 6
WIN_LON = 12
WIN = 144
TOKENS = 2 * WIN
QUAD = 72
RELPOS = 3312
SPAN = 2 * WIN_LON - 1
ROWS = 3584
GAIN_ROWS = 3456
TABLE_ROWS = 320

EPSILON = 1e-05
NEGATIVE = -1000000000.0
SCALE = 1.0 / math.sqrt(HEAD)

F32 = jnp.float32
BF16 = jnp.bfloat16


def quadrant_rows():
    rows = np.zeros(TOKENS, np.int64)
    at = 0
    for lat_half in range(2):
        for lon_half in range(2):
            for level in range(4):
                for row in range(3):
                    for col in range(6):
                        rows[at] = (level * 6 + lat_half * 3 + row) * 12 + lon_half * 6 + col
                        at += 1
    return rows


def rolled_rows():
    rows = quadrant_rows()
    level, rest = rows // 72, rows % 72
    return ((level + 3) % 4) * 72 + rest


def one_hot(rows):
    picked = np.zeros((TOKENS, TOKENS), np.float32)
    picked[np.arange(TOKENS), rows] = 1.0
    return picked


def mm(left, right):
    return lax.dot_general(left, right, (((1,), (0,)), ((), ())), preferred_element_type=F32)


def mm_nt(left, right):
    return lax.dot_general(left, right, (((1,), (1,)), ((), ())), preferred_element_type=F32)


def eye(size):
    return (
        lax.broadcasted_iota(jnp.int32, (size, size), 0) == lax.broadcasted_iota(jnp.int32, (size, size), 1)
    ).astype(F32).astype(BF16)


def turned(value):
    return mm_nt(eye(value.shape[1]), value).astype(BF16)


def norm_stats(values):
    centre = values - jnp.mean(values, axis=-1, keepdims=True)
    inverse = lax.rsqrt(jnp.mean(centre * centre, axis=-1, keepdims=True) + EPSILON)
    return centre * inverse, inverse


def norm_backward(upstream, normal_hat, inverse):
    upstream_mean = jnp.mean(upstream, axis=-1, keepdims=True)
    cross_mean = jnp.mean(upstream * normal_hat, axis=-1, keepdims=True)
    return inverse * (upstream - upstream_mean - normal_hat * cross_mean)


def head_lanes(head):
    lane = lax.broadcasted_iota(jnp.int32, (1, C), 1)
    return (lane >= head * HEAD) & (lane < (head + 1) * HEAD)


def make_pairs(pairs_ref):
    row = lax.broadcasted_iota(jnp.int32, (512, 1), 0)
    within = row & 127
    third = (within >= SPAN).astype(jnp.int32) + (within >= 2 * SPAN).astype(jnp.int32)
    row_group = (row >> 7) * 3 + third
    row_offset = within - third * SPAN
    col = lax.broadcasted_iota(jnp.int32, (1, 256), 1)
    col_group = jnp.zeros_like(col)
    for group in range(1, 12):
        col_group = col_group + (col >= group * 12).astype(jnp.int32)
    col_place = col - col_group * 12
    usable = (row_group == col_group) & (within < 3 * SPAN) & (col < WIN)
    keys = jnp.where(usable, col_place + 11 - row_offset, -1)
    for place in range(WIN_LON):
        pairs_ref[place] = jnp.where(keys == place, 1.0, 0.0).astype(BF16)


def table_start(zs, zt, hs, ht):
    return (((zs * 2 + zt) * 6 + hs) * 6 + ht) * SPAN


def spread_bias(table_ref, pairs_ref, row_ref, shaped_ref, bias_ref):
    for head in range(HEADS):
        row_ref[head * 2 : head * 2 + 2, :RELPOS] = table_ref[head].astype(F32)
    row = row_ref[: 2 * HEADS]
    for zs in range(2):
        for zt in range(2):
            for group in range(2):
                for ht in range(6):
                    pieces = []
                    for hs in range(group * 3, group * 3 + 3):
                        start = table_start(zs, zt, hs, ht)
                        pieces.append(row[:, start : start + SPAN])
                    pieces.append(jnp.zeros((2 * HEADS, 128 - 3 * SPAN), F32))
                    target = pl.ds(zt * 6 + ht, 2 * HEADS, stride=12)
                    shaped_ref[zs * 2 + group, target, :] = jnp.concatenate(pieces, axis=1)
    shaped = jnp.concatenate([shaped_ref[part, :WIN].astype(BF16) for part in range(4)], axis=1)
    for col in range(WIN_LON):
        spread = mm(shaped, pairs_ref[col])
        bias_ref[0, pl.ds(col, WIN, stride=12), :] = spread[:, :128]
        bias_ref[1, pl.ds(col, WIN, stride=12), :] = spread[:, 128:]


def collect_bias(scaled_ref, pairs_ref, levels, row_ref, shaped_ref, grads_ref, out_ref):
    for place in range(2 * HEADS):
        rows = slice(place * WIN, (place + 1) * WIN)
        piece = scaled_ref[place].astype(F32)
        grads_ref[0, rows] = piece[:, :128]
        grads_ref[1, rows] = jnp.concatenate([piece[:, 128:], jnp.zeros((WIN, 256 - WIN), F32)], axis=1)
    total = jnp.zeros((WIN, 512), F32)
    for col in range(WIN_LON):
        left = grads_ref[0, pl.ds(col, WIN, stride=12), :]
        right = grads_ref[1, pl.ds(col, WIN, stride=12), :]
        piece = jnp.concatenate([left, right], axis=1).astype(BF16)
        total = total + mm_nt(piece, pairs_ref[col])
    total = total * (1.0 / SCALE)
    for part in range(4):
        shaped_ref[part, :WIN] = total[:, part * 128 : (part + 1) * 128]
    row_ref[...] = jnp.zeros_like(row_ref)
    for zs in range(2):
        for zt in range(2):
            for group in range(2):
                for ht in range(6):
                    pieces = [
                        shaped_ref[zs * 2 + group, pl.ds(window * 72 + zt * 6 + ht, HEADS, stride=12), :]
                        for window in range(2)
                    ]
                    for level in range(2):
                        chosen = jnp.zeros((HEADS, 128), F32)
                        for window in range(2):
                            chosen = chosen + jnp.where(levels[window] == level, pieces[window], 0.0)
                        for index in range(3):
                            start = table_start(zs, zt, group * 3 + index, ht)
                            row_ref[level * 8 : level * 8 + HEADS, start : start + SPAN] = chosen[
                                :, index * SPAN : (index + 1) * SPAN
                            ]
    for slab in range(26):
        lanes = slice(slab * 128, (slab + 1) * 128)
        rows = jnp.concatenate([row_ref[:HEADS, lanes], row_ref[8 : 8 + HEADS, lanes]], axis=0)
        shaped_ref[slab // 13, slab % 13 * 12 : slab % 13 * 12 + 12] = rows
    out_ref[...] = jnp.concatenate(
        [shaped_ref[0, :156], shaped_ref[1, :156], jnp.zeros((TABLE_ROWS - 312, 128), F32)], axis=0
    ).astype(BF16)


def load_tiles(bias_ref, level, head):
    rows = pl.ds(pl.multiple_of((head * 2 + level) * WIN, 8), WIN)
    return jnp.concatenate([bias_ref[0, rows, :], bias_ref[1, rows, : WIN - 128]], axis=1)


def attention(normed, in_weight, bias_of, weights_ref):
    eye_c = eye(C)
    weight_q, weight_k, weight_v = in_weight[:, :C], in_weight[:, C : 2 * C], in_weight[:, 2 * C :]
    kept = []
    mixed = []
    for window in range(2):
        rows = normed[window * WIN : (window + 1) * WIN]
        keys = mm(rows, weight_k).astype(BF16)
        values = mm(rows, weight_v).astype(BF16)
        queries = mm(rows, weight_q).astype(BF16)
        queries_t = mm_nt(eye_c, queries).astype(BF16)
        keys_t = mm_nt(eye_c, keys).astype(BF16)
        values_t = mm_nt(eye_c, values).astype(BF16)
        parts = []
        for head in range(HEADS):
            own = jnp.where(head_lanes(head), keys.astype(F32), 0.0).astype(BF16)
            scores = mm(own, queries_t) * SCALE + bias_of(window, head)
            weights = jnp.exp(scores - jnp.max(scores, axis=0, keepdims=True))
            weights = weights * (1.0 / jnp.sum(weights, axis=0, keepdims=True))
            weights = weights.astype(BF16)
            weights_ref[window * HEADS + head] = weights
            parts.append(mm(values_t[head * HEAD : (head + 1) * HEAD], weights))
        mixed.append(jnp.concatenate(parts, axis=0).astype(BF16))
        kept.append((queries_t, keys_t, values))
    return kept, mixed


def feed_forward(hidden, gain, up_weight):
    hat, inverse = norm_stats(hidden)
    normed = (hat * gain).astype(BF16)
    return hat, inverse, normed, mm(normed, up_weight)


def gelu_parts(expanded):
    cumulative = 0.5 * (1.0 + lax.erf(expanded * (1.0 / math.sqrt(2.0))))
    slope = cumulative + expanded * jnp.exp(-0.5 * expanded * expanded) * (1.0 / math.sqrt(2.0 * math.pi))
    return (expanded * cumulative).astype(BF16), slope


def natural_mixed(mixed):
    eye_w = eye(WIN)
    return jnp.concatenate([mm_nt(eye_w, part) for part in mixed], axis=0).astype(BF16)


def pack(packed_ref, start, value):
    height = value.shape[0]
    for part in range(value.shape[1] // 128):
        rows = slice(start + part * height, start + (part + 1) * height)
        packed_ref[rows] = value[:, part * 128 : (part + 1) * 128].astype(BF16)


def backward(
    grad,
    active,
    slope,
    second_hat,
    second_inverse,
    second_norm,
    mixed,
    attended,
    weights_ref,
    first_hat,
    first_inverse,
    first_norm,
    gain_one,
    gain_two,
    in_weight,
    out_weight,
    up_weight,
    down_weight,
    scaled_ref,
    packed_ref,
):
    eye_c = eye(C)
    grad_half = grad.astype(BF16)
    pack(packed_ref, 2304, mm(turned(grad_half), active))
    grad_expanded = (mm(grad_half, down_weight) * slope).astype(BF16)
    normed_t = turned(second_norm)
    pack(packed_ref, 1152, mm(normed_t, grad_expanded))
    grad_second = mm_nt(grad_expanded, up_weight)
    gain_two_grad = jnp.sum(grad_second * second_hat, axis=0, keepdims=True)
    grad_hidden = (grad + norm_backward(grad_second * gain_two, second_hat, second_inverse)).astype(BF16)
    grad_out = mm(mixed[0], grad_hidden[:WIN]) + mm(mixed[1], grad_hidden[WIN:])
    packed_ref[960:1152] = grad_out[:, :128].astype(BF16)
    grad_mixed = mm_nt(grad_hidden, out_weight).astype(BF16)
    projected = []
    for window in range(2):
        queries_t, keys_t, values = attended[window]
        upstream_t = mm_nt(eye_c, grad_mixed[window * WIN : (window + 1) * WIN]).astype(BF16)
        grad_q, grad_k, grad_v = [], [], []
        for head in range(HEADS):
            lanes = slice(head * HEAD, (head + 1) * HEAD)
            half = weights_ref[window * HEADS + head]
            weights = half.astype(F32)
            own = jnp.where(head_lanes(head), values.astype(F32), 0.0).astype(BF16)
            grad_weights = mm(own, upstream_t)
            inner = jnp.sum(grad_weights * weights, axis=0, keepdims=True)
            grad_scores = weights * (grad_weights - inner)
            scaled = (grad_scores * SCALE).astype(BF16)
            scaled_ref[window * HEADS + head] = scaled
            grad_v.append(mm_nt(upstream_t[lanes], half))
            grad_q.append(mm(keys_t[lanes], scaled))
            grad_k.append(mm_nt(queries_t[lanes], scaled))
        projected_t = jnp.concatenate(grad_q + grad_k + grad_v, axis=0).astype(BF16)
        projected.append(mm_nt(eye(WIN), projected_t))
    projected = jnp.concatenate(projected, axis=0).astype(BF16)
    first_t = turned(first_norm)
    grad_in = mm(first_t, projected)
    pack(packed_ref, 0, grad_in[:, :512])
    packed_ref[768:960] = jnp.concatenate([grad_in[:, 512:], grad_out[:, 128:]], axis=1).astype(BF16)
    grad_first = mm_nt(projected, in_weight)
    gain_one_grad = jnp.sum(grad_first * first_hat, axis=0, keepdims=True)
    gain_rows = jnp.concatenate(
        [
            gain_one_grad[:, :128],
            jnp.concatenate([gain_one_grad[:, 128:], gain_two_grad[:, 128:]], axis=1),
            gain_two_grad[:, :128],
            jnp.zeros((ROWS - GAIN_ROWS - 3, 128), F32),
        ],
        axis=0,
    )
    packed_ref[GAIN_ROWS:ROWS] = gain_rows.astype(BF16)
    return (
        grad_hidden.astype(F32) + norm_backward(grad_first * gain_one, first_hat, first_inverse)
    ).astype(BF16)


def load_grid(grid_ref, rows_ref):
    for row in range(6):
        for col in range(12):
            piece = grid_ref[row, col].astype(F32)
            target = pl.ds(row * 12 + col, 4, stride=72)
            rows_ref[0, target, :] = piece[:, :128]
            rows_ref[1, target, :] = jnp.concatenate([piece[:, 128:], jnp.zeros((4, 64), F32)], axis=1)
    return jnp.concatenate([rows_ref[0], rows_ref[1][:, :64]], axis=1)


def store_grid(rows, rows_ref, grid_ref):
    rows_ref[0] = rows[:, :128]
    rows_ref[1] = jnp.concatenate([rows[:, 128:], jnp.zeros((TOKENS, 64), F32)], axis=1)
    for row in range(6):
        for col in range(12):
            source = pl.ds(row * 12 + col, 4, stride=72)
            piece = jnp.concatenate([rows_ref[0, source, :], rows_ref[1, source, :][:, :64]], axis=1)
            grid_ref[row, col] = piece.astype(BF16)


def block_weights(gains_ref, in_ref, out_ref, up_ref, down_ref):
    gains = gains_ref[...]
    return gains[0:1], gains[1:2], in_ref[...], out_ref[...], up_ref[...], down_ref[...]


def write_halves(upper_ref, packed_ref, keep_ref, send_ref):
    half = ROWS // 2
    is_upper = upper_ref[0] == 1

    @pl.when(is_upper)
    def _():
        keep_ref[...] = packed_ref[half:]
        send_ref[...] = packed_ref[:half]

    @pl.when(jnp.logical_not(is_upper))
    def _():
        keep_ref[...] = packed_ref[:half]
        send_ref[...] = packed_ref[half:]


def first_kernel(
    levels_ref,
    inputs_ref,
    grad_ref,
    gains_ref,
    in_ref,
    out_ref,
    up_ref,
    down_ref,
    table_ref,
    order_ref,
    quad_0,
    quad_1,
    quad_2,
    quad_3,
    weights_out,
    qkt_out,
    values_out,
    mixed_out,
    hidden_out,
    pairs_ref,
    rows_ref,
    row_ref,
    shaped_ref,
    bias_ref,
):
    levels = [levels_ref[0, 0], levels_ref[0, 1]]
    gain_one, gain_two, in_weight, out_weight, up_weight, down_weight = block_weights(
        gains_ref, in_ref, out_ref, up_ref, down_ref
    )
    order = order_ref[...]
    grad_quads = mm(order, load_grid(grad_ref, rows_ref).astype(BF16))
    flat = load_grid(inputs_ref, rows_ref)
    make_pairs(pairs_ref)
    spread_bias(table_ref, pairs_ref, row_ref, shaped_ref, bias_ref)
    hat, _ = norm_stats(flat)
    normed = (hat * gain_one).astype(BF16)
    attended, mixed = attention(
        normed, in_weight, lambda window, head: load_tiles(bias_ref, levels[window], head), weights_out
    )
    for window in range(2):
        qkt_out[window, 0] = attended[window][0]
        qkt_out[window, 1] = attended[window][1]
        values_out[window] = attended[window][2]
        mixed_out[window] = mixed[window]
    hidden = (flat + mm(natural_mixed(mixed), out_weight)).astype(BF16)
    hidden_out[...] = hidden
    hidden = hidden.astype(F32)
    _, _, _, expanded = feed_forward(hidden, gain_two, up_weight)
    active = (expanded * 0.5 * (1.0 + lax.erf(expanded * (1.0 / math.sqrt(2.0))))).astype(BF16)
    result = (hidden + mm_nt(active, down_weight)).astype(BF16)
    result_quads = mm(order, result)
    for index, quad in enumerate((quad_0, quad_1, quad_2, quad_3)):
        rows = slice(index * QUAD, (index + 1) * QUAD)
        quad[...] = jnp.concatenate([result_quads[rows], grad_quads[rows]], axis=0).astype(BF16)


def region_row(region_ref, window):
    pieces = [region_ref[row, window * 2 + level : window * 2 + level + 1, :] for level in range(2) for row in range(6)]
    return jnp.concatenate(pieces, axis=1)


def prepare_kernel(
    levels_ref, region_ref, table_ref, bias_out, pairs_ref, row_ref, shaped_ref, bias_ref
):
    levels = [levels_ref[0, 0], levels_ref[0, 1]]
    make_pairs(pairs_ref)
    spread_bias(table_ref, pairs_ref, row_ref, shaped_ref, bias_ref)
    diagonal = lax.broadcasted_iota(jnp.int32, (WIN, WIN), 0) == lax.broadcasted_iota(jnp.int32, (WIN, WIN), 1)
    for window in range(2):
        across = region_row(region_ref, window).astype(F32)
        down = jnp.sum(jnp.where(diagonal, across, 0.0), axis=1, keepdims=True)
        same = across == down
        for head in range(HEADS):
            bias = jnp.where(same, load_tiles(bias_ref, levels[window], head), NEGATIVE)
            bias_out[window * HEADS + head] = bias.astype(BF16)


def second_kernel(
    upper_ref,
    quad_0,
    quad_1,
    quad_2,
    quad_3,
    bias_ref,
    gains_ref,
    in_ref,
    out_ref,
    up_ref,
    down_ref,
    ahead_ref,
    back_ref,
    back_0,
    back_1,
    back_2,
    back_3,
    keep_ref,
    send_ref,
    scaled_ref,
    weights_ref,
    packed_ref,
):
    quads = [quad[...].astype(F32) for quad in (quad_0, quad_1, quad_2, quad_3)]
    ahead = ahead_ref[...]
    flat = mm(ahead, jnp.concatenate([quad[:QUAD] for quad in quads], axis=0).astype(BF16))
    grad = mm(ahead, jnp.concatenate([quad[QUAD:] for quad in quads], axis=0).astype(BF16))
    gain_one, gain_two, in_weight, out_weight, up_weight, down_weight = block_weights(
        gains_ref, in_ref, out_ref, up_ref, down_ref
    )
    first_hat, first_inverse = norm_stats(flat)
    first_norm = (first_hat * gain_one).astype(BF16)
    attended, mixed = attention(
        first_norm, in_weight, lambda window, head: bias_ref[window * HEADS + head].astype(F32), weights_ref
    )
    hidden = (flat + mm(natural_mixed(mixed), out_weight)).astype(BF16).astype(F32)
    second_hat, second_inverse, second_norm, expanded = feed_forward(hidden, gain_two, up_weight)
    active, slope = gelu_parts(expanded)
    result = (hidden + mm_nt(active, down_weight)).astype(BF16)
    grad_in = backward(
        grad, active, slope, second_hat, second_inverse, second_norm, mixed, attended, weights_ref,
        first_hat, first_inverse, first_norm, gain_one, gain_two, in_weight, out_weight, up_weight,
        down_weight, scaled_ref, packed_ref,
    )
    back = back_ref[...]
    result_quads, grad_quads = mm(back, result), mm(back, grad_in)
    for index, quad in enumerate((back_0, back_1, back_2, back_3)):
        rows = slice(index * QUAD, (index + 1) * QUAD)
        quad[...] = jnp.concatenate([result_quads[rows], grad_quads[rows]], axis=0).astype(BF16)
    write_halves(upper_ref, packed_ref, keep_ref, send_ref)


def collect_kernel(
    levels_ref,
    scaled_ref,
    hidden_ref,
    gains_ref,
    up_ref,
    tables_out,
    active_out,
    slope_out,
    pairs_ref,
    row_ref,
    shaped_ref,
    grads_ref,
):
    levels = [levels_ref[0, 0], levels_ref[0, 1]]
    make_pairs(pairs_ref)
    collect_bias(scaled_ref, pairs_ref, levels, row_ref, shaped_ref, grads_ref, tables_out)
    _, _, _, expanded = feed_forward(hidden_ref[...].astype(F32), gains_ref[1:2], up_ref[...])
    active, slope = gelu_parts(expanded)
    active_out[...] = active
    slope_out[...] = slope.astype(BF16)


def third_kernel(
    upper_ref,
    quad_0,
    quad_1,
    quad_2,
    quad_3,
    inputs_ref,
    weights_ref,
    qkt_ref,
    values_ref,
    mixed_ref,
    hidden_ref,
    active_ref,
    slope_ref,
    gains_ref,
    in_ref,
    out_ref,
    up_ref,
    down_ref,
    natural_ref,
    keep_ref,
    send_ref,
    rows_out,
    scaled_ref,
    rows_ref,
    packed_ref,
):
    quads = [quad[...].astype(F32) for quad in (quad_0, quad_1, quad_2, quad_3)]
    grad = mm(natural_ref[...], jnp.concatenate([quad[QUAD:] for quad in quads], axis=0).astype(BF16))
    gain_one, gain_two, in_weight, out_weight, up_weight, down_weight = block_weights(
        gains_ref, in_ref, out_ref, up_ref, down_ref
    )
    first_hat, first_inverse = norm_stats(load_grid(inputs_ref, rows_ref))
    first_norm = (first_hat * gain_one).astype(BF16)
    second_hat, second_inverse = norm_stats(hidden_ref[...].astype(F32))
    second_norm = (second_hat * gain_two).astype(BF16)
    attended = [(qkt_ref[window, 0], qkt_ref[window, 1], values_ref[window]) for window in range(2)]
    mixed = [mixed_ref[0], mixed_ref[1]]
    rows_out[...] = backward(
        grad, active_ref[...], slope_ref[...].astype(F32), second_hat, second_inverse, second_norm, mixed,
        attended, weights_ref, first_hat, first_inverse, first_norm, gain_one, gain_two, in_weight,
        out_weight, up_weight, down_weight, scaled_ref, packed_ref,
    )
    write_halves(upper_ref, packed_ref, keep_ref, send_ref)


def finish_kernel(
    levels_ref, scaled_ref, second_tables_ref, tables_out, pairs_ref, row_ref, shaped_ref, grads_ref
):
    levels = [levels_ref[0, 0], levels_ref[0, 1]]
    make_pairs(pairs_ref)
    collect_bias(scaled_ref, pairs_ref, levels, row_ref, shaped_ref, grads_ref, tables_out.at[:TABLE_ROWS])
    tables_out[TABLE_ROWS:] = second_tables_ref[...]


def grids_kernel(quad_0, quad_1, quad_2, quad_3, natural_ref, grad_rows_ref, blocks_out, grad_out, rows_ref):
    quads = [quad[:QUAD].astype(F32) for quad in (quad_0, quad_1, quad_2, quad_3)]
    blocks = mm(natural_ref[...], jnp.concatenate(quads, axis=0).astype(BF16))
    store_grid(blocks, rows_ref, blocks_out)
    store_grid(grad_rows_ref[...].astype(F32), rows_ref, grad_out)


SMEM = pl.BlockSpec(memory_space=pltpu.SMEM)
VMEM_LIMIT = 60 * 1024 * 1024


def whole(array):
    return pl.BlockSpec(array.shape, lambda *_: (0,) * len(array.shape))


class Part:
    def __init__(self, array, block):
        self.array, self.block = array, block

    def spec(self):
        kept = [size for size in self.array.shape[1:] if size != 1]
        lead = len(self.array.shape) - len(kept)
        return pl.BlockSpec((None,) * lead + tuple(kept), lambda *_: (self.block,) + (0,) * (lead - 1 + len(kept)))


def call(kernel, scalars, operands, out_shapes, scratch, flops):
    specs = [operand.spec() if isinstance(operand, Part) else whole(operand) for operand in operands]
    arrays = [operand.array if isinstance(operand, Part) else operand for operand in operands]
    return pl.pallas_call(
        kernel,
        grid=(1,),
        in_specs=[SMEM] * len(scalars) + specs,
        out_specs=[whole(shape) for shape in out_shapes],
        out_shape=out_shapes,
        scratch_shapes=scratch,
        compiler_params=pltpu.CompilerParams(vmem_limit_bytes=VMEM_LIMIT),
        cost_estimate=pl.CostEstimate(flops=flops, bytes_accessed=4_000_000, transcendentals=1_000_000),
    )(*scalars, *arrays)


def shape_of(shape, dtype):
    return jax.ShapeDtypeStruct(shape, dtype)


def shifted(value, lat_steps, lon_steps):
    lon_count, lat_count = lax.axis_size("lon"), lax.axis_size("lat")
    pairs = []
    for lon in range(lon_count):
        for lat in range(lat_count):
            source = ((lon + lon_steps) % lon_count) * lat_count + (lat + lat_steps) % lat_count
            pairs.append((source, lon * lat_count + lat))
    return lax.ppermute(value, ("lon", "lat"), pairs)


def per_device(
    inputs,
    grad_out,
    region,
    bias_level,
    norm_gains,
    in_weight,
    out_weight,
    up_weight,
    down_weight,
    bias_tables,
):
    weights = (norm_gains, in_weight, out_weight, up_weight, down_weight.transpose(0, 2, 1))
    first_weights = [Part(array, 0) for array in weights]
    second_weights = [Part(array, 1) for array in weights]
    inputs, grad_out = inputs.transpose(1, 2, 0, 3), grad_out.transpose(1, 2, 0, 3)
    bias_tables = bias_tables.transpose(0, 1, 3, 2, 4)
    bias_level = bias_level.T
    quadrant = one_hot(quadrant_rows())
    rolled = one_hot(rolled_rows())
    half = [jnp.asarray(array, BF16) for array in (quadrant, quadrant.T, rolled, rolled.T)]
    to_quads, from_quads, rolled_back, rolled_ahead = half
    is_upper = (lax.axis_index("lat") & 1).astype(jnp.int32).reshape(1)

    quad_shape = shape_of((2 * QUAD, C), BF16)
    grid_shape = shape_of((6, 12, 4, C), BF16)
    half_shape = shape_of((ROWS // 2, 128), BF16)
    table_shape = shape_of((TABLE_ROWS, 128), BF16)
    weights_shape = (2 * HEADS, WIN, WIN)
    pairs_scratch = pltpu.VMEM((WIN_LON, 512, 256), BF16)
    grads_scratch = pltpu.VMEM((2, 2 * HEADS * WIN, 128), F32)
    row_scratch = pltpu.VMEM((16, 26 * 128), F32)
    shaped_scratch = pltpu.VMEM((4, 2 * 72 + 16, 128), F32)
    bias_scratch = pltpu.VMEM((2, 2 * HEADS * WIN, 128), F32)
    rows_scratch = pltpu.VMEM((2, TOKENS, 128), F32)
    packed_scratch = pltpu.VMEM((ROWS, 128), BF16)

    quads = call(
        first_kernel,
        (bias_level,),
        (inputs, grad_out, *first_weights, Part(bias_tables, 0), to_quads),
        [quad_shape] * 4
        + [
            shape_of(weights_shape, BF16),
            shape_of((2, 2, C, WIN), BF16),
            shape_of((2, WIN, C), BF16),
            shape_of((2, C, WIN), BF16),
            shape_of((TOKENS, C), BF16),
        ],
        [pairs_scratch, rows_scratch, row_scratch, shaped_scratch, bias_scratch],
        1_000_000_000,
    )
    stored = quads[4:]
    ahead = (
        quads[3],
        shifted(quads[2], 0, 1),
        shifted(quads[1], 1, 0),
        shifted(quads[0], 1, 1),
    )
    (bias,) = call(
        prepare_kernel,
        (bias_level,),
        (region.transpose(1, 0, 2), Part(bias_tables, 1)),
        [shape_of(weights_shape, BF16)],
        [pairs_scratch, row_scratch, shaped_scratch, bias_scratch],
        500_000_000,
    )
    *back, second_keep, second_send, second_scaled = call(
        second_kernel,
        (is_upper,),
        (*ahead, bias, *second_weights, rolled_ahead, rolled_back),
        [quad_shape] * 4 + [half_shape, half_shape, shape_of(weights_shape, BF16)],
        [pltpu.VMEM(weights_shape, BF16), packed_scratch],
        3_000_000_000,
    )
    second_tables, active, slope = call(
        collect_kernel,
        (bias_level,),
        (second_scaled, stored[4], first_weights[0], first_weights[3]),
        [table_shape, shape_of((TOKENS, FFN), BF16), shape_of((TOKENS, FFN), BF16)],
        [pairs_scratch, row_scratch, shaped_scratch, grads_scratch],
        500_000_000,
    )
    home = [
        shifted(back[3], -1, -1),
        shifted(back[2], -1, 0),
        shifted(back[1], 0, -1),
        back[0],
    ]
    second = added(second_keep, exchanged(second_send, CORE))
    home[3], second = lax.optimization_barrier((home[3], second))
    first_keep, first_send, grad_rows, first_scaled = call(
        third_kernel,
        (is_upper,),
        (*home, inputs, *stored, active, slope, *first_weights, from_quads),
        [half_shape, half_shape, shape_of((TOKENS, C), BF16), shape_of(weights_shape, BF16)],
        [rows_scratch, packed_scratch],
        2_000_000_000,
    )
    blocks_out, grad_inputs = call(
        grids_kernel,
        (),
        (*home, from_quads, grad_rows),
        [grid_shape, grid_shape],
        [rows_scratch],
        100_000_000,
    )
    first = added(first_keep, exchanged(first_send, CORE))
    first, first_scaled = lax.optimization_barrier((first, first_scaled))
    (tables,) = call(
        finish_kernel,
        (bias_level,),
        (first_scaled, second_tables),
        [shape_of((2 * TABLE_ROWS, 128), BF16)],
        [pairs_scratch, row_scratch, shaped_scratch, grads_scratch],
        500_000_000,
    )
    totals = unpack(is_upper, *sum_all(first, second, tables))
    gains, grad_in, grad_out_weight, grad_up, grad_down, grad_tables = totals
    return (
        blocks_out.transpose(2, 0, 1, 3),
        grad_inputs.transpose(2, 0, 1, 3),
        gains,
        grad_in,
        grad_out_weight,
        grad_up,
        grad_down.transpose(0, 2, 1),
        grad_tables.transpose(0, 1, 3, 2, 4),
    )


def exchanged(value, mask):
    lon_count, lat_count = lax.axis_size("lon"), lax.axis_size("lat")
    pairs = []
    for lon in range(lon_count):
        for lat in range(lat_count):
            pairs.append(((lon ^ mask[1]) * lat_count + (lat ^ mask[0]), lon * lat_count + lat))
    return lax.ppermute(value, ("lon", "lat"), pairs)


def added(left, right):
    return (left.astype(F32) + right.astype(F32)).astype(BF16)


def odd(mask):
    lat, lon = lax.axis_index("lat") & mask[0], lax.axis_index("lon") & mask[1]
    parity = jnp.int32(0)
    for place in range(5):
        parity = parity ^ (lat >> place) ^ (lon >> place)
    return (parity & 1) != 0


def split(value, owner):
    half = value.shape[0] // 2
    up = odd(owner)
    return jnp.where(up, value[half:], value[:half]), jnp.where(up, value[:half], value[half:])


def halve(value, mask, owner):
    keep, send = split(value, owner)
    return added(keep, exchanged(send, mask))


def double(value, mask, owner):
    other = exchanged(value, mask)
    up = odd(owner)
    return jnp.concatenate([jnp.where(up, other, value), jnp.where(up, value, other)], axis=0)


CORE = (1, 0)


def sum_all(first, second, tables):
    if lax.axis_size("lat") != 16 or lax.axis_size("lon") != 16:
        return sum_small(first, second, tables)
    y_low, y_high = ((2, 0), (2, 0)), (0, 8)
    x_low, x_high = ((4, 0), (12, 0)), ((12, 0), (8, 0))
    z_low, z_mid, z_high = ((0, 1), (0, 5)), ((0, 2), (0, 6)), (0, 7)
    tie = lax.optimization_barrier

    second = halve(second, *x_low)
    first = halve(first, *y_low)
    first, second = tie((first, second))
    first, second = halve(first, *x_low), halve(second, *y_low)
    rows = first.shape[0]
    joined = halve(jnp.concatenate([first, second], axis=0), *x_high)
    joined, tables = tie((joined, tables))
    for mask, owner in (z_low, z_mid):
        keep, send = split(tables, owner)
        got = exchanged(jnp.concatenate([joined, send], axis=0), mask)
        joined, tables = added(joined, got[:rows]), added(keep, got[rows:])
    joined = jnp.concatenate([joined, tables], axis=0)
    for mask in (z_high, y_high):
        joined = added(joined, exchanged(joined, mask))
    joined, tables = tie((joined[:rows], joined[rows:]))
    joined, tables = double(joined, *x_high), double(tables, *z_mid)
    first, second, tables = tie((joined[:rows], joined[rows:], tables))
    first, second, tables = double(first, *x_low), double(second, *y_low), double(tables, *z_low)
    first, second, tables = tie((first, second, tables))
    first, second = double(first, *y_low), double(second, *x_low)
    first, second = tie((first, second))
    return first, exchanged(first, CORE), second, exchanged(second, CORE), tables


def sum_small(first, second, tables):
    def over(value, axis):
        for place in range(lax.axis_size(axis).bit_length() - 1):
            if axis == "lon" or place:
                value = added(value, exchanged(value, (1 << place, 0) if axis == "lat" else (0, 1 << place)))
        return value

    first, second = over(over(first, "lat"), "lon"), over(over(second, "lat"), "lon")
    return first, exchanged(first, CORE), second, exchanged(second, CORE), over(tables, "lon")


def unpack_kernel(
    upper_ref,
    first_own,
    first_other,
    second_own,
    second_other,
    tables_ref,
    gains_ref,
    in_ref,
    out_ref,
    up_ref,
    down_ref,
    grads_ref,
    rows_ref,
):
    half = ROWS // 2
    is_upper = jnp.broadcast_to(upper_ref[0] == 1, (1, 128))
    for block, (own, other) in enumerate(((first_own, first_other), (second_own, second_other))):

        def rows(start, stop, own=own, other=other):
            if start < half < stop:
                return jnp.concatenate([rows(start, half), rows(half, stop)], axis=0)
            lower = start < half
            start, stop = (start, stop) if lower else (start - half, stop - half)
            mine, theirs = own[start:stop].astype(F32), other[start:stop].astype(F32)
            return jnp.where(is_upper, theirs, mine) if lower else jnp.where(is_upper, mine, theirs)

        rows_ref[...] = tables_ref[block * TABLE_ROWS : (block + 1) * TABLE_ROWS].astype(F32)
        for part in range(4):
            in_ref[block, :, part * 128 : (part + 1) * 128] = rows(part * C, (part + 1) * C)
        shared = rows(768, 960)
        in_ref[block, :, 512:] = shared[:, :64]
        out_ref[block, :, :128] = rows(960, 1152)
        out_ref[block, :, 128:] = shared[:, 64:]
        for part in range(6):
            lanes = slice(part * 128, (part + 1) * 128)
            up_ref[block, :, lanes] = rows(1152 + part * C, 1152 + (part + 1) * C)
            down_ref[block, :, lanes] = rows(2304 + part * C, 2304 + (part + 1) * C)
        gains = rows(GAIN_ROWS, GAIN_ROWS + 16)
        gains_ref[block, 0:1, :128] = gains[0:1]
        gains_ref[block, 0:1, 128:] = gains[1:2, :64]
        gains_ref[block, 1:2, :128] = gains[2:3]
        gains_ref[block, 1:2, 128:] = gains[1:2, 64:]
        for slab in range(26):
            width = min(128, RELPOS - slab * 128)
            for level in range(2):
                start = slab * 12 + level * HEADS
                grads_ref[block, 0, :, level, slab * 128 : slab * 128 + width] = rows_ref[start : start + HEADS, :width]


def unpack(is_upper, *values):
    return call(
        unpack_kernel,
        (is_upper,),
        values,
        [
            shape_of((2, 2, C), F32),
            shape_of((2, C, 3 * C), F32),
            shape_of((2, C, C), F32),
            shape_of((2, C, FFN), F32),
            shape_of((2, C, FFN), F32),
            shape_of((2, 1, HEADS, 2, RELPOS), F32),
        ],
        [pltpu.VMEM((TABLE_ROWS, 128), F32)],
        1_000_000,
    )


def solution(mesh):
    placed = (
        P(None, "lat", "lon", None),
        P(None, "lat", "lon", None),
        P(None, "lat", "lon"),
        P(None, "lat"),
        P(),
        P(),
        P(),
        P(),
        P(),
        P(None, "lat", None, None, None),
    )
    return jax.shard_map(
        per_device,
        mesh=mesh,
        in_specs=placed,
        out_specs=(
            P(None, "lat", "lon", None),
            P(None, "lat", "lon", None),
            P(),
            P(),
            P(),
            P(),
            P(),
            P(None, "lat", None, None, None),
        ),
        check_vma=False,
    )
```

```python
import functools
import math

import jax
import jax.numpy as jnp
import numpy as np
from jax import lax
from jax.experimental import pallas as pl
from jax.experimental.pallas import tpu as pltpu
from jax.sharding import PartitionSpec as P

C = 192
HEADS = 6
HEAD = 32
FFN = 768
WIN_Z = 2
WIN_LAT = 6
WIN_LON = 12
WIN = 144
TOKENS = 2 * WIN
QUAD = 72
RELPOS = 3312
SPAN = 2 * WIN_LON - 1
ROWS = 3584
GAIN_ROWS = 3456
TABLE_ROWS = 320

EPSILON = 1e-05
NEGATIVE = -1000000000.0
SCALE = 1.0 / math.sqrt(HEAD)

F32 = jnp.float32
BF16 = jnp.bfloat16


def quadrant_rows():
    rows = np.zeros(TOKENS, np.int64)
    at = 0
    for lat_half in range(2):
        for lon_half in range(2):
            for level in range(4):
                for row in range(3):
                    for col in range(6):
                        rows[at] = (level * 6 + lat_half * 3 + row) * 12 + lon_half * 6 + col
                        at += 1
    return rows


def rolled_rows():
    rows = quadrant_rows()
    level, rest = rows // 72, rows % 72
    return ((level + 3) % 4) * 72 + rest


def one_hot(rows):
    picked = np.zeros((TOKENS, TOKENS), np.float32)
    picked[np.arange(TOKENS), rows] = 1.0
    return picked


def mm(left, right):
    return lax.dot_general(left, right, (((1,), (0,)), ((), ())), preferred_element_type=F32)


def mm_nt(left, right):
    return lax.dot_general(left, right, (((1,), (1,)), ((), ())), preferred_element_type=F32)


def eye(size):
    return (
        lax.broadcasted_iota(jnp.int32, (size, size), 0) == lax.broadcasted_iota(jnp.int32, (size, size), 1)
    ).astype(F32).astype(BF16)


def turned(value):
    return mm_nt(eye(value.shape[1]), value).astype(BF16)


def norm_stats(values):
    centre = values - jnp.mean(values, axis=-1, keepdims=True)
    inverse = lax.rsqrt(jnp.mean(centre * centre, axis=-1, keepdims=True) + EPSILON)
    return centre * inverse, inverse


def norm_backward(upstream, normal_hat, inverse):
    upstream_mean = jnp.mean(upstream, axis=-1, keepdims=True)
    cross_mean = jnp.mean(upstream * normal_hat, axis=-1, keepdims=True)
    return inverse * (upstream - upstream_mean - normal_hat * cross_mean)


def head_lanes(head):
    lane = lax.broadcasted_iota(jnp.int32, (1, C), 1)
    return ((lane >= head * HEAD) & (lane < (head + 1) * HEAD)).astype(F32).astype(BF16)


def pair_keys():
    row = lax.broadcasted_iota(jnp.int32, (512, 1), 0)
    within = row & 127
    third = (within >= SPAN).astype(jnp.int32) + (within >= 2 * SPAN).astype(jnp.int32)
    row_group = (row >> 7) * 3 + third
    row_offset = within - third * SPAN
    col = lax.broadcasted_iota(jnp.int32, (1, 256), 1)
    col_group = jnp.zeros_like(col)
    for group in range(1, 12):
        col_group = col_group + (col >= group * 12).astype(jnp.int32)
    col_place = col - col_group * 12
    usable = (row_group == col_group) & (within < 3 * SPAN) & (col < WIN)
    return jnp.where(usable, col_place + 11 - row_offset, -1).astype(F32).astype(BF16)


def pairs_of(keys, place):
    return jnp.where(keys == jnp.asarray(place, BF16), jnp.asarray(1, BF16), jnp.asarray(0, BF16))


def table_start(zs, zt, hs, ht):
    return (((zs * 2 + zt) * 6 + hs) * 6 + ht) * SPAN


def spread_bias(table_ref, row_ref, shaped_ref, bias_ref):
    for head in range(HEADS):
        row_ref[head * 2 : head * 2 + 2, :RELPOS] = table_ref[head].astype(F32)
    row = row_ref[: 2 * HEADS]
    for zs in range(2):
        for zt in range(2):
            for group in range(2):
                for ht in range(6):
                    pieces = []
                    for hs in range(group * 3, group * 3 + 3):
                        start = table_start(zs, zt, hs, ht)
                        pieces.append(row[:, start : start + SPAN])
                    pieces.append(jnp.zeros((2 * HEADS, 128 - 3 * SPAN), F32))
                    target = pl.ds(zt * 6 + ht, 2 * HEADS, stride=12)
                    shaped_ref[zs * 2 + group, target, :] = jnp.concatenate(pieces, axis=1)
    keys = pair_keys()
    shaped = jnp.concatenate([shaped_ref[part, :WIN].astype(BF16) for part in range(4)], axis=1)
    for col in range(WIN_LON):
        spread = mm(shaped, pairs_of(keys, col))
        bias_ref[0, pl.ds(col, WIN, stride=12), :] = spread[:, :128]
        bias_ref[1, pl.ds(col, WIN, stride=12), :] = spread[:, 128:]


def collect_bias(scaled_ref, levels, row_ref, shaped_ref, grads_ref, out_ref):
    for place in range(2 * HEADS):
        rows = slice(place * WIN, (place + 1) * WIN)
        piece = scaled_ref[place].astype(F32)
        grads_ref[0, rows] = piece[:, :128]
        grads_ref[1, rows] = jnp.concatenate([piece[:, 128:], jnp.zeros((WIN, 256 - WIN), F32)], axis=1)
    keys = pair_keys()
    total = jnp.zeros((WIN, 512), F32)
    for col in range(WIN_LON):
        left = grads_ref[0, pl.ds(col, WIN, stride=12), :]
        right = grads_ref[1, pl.ds(col, WIN, stride=12), :]
        piece = jnp.concatenate([left, right], axis=1).astype(BF16)
        total = total + mm_nt(piece, pairs_of(keys, col))
    total = total * (1.0 / SCALE)
    for part in range(4):
        shaped_ref[part, :WIN] = total[:, part * 128 : (part + 1) * 128]
    row_ref[...] = jnp.zeros_like(row_ref)
    for zs in range(2):
        for zt in range(2):
            for group in range(2):
                for ht in range(6):
                    pieces = [
                        shaped_ref[zs * 2 + group, pl.ds(window * 72 + zt * 6 + ht, HEADS, stride=12), :]
                        for window in range(2)
                    ]
                    for level in range(2):
                        chosen = jnp.zeros((HEADS, 128), F32)
                        for window in range(2):
                            chosen = chosen + jnp.where(levels[window] == level, pieces[window], 0.0)
                        for index in range(3):
                            start = table_start(zs, zt, group * 3 + index, ht)
                            row_ref[level * 8 : level * 8 + HEADS, start : start + SPAN] = chosen[
                                :, index * SPAN : (index + 1) * SPAN
                            ]
    for slab in range(26):
        lanes = slice(slab * 128, (slab + 1) * 128)
        rows = jnp.concatenate([row_ref[:HEADS, lanes], row_ref[8 : 8 + HEADS, lanes]], axis=0)
        shaped_ref[slab // 13, slab % 13 * 12 : slab % 13 * 12 + 12] = rows
    out_ref[...] = jnp.concatenate(
        [shaped_ref[0, :156], shaped_ref[1, :156], jnp.zeros((TABLE_ROWS - 312, 128), F32)], axis=0
    ).astype(BF16)


def load_tiles(bias_ref, level, head):
    rows = pl.ds(pl.multiple_of((head * 2 + level) * WIN, 8), WIN)
    return jnp.concatenate([bias_ref[0, rows, :], bias_ref[1, rows, : WIN - 128]], axis=1)


def attention(normed, in_weight, bias_of, weights_ref):
    eye_c = eye(C)
    weight_q, weight_k, weight_v = in_weight[:, :C], in_weight[:, C : 2 * C], in_weight[:, 2 * C :]
    kept = []
    mixed = []
    for window in range(2):
        rows = normed[window * WIN : (window + 1) * WIN]
        keys = mm(rows, weight_k).astype(BF16)
        values = mm(rows, weight_v).astype(BF16)
        queries = mm(rows, weight_q).astype(BF16)
        queries_t = mm_nt(eye_c, queries).astype(BF16)
        keys_t = mm_nt(eye_c, keys).astype(BF16)
        values_t = mm_nt(eye_c, values).astype(BF16)
        parts = []
        for head in range(HEADS):
            own = keys * head_lanes(head)
            scores = mm(own, queries_t) * SCALE + bias_of(window, head)
            weights = jnp.exp(scores - jnp.max(scores, axis=0, keepdims=True))
            weights = weights * (1.0 / jnp.sum(weights, axis=0, keepdims=True))
            weights = weights.astype(BF16)
            weights_ref[window * HEADS + head] = weights
            parts.append(mm(values_t[head * HEAD : (head + 1) * HEAD], weights))
        mixed.append(jnp.concatenate(parts, axis=0).astype(BF16))
        kept.append((queries_t, keys_t, values))
    return kept, mixed


def feed_forward(hidden, gain, up_weight):
    hat, inverse = norm_stats(hidden)
    normed = (hat * gain).astype(BF16)
    return hat, inverse, normed, mm(normed, up_weight)


def gelu_parts(expanded):
    cumulative = 0.5 * (1.0 + lax.erf(expanded * (1.0 / math.sqrt(2.0))))
    slope = cumulative + expanded * jnp.exp(-0.5 * expanded * expanded) * (1.0 / math.sqrt(2.0 * math.pi))
    return (expanded * cumulative).astype(BF16), slope


def natural_mixed(mixed):
    eye_w = eye(WIN)
    return jnp.concatenate([mm_nt(eye_w, part) for part in mixed], axis=0).astype(BF16)


def pack(packed_ref, start, value):
    height = value.shape[0]
    for part in range(value.shape[1] // 128):
        rows = slice(start + part * height, start + (part + 1) * height)
        packed_ref[rows] = value[:, part * 128 : (part + 1) * 128].astype(BF16)


def backward(
    grad,
    active,
    slope,
    second_hat,
    second_inverse,
    second_norm,
    mixed,
    attended,
    weights_ref,
    first_hat,
    first_inverse,
    first_norm,
    gain_one,
    gain_two,
    in_weight,
    out_weight,
    up_weight,
    down_weight,
    scaled_ref,
    packed_ref,
):
    eye_c = eye(C)
    grad_half = grad.astype(BF16)
    pack(packed_ref, 2304, mm(turned(grad_half), active))
    grad_expanded = (mm(grad_half, down_weight) * slope).astype(BF16)
    normed_t = turned(second_norm)
    pack(packed_ref, 1152, mm(normed_t, grad_expanded))
    grad_second = mm_nt(grad_expanded, up_weight)
    gain_two_grad = jnp.sum(grad_second * second_hat, axis=0, keepdims=True)
    grad_hidden = (grad + norm_backward(grad_second * gain_two, second_hat, second_inverse)).astype(BF16)
    grad_out = mm(mixed[0], grad_hidden[:WIN]) + mm(mixed[1], grad_hidden[WIN:])
    packed_ref[960:1152] = grad_out[:, :128].astype(BF16)
    grad_mixed = mm_nt(grad_hidden, out_weight).astype(BF16)
    projected = []
    for window in range(2):
        queries_t, keys_t, values = attended[window]
        upstream_t = mm_nt(eye_c, grad_mixed[window * WIN : (window + 1) * WIN]).astype(BF16)
        grad_q, grad_k, grad_v = [], [], []
        for head in range(HEADS):
            lanes = slice(head * HEAD, (head + 1) * HEAD)
            half = weights_ref[window * HEADS + head]
            weights = half.astype(F32)
            own = values * head_lanes(head)
            grad_weights = mm(own, upstream_t)
            inner = jnp.sum(grad_weights * weights, axis=0, keepdims=True)
            grad_scores = weights * (grad_weights - inner)
            scaled = (grad_scores * SCALE).astype(BF16)
            scaled_ref[window * HEADS + head] = scaled
            grad_v.append(mm_nt(upstream_t[lanes], half))
            grad_q.append(mm(keys_t[lanes], scaled))
            grad_k.append(mm_nt(queries_t[lanes], scaled))
        projected_t = jnp.concatenate(grad_q + grad_k + grad_v, axis=0).astype(BF16)
        projected.append(mm_nt(eye(WIN), projected_t))
    projected = jnp.concatenate(projected, axis=0).astype(BF16)
    first_t = turned(first_norm)
    grad_in = mm(first_t, projected)
    pack(packed_ref, 0, grad_in[:, :512])
    packed_ref[768:960] = jnp.concatenate([grad_in[:, 512:], grad_out[:, 128:]], axis=1).astype(BF16)
    grad_first = mm_nt(projected, in_weight)
    gain_one_grad = jnp.sum(grad_first * first_hat, axis=0, keepdims=True)
    gain_rows = jnp.concatenate(
        [
            gain_one_grad[:, :128],
            jnp.concatenate([gain_one_grad[:, 128:], gain_two_grad[:, 128:]], axis=1),
            gain_two_grad[:, :128],
            jnp.zeros((ROWS - GAIN_ROWS - 3, 128), F32),
        ],
        axis=0,
    )
    packed_ref[GAIN_ROWS:ROWS] = gain_rows.astype(BF16)
    return (
        grad_hidden.astype(F32) + norm_backward(grad_first * gain_one, first_hat, first_inverse)
    ).astype(BF16)


def load_grid(grid_ref, rows_ref):
    for row in range(6):
        for col in range(12):
            piece = grid_ref[row, col].astype(F32)
            target = pl.ds(row * 12 + col, 4, stride=72)
            rows_ref[0, target, :] = piece[:, :128]
            rows_ref[1, target, :] = jnp.concatenate([piece[:, 128:], jnp.zeros((4, 64), F32)], axis=1)
    return jnp.concatenate([rows_ref[0], rows_ref[1][:, :64]], axis=1)


def store_grid(rows, rows_ref, grid_ref):
    rows_ref[0] = rows[:, :128]
    rows_ref[1] = jnp.concatenate([rows[:, 128:], jnp.zeros((TOKENS, 64), F32)], axis=1)
    for row in range(6):
        for col in range(12):
            source = pl.ds(row * 12 + col, 4, stride=72)
            piece = jnp.concatenate([rows_ref[0, source, :], rows_ref[1, source, :][:, :64]], axis=1)
            grid_ref[row, col] = piece.astype(BF16)


def block_weights(gains_ref, in_ref, out_ref, up_ref, down_ref):
    gains = gains_ref[...]
    return gains[0:1], gains[1:2], in_ref[...], out_ref[...], up_ref[...], down_ref[...]


def write_halves(upper_ref, packed_ref, keep_ref, send_ref):
    half = ROWS // 2
    is_upper = upper_ref[0] == 1

    @pl.when(is_upper)
    def _():
        keep_ref[...] = packed_ref[half:]
        send_ref[...] = packed_ref[:half]

    @pl.when(jnp.logical_not(is_upper))
    def _():
        keep_ref[...] = packed_ref[:half]
        send_ref[...] = packed_ref[half:]


def first_kernel(
    levels_ref,
    inputs_ref,
    grad_ref,
    gains_ref,
    in_ref,
    out_ref,
    up_ref,
    down_ref,
    table_ref,
    order_ref,
    quad_0,
    quad_1,
    quad_2,
    quad_3,
    weights_out,
    turned_out,
    flat_out,
    rows_ref,
    row_ref,
    shaped_ref,
    bias_ref,
):
    levels = [levels_ref[0, 0], levels_ref[0, 1]]
    gain_one, gain_two, in_weight, out_weight, up_weight, down_weight = block_weights(
        gains_ref, in_ref, out_ref, up_ref, down_ref
    )
    order = order_ref[...]
    grad_quads = mm(order, load_grid(grad_ref, rows_ref).astype(BF16))
    flat = load_grid(inputs_ref, rows_ref)
    flat_out[0] = flat.astype(BF16)
    spread_bias(table_ref, row_ref, shaped_ref, bias_ref)
    hat, _ = norm_stats(flat)
    normed = (hat * gain_one).astype(BF16)
    attended, mixed = attention(
        normed, in_weight, lambda window, head: load_tiles(bias_ref, levels[window], head), weights_out
    )
    for window in range(2):
        turned_out[window, 0] = attended[window][0]
        turned_out[window, 1] = attended[window][1]
        turned_out[window, 2] = mixed[window]
        flat_out[2, window * WIN : (window + 1) * WIN] = attended[window][2]
    hidden = (flat + mm(natural_mixed(mixed), out_weight)).astype(BF16)
    flat_out[1] = hidden
    hidden = hidden.astype(F32)
    _, _, _, expanded = feed_forward(hidden, gain_two, up_weight)
    active = (expanded * 0.5 * (1.0 + lax.erf(expanded * (1.0 / math.sqrt(2.0))))).astype(BF16)
    result = (hidden + mm_nt(active, down_weight)).astype(BF16)
    result_quads = mm(order, result)
    for index, quad in enumerate((quad_0, quad_1, quad_2, quad_3)):
        rows = slice(index * QUAD, (index + 1) * QUAD)
        quad[...] = jnp.concatenate([result_quads[rows], grad_quads[rows]], axis=0).astype(BF16)


def region_row(region_ref, window):
    pieces = [region_ref[row, window * 2 + level : window * 2 + level + 1, :] for level in range(2) for row in range(6)]
    return jnp.concatenate(pieces, axis=1)


def prepare_kernel(
    levels_ref, region_ref, table_ref, bias_out, row_ref, shaped_ref, bias_ref
):
    levels = [levels_ref[0, 0], levels_ref[0, 1]]
    spread_bias(table_ref, row_ref, shaped_ref, bias_ref)
    diagonal = lax.broadcasted_iota(jnp.int32, (WIN, WIN), 0) == lax.broadcasted_iota(jnp.int32, (WIN, WIN), 1)
    for window in range(2):
        across = region_row(region_ref, window).astype(F32)
        down = jnp.sum(jnp.where(diagonal, across, 0.0), axis=1, keepdims=True)
        same = across == down
        for head in range(HEADS):
            bias = jnp.where(same, load_tiles(bias_ref, levels[window], head), NEGATIVE)
            bias_out[window * HEADS + head] = bias.astype(BF16)


def second_kernel(
    upper_ref,
    quad_0,
    quad_1,
    quad_2,
    quad_3,
    bias_ref,
    gains_ref,
    in_ref,
    out_ref,
    up_ref,
    down_ref,
    ahead_ref,
    back_ref,
    back_0,
    back_1,
    back_2,
    back_3,
    keep_ref,
    send_ref,
    scaled_ref,
    weights_ref,
    packed_ref,
):
    quads = [quad[...].astype(F32) for quad in (quad_0, quad_1, quad_2, quad_3)]
    ahead = ahead_ref[...]
    flat = mm(ahead, jnp.concatenate([quad[:QUAD] for quad in quads], axis=0).astype(BF16))
    grad = mm(ahead, jnp.concatenate([quad[QUAD:] for quad in quads], axis=0).astype(BF16))
    gain_one, gain_two, in_weight, out_weight, up_weight, down_weight = block_weights(
        gains_ref, in_ref, out_ref, up_ref, down_ref
    )
    first_hat, first_inverse = norm_stats(flat)
    first_norm = (first_hat * gain_one).astype(BF16)
    attended, mixed = attention(
        first_norm, in_weight, lambda window, head: bias_ref[window * HEADS + head].astype(F32), weights_ref
    )
    hidden = (flat + mm(natural_mixed(mixed), out_weight)).astype(BF16).astype(F32)
    second_hat, second_inverse, second_norm, expanded = feed_forward(hidden, gain_two, up_weight)
    active, slope = gelu_parts(expanded)
    result = (hidden + mm_nt(active, down_weight)).astype(BF16)
    grad_in = backward(
        grad, active, slope, second_hat, second_inverse, second_norm, mixed, attended, weights_ref,
        first_hat, first_inverse, first_norm, gain_one, gain_two, in_weight, out_weight, up_weight,
        down_weight, scaled_ref, packed_ref,
    )
    back = back_ref[...]
    result_quads, grad_quads = mm(back, result), mm(back, grad_in)
    for index, quad in enumerate((back_0, back_1, back_2, back_3)):
        rows = slice(index * QUAD, (index + 1) * QUAD)
        quad[...] = jnp.concatenate([result_quads[rows], grad_quads[rows]], axis=0).astype(BF16)
    write_halves(upper_ref, packed_ref, keep_ref, send_ref)


def collect_kernel(levels_ref, scaled_ref, tables_out, row_ref, shaped_ref, grads_ref):
    levels = [levels_ref[0, 0], levels_ref[0, 1]]
    collect_bias(scaled_ref, levels, row_ref, shaped_ref, grads_ref, tables_out)


def finish_kernel(
    levels_ref, scaled_ref, second_tables_ref, tables_out, row_ref, shaped_ref, grads_ref
):
    levels = [levels_ref[0, 0], levels_ref[0, 1]]
    collect_bias(scaled_ref, levels, row_ref, shaped_ref, grads_ref, tables_out.at[:TABLE_ROWS])
    tables_out[TABLE_ROWS:] = second_tables_ref[...]


def activation_kernel(flat_ref, gains_ref, up_ref, active_out, slope_out):
    _, _, _, expanded = feed_forward(flat_ref[1].astype(F32), gains_ref[1:2], up_ref[...])
    active, slope = gelu_parts(expanded)
    active_out[...] = active
    slope_out[...] = slope.astype(BF16)


def third_kernel(
    upper_ref,
    quad_0,
    quad_1,
    quad_2,
    quad_3,
    weights_ref,
    turned_ref,
    flat_ref,
    active_ref,
    slope_ref,
    gains_ref,
    in_ref,
    out_ref,
    up_ref,
    down_ref,
    natural_ref,
    keep_ref,
    send_ref,
    rows_out,
    scaled_ref,
    packed_ref,
):
    quads = [quad[...].astype(F32) for quad in (quad_0, quad_1, quad_2, quad_3)]
    grad = mm(natural_ref[...], jnp.concatenate([quad[QUAD:] for quad in quads], axis=0).astype(BF16))
    gain_one, gain_two, in_weight, out_weight, up_weight, down_weight = block_weights(
        gains_ref, in_ref, out_ref, up_ref, down_ref
    )
    first_hat, first_inverse = norm_stats(flat_ref[0].astype(F32))
    first_norm = (first_hat * gain_one).astype(BF16)
    second_hat, second_inverse = norm_stats(flat_ref[1].astype(F32))
    second_norm = (second_hat * gain_two).astype(BF16)
    attended = [
        (turned_ref[window, 0], turned_ref[window, 1], flat_ref[2, window * WIN : (window + 1) * WIN])
        for window in range(2)
    ]
    mixed = [turned_ref[0, 2], turned_ref[1, 2]]
    rows_out[...] = backward(
        grad, active_ref[...], slope_ref[...].astype(F32), second_hat, second_inverse, second_norm, mixed,
        attended, weights_ref, first_hat, first_inverse, first_norm, gain_one, gain_two, in_weight,
        out_weight, up_weight, down_weight, scaled_ref, packed_ref,
    )
    write_halves(upper_ref, packed_ref, keep_ref, send_ref)


def grids_kernel(quad_0, quad_1, quad_2, quad_3, natural_ref, grad_rows_ref, blocks_out, grad_out, rows_ref):
    quads = [quad[:QUAD].astype(F32) for quad in (quad_0, quad_1, quad_2, quad_3)]
    blocks = mm(natural_ref[...], jnp.concatenate(quads, axis=0).astype(BF16))
    store_grid(blocks, rows_ref, blocks_out)
    store_grid(grad_rows_ref[...].astype(F32), rows_ref, grad_out)


SMEM = pl.BlockSpec(memory_space=pltpu.SMEM)
VMEM = pl.BlockSpec(memory_space=pltpu.VMEM)
ANY = pl.BlockSpec(memory_space=pl.ANY)
FAR_LIMIT = 60 * 1024 * 1024
NEAR_LIMIT = 28 * 1024 * 1024


class Part:
    def __init__(self, array, block):
        self.array, self.block = array, block
        self.lead = sum(size == 1 for size in array.shape[1:]) + 1
        self.shape, self.dtype = array.shape[self.lead :], array.dtype

    def spec(self):
        return pl.BlockSpec(
            (None,) * self.lead + self.shape, lambda *_: (self.block,) + (0,) * (self.lead - 1 + len(self.shape))
        )

    def of(self, ref):
        return ref.at[(self.block,) + (0,) * (self.lead - 1)]


class Near:
    def __init__(self, array):
        self.array = array


def whole(array):
    return pl.BlockSpec(array.shape, lambda *_: (0,) * len(array.shape))


def call(kernel, scalars, operands, out_shapes, scratch, flops):
    specs = [operand.spec() if isinstance(operand, Part) else whole(operand) for operand in operands]
    arrays = [operand.array if isinstance(operand, Part) else operand for operand in operands]
    return pl.pallas_call(
        kernel,
        grid=(1,),
        in_specs=[SMEM] * len(scalars) + specs,
        out_specs=[whole(shape) for shape in out_shapes],
        out_shape=out_shapes,
        scratch_shapes=scratch,
        compiler_params=pltpu.CompilerParams(vmem_limit_bytes=FAR_LIMIT),
        cost_estimate=pl.CostEstimate(flops=flops, bytes_accessed=4_000_000, transcendentals=1_000_000),
    )(*scalars, *arrays)


def near_call(kernel, scalars, operands, out_shapes, scratch, flops, near_outs=(), carried=()):
    def is_near(operand):
        return isinstance(operand, Near)

    def plain_array(operand):
        return operand.array if isinstance(operand, (Near, Part)) else operand

    def source_of(operand, ref):
        return operand.of(ref) if isinstance(operand, Part) else ref

    far = [operand for operand in operands if not is_near(operand)]
    far_outs = [shape for place, shape in enumerate(out_shapes) if place not in near_outs]

    def body(*refs):
        refs = list(refs)

        def take(count):
            taken = refs[:count]
            del refs[:count]
            return taken

        scalar_refs, operand_refs, carried_refs = take(len(scalars)), take(len(operands)), take(len(carried))
        out_refs, carried_outs = take(len(out_shapes)), take(len(carried))
        scratch_refs, buffers, out_buffers = take(len(scratch)), take(len(far)), take(len(far_outs))
        sems, carried_sems, out_sems = refs
        inputs, arriving = [], []
        for operand, ref in zip(operands, operand_refs, strict=True):
            if is_near(operand):
                inputs.append(ref)
                continue
            place = len(arriving)
            arriving.append(pltpu.make_async_copy(source_of(operand, ref), buffers[place], sems.at[place]))
            inputs.append(buffers[place])
        for copy in arriving:
            copy.start()
        passing = [
            pltpu.make_async_copy(source_of(operand, ref), target, carried_sems.at[place])
            for place, (operand, ref, target) in enumerate(zip(carried, carried_refs, carried_outs, strict=True))
        ]
        for copy in passing:
            copy.start()
        for copy in arriving:
            copy.wait()
        outputs, leaving = [], []
        for place, ref in enumerate(out_refs):
            if place in near_outs:
                outputs.append(ref)
                continue
            outputs.append(out_buffers[len(leaving)])
            leaving.append(pltpu.make_async_copy(outputs[-1], ref, out_sems.at[len(leaving)]))
        kernel(*scalar_refs, *inputs, *outputs, *scratch_refs)
        for copy in leaving:
            copy.start()
        for copy in passing + leaving:
            copy.wait()

    return pl.pallas_call(
        body,
        in_specs=[SMEM] * len(scalars)
        + [VMEM if is_near(operand) else ANY for operand in operands]
        + [ANY] * len(carried),
        out_specs=[VMEM if place in near_outs else ANY for place in range(len(out_shapes))] + [VMEM] * len(carried),
        out_shape=[*out_shapes, *[shape_of(operand.shape, operand.dtype) for operand in carried]],
        scratch_shapes=[
            *scratch,
            *[pltpu.VMEM(operand.shape, operand.dtype) for operand in far],
            *[pltpu.VMEM(shape.shape, shape.dtype) for shape in far_outs],
            pltpu.SemaphoreType.DMA((max(len(far), 1),)),
            pltpu.SemaphoreType.DMA((max(len(carried), 1),)),
            pltpu.SemaphoreType.DMA((max(len(far_outs), 1),)),
        ],
        compiler_params=pltpu.CompilerParams(vmem_limit_bytes=NEAR_LIMIT),
        cost_estimate=pl.CostEstimate(flops=flops, bytes_accessed=4_000_000, transcendentals=1_000_000),
    )(*scalars, *[plain_array(operand) for operand in operands], *[plain_array(operand) for operand in carried])


def shape_of(shape, dtype):
    return jax.ShapeDtypeStruct(shape, dtype)


def shifted(value, lat_steps, lon_steps):
    lon_count, lat_count = lax.axis_size("lon"), lax.axis_size("lat")
    pairs = []
    for lon in range(lon_count):
        for lat in range(lat_count):
            source = ((lon + lon_steps) % lon_count) * lat_count + (lat + lat_steps) % lat_count
            pairs.append((source, lon * lat_count + lat))
    return lax.ppermute(value, ("lon", "lat"), pairs)


def per_device(
    inputs,
    grad_out,
    region,
    bias_level,
    norm_gains,
    in_weight,
    out_weight,
    up_weight,
    down_weight,
    bias_tables,
):
    weights = (norm_gains, in_weight, out_weight, up_weight, down_weight.transpose(0, 2, 1))
    first_weights = [Part(array, 0) for array in weights]
    second_weights = [Part(array, 1) for array in weights]
    inputs, grad_out = inputs.transpose(1, 2, 0, 3), grad_out.transpose(1, 2, 0, 3)
    bias_tables = bias_tables.transpose(0, 1, 3, 2, 4)
    bias_level = bias_level.T
    quadrant = one_hot(quadrant_rows())
    rolled = one_hot(rolled_rows())
    half = [jnp.asarray(array, BF16) for array in (quadrant, quadrant.T, rolled, rolled.T)]
    to_quads, from_quads, rolled_back, rolled_ahead = half
    is_upper = odd(core_step()[1]).reshape(1)

    quad_shape = shape_of((2 * QUAD, C), BF16)
    grid_shape = shape_of((6, 12, 4, C), BF16)
    half_shape = shape_of((ROWS // 2, 128), BF16)
    table_shape = shape_of((TABLE_ROWS, 128), BF16)
    weights_shape = (2 * HEADS, WIN, WIN)
    grads_scratch = pltpu.VMEM((2, 2 * HEADS * WIN, 128), F32)
    row_scratch = pltpu.VMEM((16, 26 * 128), F32)
    shaped_scratch = pltpu.VMEM((4, 2 * 72 + 16, 128), F32)
    bias_scratch = pltpu.VMEM((2, 2 * HEADS * WIN, 128), F32)
    rows_scratch = pltpu.VMEM((2, TOKENS, 128), F32)
    packed_scratch = pltpu.VMEM((ROWS, 128), BF16)

    quads = call(
        first_kernel,
        (bias_level,),
        (inputs, grad_out, *first_weights, Part(bias_tables, 0), to_quads),
        [quad_shape] * 4
        + [
            shape_of(weights_shape, BF16),
            shape_of((2, 3, C, WIN), BF16),
            shape_of((3, TOKENS, C), BF16),
        ],
        [rows_scratch, row_scratch, shaped_scratch, bias_scratch],
        1_000_000_000,
    )
    stored = list(quads[4:])
    ahead = (
        quads[3],
        shifted(quads[2], 0, 1),
        shifted(quads[1], 1, 0),
        shifted(quads[0], 1, 1),
    )
    (bias,) = call(
        prepare_kernel,
        (bias_level,),
        (region.transpose(1, 0, 2), Part(bias_tables, 1)),
        [shape_of(weights_shape, BF16)],
        [row_scratch, shaped_scratch, bias_scratch],
        500_000_000,
    )
    *back, second_keep, second_send, second_scaled = call(
        second_kernel,
        (is_upper,),
        (*ahead, bias, *second_weights, rolled_ahead, rolled_back),
        [quad_shape] * 4 + [half_shape, half_shape, shape_of(weights_shape, BF16)],
        [pltpu.VMEM(weights_shape, BF16), packed_scratch],
        3_000_000_000,
    )
    home = [
        shifted(back[3], -1, -1),
        shifted(back[2], -1, 0),
        shifted(back[1], 0, -1),
        back[0],
    ]
    home[3], stored[2] = tie((home[3], stored[2]))
    active, slope, *first_near = near_call(
        activation_kernel,
        (),
        (stored[2], first_weights[0], first_weights[3]),
        [shape_of((TOKENS, FFN), BF16), shape_of((TOKENS, FFN), BF16)],
        [],
        300_000_000,
        (0, 1),
        (home[3], *stored, *first_weights, from_quads),
    )
    second_got = exchanged(second_send, core_step()[0])
    first_keep, first_send, grad_rows, first_scaled = near_call(
        third_kernel,
        (is_upper,),
        tuple(map(Near, (*home[:3], *first_near[:4], active, slope, *first_near[4:]))),
        [half_shape, half_shape, shape_of((TOKENS, C), BF16), shape_of(weights_shape, BF16)],
        [packed_scratch],
        2_000_000_000,
    )
    blocks_out, grad_inputs = near_call(
        grids_kernel,
        (),
        (*home, from_quads, grad_rows),
        [grid_shape, grid_shape],
        [rows_scratch],
        100_000_000,
    )

    def collect(kernel, rows, *operands):
        return near_call(
            kernel,
            (bias_level,),
            operands,
            [shape_of((rows, 128), BF16)],
            [row_scratch, shaped_scratch, grads_scratch],
            500_000_000,
        )[0]

    first_got = exchanged(first_send, core_step()[0])
    second = added(second_keep, second_got)
    first = added(first_keep, first_got)
    first, second, first_scaled, second_scaled = tie((first, second, first_scaled, second_scaled))
    second_tables = collect(collect_kernel, TABLE_ROWS, second_scaled)
    tables = collect(finish_kernel, 2 * TABLE_ROWS, first_scaled, second_tables)
    totals = unpack(is_upper, *sum_all(first, second, tables, second_tables))
    gains, grad_in, grad_out_weight, grad_up, grad_down, grad_tables = totals
    return (
        blocks_out.transpose(2, 0, 1, 3),
        grad_inputs.transpose(2, 0, 1, 3),
        gains,
        grad_in,
        grad_out_weight,
        grad_up,
        grad_down.transpose(0, 2, 1),
        grad_tables.transpose(0, 1, 3, 2, 4),
    )


def exchanged(value, mask):
    lon_count, lat_count = lax.axis_size("lon"), lax.axis_size("lat")
    pairs = []
    for lon in range(lon_count):
        for lat in range(lat_count):
            pairs.append(((lon ^ mask[1]) * lat_count + (lat ^ mask[0]), lon * lat_count + lat))
    return lax.ppermute(value, ("lon", "lat"), pairs)


def added(left, right):
    return (left.astype(F32) + right.astype(F32)).astype(BF16)


def odd(mask):
    lat, lon = lax.axis_index("lat") & mask[0], lax.axis_index("lon") & mask[1]
    parity = jnp.int32(0)
    for place in range(5):
        parity = parity ^ (lat >> place) ^ (lon >> place)
    return parity & 1


def split(value, owner):
    half = value.shape[0] // 2
    up = odd(owner) != 0
    return jnp.where(up, value[half:], value[:half]), jnp.where(up, value[:half], value[half:])


def halve(value, mask, owner):
    keep, send = split(value, owner)
    return added(keep, exchanged(send, mask))


def double(value, mask, owner):
    other = exchanged(value, mask)
    up = odd(owner) != 0
    return jnp.concatenate([jnp.where(up, other, value), jnp.where(up, value, other)], axis=0)


def tie(values):
    return lax.optimization_barrier(values)


def core_step():
    return (1, 0), (1, 0)


def sum_all(first, second, tables, second_tables):
    core = core_step()[0]
    if lax.axis_size("lat") != 16 or lax.axis_size("lon") != 16:
        return sum_small(first, second, tables)
    y_low, y_high = ((2, 0), (2, 0)), (0, 8)
    x_low, x_high = ((4, 0), (12, 0)), ((12, 0), (8, 0))
    z_low, z_mid, z_high = ((0, 1), (0, 5)), ((0, 2), (0, 6)), (0, 7)

    first, second = halve(first, *y_low), halve(second, *x_low)
    first, second, second_tables = tie((first, second, second_tables))
    first, second = halve(first, *x_low), halve(second, *y_low)
    first, second = tie((first, second))
    rows = first.shape[0]
    joined = halve(jnp.concatenate([first, second], axis=0), *x_high)
    joined, tables = tie((joined, tables))
    for mask, owner in (z_low, z_mid):
        keep, send = split(tables, owner)
        got = exchanged(jnp.concatenate([joined, send], axis=0), mask)
        joined, tables = added(joined, got[:rows]), added(keep, got[rows:])
    joined = jnp.concatenate([joined, tables], axis=0)
    for mask in (z_high, y_high):
        joined = added(joined, exchanged(joined, mask))
    joined, tables = tie((joined[:rows], joined[rows:]))
    joined, tables = double(joined, *x_high), double(tables, *z_mid)
    first, second, tables = tie((joined[:rows], joined[rows:], tables))
    first, second, tables = double(first, *x_low), double(second, *y_low), double(tables, *z_low)
    first, second, tables = tie((first, second, tables))
    first, second = double(first, *y_low), double(second, *x_low)
    first, second = tie((first, second))
    return first, exchanged(first, core), second, exchanged(second, core), tables


def sum_small(first, second, tables):
    def over(value, axis):
        for place in range(lax.axis_size(axis).bit_length() - 1):
            if axis == "lon" or place:
                value = added(value, exchanged(value, (1 << place, 0) if axis == "lat" else (0, 1 << place)))
        return value

    core = core_step()[0]
    first, second = over(over(first, "lat"), "lon"), over(over(second, "lat"), "lon")
    return first, exchanged(first, core), second, exchanged(second, core), over(tables, "lon")


def unpack_kernel(upper_ref, first_own, first_other, second_own, second_other, tables_ref, *refs):
    results, (rows_ref, *buffers, sems) = refs[:6], refs[6:]
    gains_ref, in_ref, out_ref, up_ref, down_ref, grads_ref = buffers
    half = ROWS // 2
    is_upper = jnp.broadcast_to(upper_ref[0] == 1, (1, 128))
    copies = []

    def leave(index, block):
        copy = pltpu.make_async_copy(buffers[index].at[block], results[index].at[block], sems.at[index, block])
        copy.start()
        copies.append(copy)

    for block, (own, other) in enumerate(((first_own, first_other), (second_own, second_other))):

        def rows(start, stop, own=own, other=other):
            if start < half < stop:
                return jnp.concatenate([rows(start, half), rows(half, stop)], axis=0)
            lower = start < half
            start, stop = (start, stop) if lower else (start - half, stop - half)
            mine, theirs = own[start:stop].astype(F32), other[start:stop].astype(F32)
            return jnp.where(is_upper, theirs, mine) if lower else jnp.where(is_upper, mine, theirs)

        for index, (ref, start) in enumerate(((up_ref, 1152), (down_ref, 2304))):
            for part in range(6):
                lanes = slice(part * 128, (part + 1) * 128)
                ref[block, :, lanes] = rows(start + part * C, start + (part + 1) * C)
            leave(3 + index, block)
        for part in range(4):
            in_ref[block, :, part * 128 : (part + 1) * 128] = rows(part * C, (part + 1) * C)
        shared = rows(768, 960)
        in_ref[block, :, 512:] = shared[:, :64]
        leave(1, block)
        out_ref[block, :, :128] = rows(960, 1152)
        out_ref[block, :, 128:] = shared[:, 64:]
        leave(2, block)
        rows_ref[...] = tables_ref[block * TABLE_ROWS : (block + 1) * TABLE_ROWS].astype(F32)
        for slab in range(26):
            width = min(128, RELPOS - slab * 128)
            for level in range(2):
                start = slab * 12 + level * HEADS
                grads_ref[block, 0, :, level, slab * 128 : slab * 128 + width] = rows_ref[start : start + HEADS, :width]
        leave(5, block)
        gains = rows(GAIN_ROWS, GAIN_ROWS + 16)
        gains_ref[block, 0:1, :128] = gains[0:1]
        gains_ref[block, 0:1, 128:] = gains[1:2, :64]
        gains_ref[block, 1:2, :128] = gains[2:3]
        gains_ref[block, 1:2, 128:] = gains[1:2, 64:]
        leave(0, block)
    for copy in copies:
        copy.wait()


def unpack(is_upper, *values):
    shapes = [
        (2, 2, C),
        (2, C, 3 * C),
        (2, C, C),
        (2, C, FFN),
        (2, C, FFN),
        (2, 1, HEADS, 2, RELPOS),
    ]
    return pl.pallas_call(
        unpack_kernel,
        in_specs=[SMEM] + [pl.BlockSpec(memory_space=pltpu.VMEM)] * len(values),
        out_specs=[pl.BlockSpec(memory_space=pl.ANY)] * len(shapes),
        out_shape=[shape_of(shape, F32) for shape in shapes],
        scratch_shapes=[pltpu.VMEM((TABLE_ROWS, 128), F32)]
        + [pltpu.VMEM(shape, F32) for shape in shapes]
        + [pltpu.SemaphoreType.DMA((len(shapes), 2))],
        compiler_params=pltpu.CompilerParams(vmem_limit_bytes=NEAR_LIMIT),
    )(is_upper, *values)


def solution(mesh):
    placed = (
        P(None, "lat", "lon", None),
        P(None, "lat", "lon", None),
        P(None, "lat", "lon"),
        P(None, "lat"),
        P(),
        P(),
        P(),
        P(),
        P(),
        P(None, "lat", None, None, None),
    )
    return jax.shard_map(
        per_device,
        mesh=mesh,
        in_specs=placed,
        out_specs=(
            P(None, "lat", "lon", None),
            P(None, "lat", "lon", None),
            P(),
            P(),
            P(),
            P(),
            P(),
            P(None, "lat", None, None, None),
        ),
        check_vma=False,
    )
```

```python
import functools
import math

import jax
import jax.numpy as jnp
from jax import lax
from jax.experimental import pallas as pl
from jax.experimental.pallas import tpu as pltpu
from jax.sharding import PartitionSpec as P

C = 192
HEADS = 6
HEAD = 32
FFN = 768
WIN_Z = 2
WIN_LAT = 6
WIN_LON = 12
WIN = 144
TOKENS = 2 * WIN
QUAD = 72
RELPOS = 3312
SPAN = 2 * WIN_LON - 1
ROWS = 3584
GAIN_ROWS = 3456
TABLE_ROWS = 320

EPSILON = 1e-05
NEGATIVE = -1000000000.0
SCALE = 1.0 / math.sqrt(HEAD)

F32 = jnp.float32
BF16 = jnp.bfloat16


def mm(left, right):
    return lax.dot_general(left, right, (((1,), (0,)), ((), ())), preferred_element_type=F32)


def mm_nt(left, right):
    return lax.dot_general(left, right, (((1,), (1,)), ((), ())), preferred_element_type=F32)


def eye(size):
    return (
        lax.broadcasted_iota(jnp.int32, (size, size), 0) == lax.broadcasted_iota(jnp.int32, (size, size), 1)
    ).astype(F32).astype(BF16)


def divided(value, divisor, count):
    quotient = jnp.zeros_like(value)
    for number in range(1, count):
        quotient = quotient + (value >= number * divisor).astype(jnp.int32)
    return quotient, value - quotient * divisor


def lanes_of_tokens():
    return lax.broadcasted_iota(jnp.int32, (1, TOKENS), 1)


def row_of_quad(roll):
    lat_half, rest = divided(lanes_of_tokens(), 2 * QUAD, 2)
    lon_half, rest = divided(rest, QUAD, 2)
    level, rest = divided(rest, 18, 4)
    row, col = divided(rest, 6, 3)
    level = (level + 4 - roll) & 3
    return (level * 6 + lat_half * 3 + row) * 12 + lon_half * 6 + col


def quad_of_row(roll):
    level, rest = divided(lanes_of_tokens(), QUAD, 4)
    row, col = divided(rest, 12, 6)
    lat_half, row = divided(row, 3, 2)
    lon_half, col = divided(col, 6, 2)
    level = (level + roll) & 3
    return lat_half * 2 * QUAD + lon_half * QUAD + level * 18 + row * 6 + col


def places(rows):
    return (lax.broadcasted_iota(jnp.int32, (TOKENS, TOKENS), 0) == rows).astype(F32).astype(BF16)


def turned(value):
    return mm_nt(eye(value.shape[1]), value).astype(BF16)


def norm_stats(values):
    centre = values - jnp.mean(values, axis=-1, keepdims=True)
    inverse = lax.rsqrt(jnp.mean(centre * centre, axis=-1, keepdims=True) + EPSILON)
    return centre * inverse, inverse


def norm_backward(upstream, normal_hat, inverse):
    upstream_mean = jnp.mean(upstream, axis=-1, keepdims=True)
    cross_mean = jnp.mean(upstream * normal_hat, axis=-1, keepdims=True)
    return inverse * (upstream - upstream_mean - normal_hat * cross_mean)


def head_lanes(head):
    lane = lax.broadcasted_iota(jnp.int32, (1, C), 1)
    return ((lane >= head * HEAD) & (lane < (head + 1) * HEAD)).astype(F32).astype(BF16)


def pair_keys():
    row = lax.broadcasted_iota(jnp.int32, (512, 1), 0)
    within = row & 127
    third = (within >= SPAN).astype(jnp.int32) + (within >= 2 * SPAN).astype(jnp.int32)
    row_group = (row >> 7) * 3 + third
    row_offset = within - third * SPAN
    col = lax.broadcasted_iota(jnp.int32, (1, 256), 1)
    col_group = jnp.zeros_like(col)
    for group in range(1, 12):
        col_group = col_group + (col >= group * 12).astype(jnp.int32)
    col_place = col - col_group * 12
    usable = (row_group == col_group) & (within < 3 * SPAN) & (col < WIN)
    return jnp.where(usable, col_place + 11 - row_offset, -1).astype(F32).astype(BF16)


def pairs_of(keys, place):
    return jnp.where(keys == jnp.asarray(place, BF16), jnp.asarray(1, BF16), jnp.asarray(0, BF16))


def table_start(zs, zt, hs, ht):
    return (((zs * 2 + zt) * 6 + hs) * 6 + ht) * SPAN


def spread_bias(table_ref, row_ref, shaped_ref, bias_ref):
    for head in range(HEADS):
        row_ref[head * 2 : head * 2 + 2, :RELPOS] = table_ref[head].astype(F32)
    row = row_ref[: 2 * HEADS]
    for zs in range(2):
        for zt in range(2):
            for group in range(2):
                for ht in range(6):
                    pieces = []
                    for hs in range(group * 3, group * 3 + 3):
                        start = table_start(zs, zt, hs, ht)
                        pieces.append(row[:, start : start + SPAN])
                    pieces.append(jnp.zeros((2 * HEADS, 128 - 3 * SPAN), F32))
                    target = pl.ds(zt * 6 + ht, 2 * HEADS, stride=12)
                    shaped_ref[zs * 2 + group, target, :] = jnp.concatenate(pieces, axis=1)
    keys = pair_keys()
    shaped = jnp.concatenate([shaped_ref[part, :WIN].astype(BF16) for part in range(4)], axis=1)
    for col in range(WIN_LON):
        spread = mm(shaped, pairs_of(keys, col))
        bias_ref[0, pl.ds(col, WIN, stride=12), :] = spread[:, :128]
        bias_ref[1, pl.ds(col, WIN, stride=12), :] = spread[:, 128:]


def collect_bias(scaled_ref, levels, row_ref, shaped_ref, grads_ref, out_ref):
    for place in range(2 * HEADS):
        rows = slice(place * WIN, (place + 1) * WIN)
        piece = scaled_ref[place].astype(F32)
        grads_ref[0, rows] = piece[:, :128]
        grads_ref[1, rows] = jnp.concatenate([piece[:, 128:], jnp.zeros((WIN, 256 - WIN), F32)], axis=1)
    keys = pair_keys()
    total = jnp.zeros((WIN, 512), F32)
    for col in range(WIN_LON):
        left = grads_ref[0, pl.ds(col, WIN, stride=12), :]
        right = grads_ref[1, pl.ds(col, WIN, stride=12), :]
        piece = jnp.concatenate([left, right], axis=1).astype(BF16)
        total = total + mm_nt(piece, pairs_of(keys, col))
    total = total * (1.0 / SCALE)
    for part in range(4):
        shaped_ref[part, :WIN] = total[:, part * 128 : (part + 1) * 128]
    row_ref[...] = jnp.zeros_like(row_ref)
    for zs in range(2):
        for zt in range(2):
            for group in range(2):
                for ht in range(6):
                    pieces = [
                        shaped_ref[zs * 2 + group, pl.ds(window * 72 + zt * 6 + ht, HEADS, stride=12), :]
                        for window in range(2)
                    ]
                    for level in range(2):
                        chosen = jnp.zeros((HEADS, 128), F32)
                        for window in range(2):
                            chosen = chosen + jnp.where(levels[window] == level, pieces[window], 0.0)
                        for index in range(3):
                            start = table_start(zs, zt, group * 3 + index, ht)
                            row_ref[level * 8 : level * 8 + HEADS, start : start + SPAN] = chosen[
                                :, index * SPAN : (index + 1) * SPAN
                            ]
    for slab in range(26):
        lanes = slice(slab * 128, (slab + 1) * 128)
        rows = jnp.concatenate([row_ref[:HEADS, lanes], row_ref[8 : 8 + HEADS, lanes]], axis=0)
        shaped_ref[slab // 13, slab % 13 * 12 : slab % 13 * 12 + 12] = rows
    out_ref[...] = jnp.concatenate(
        [shaped_ref[0, :156], shaped_ref[1, :156], jnp.zeros((TABLE_ROWS - 312, 128), F32)], axis=0
    ).astype(BF16)


def load_tiles(bias_ref, level, head):
    rows = pl.ds(pl.multiple_of((head * 2 + level) * WIN, 8), WIN)
    return jnp.concatenate([bias_ref[0, rows, :], bias_ref[1, rows, : WIN - 128]], axis=1)


def attention(normed, in_weight, bias_of, weights_ref):
    eye_c = eye(C)
    weight_q, weight_k, weight_v = in_weight[:, :C], in_weight[:, C : 2 * C], in_weight[:, 2 * C :]
    kept = []
    mixed = []
    for window in range(2):
        rows = normed[window * WIN : (window + 1) * WIN]
        keys = mm(rows, weight_k).astype(BF16)
        values = mm(rows, weight_v).astype(BF16)
        queries = mm(rows, weight_q).astype(BF16)
        queries_t = mm_nt(eye_c, queries).astype(BF16)
        keys_t = mm_nt(eye_c, keys).astype(BF16)
        values_t = mm_nt(eye_c, values).astype(BF16)
        parts = []
        for head in range(HEADS):
            own = keys * head_lanes(head)
            scores = mm(own, queries_t) * SCALE + bias_of(window, head)
            weights = jnp.exp(scores - jnp.max(scores, axis=0, keepdims=True))
            weights = weights * (1.0 / jnp.sum(weights, axis=0, keepdims=True))
            weights = weights.astype(BF16)
            weights_ref[window * HEADS + head] = weights
            parts.append(mm(values_t[head * HEAD : (head + 1) * HEAD], weights))
        mixed.append(jnp.concatenate(parts, axis=0).astype(BF16))
        kept.append((queries_t, keys_t, values))
    return kept, mixed


def feed_forward(hidden, gain, up_weight):
    hat, inverse = norm_stats(hidden)
    normed = (hat * gain).astype(BF16)
    return hat, inverse, normed, mm(normed, up_weight)


def gelu_parts(expanded):
    cumulative = 0.5 * (1.0 + lax.erf(expanded * (1.0 / math.sqrt(2.0))))
    slope = cumulative + expanded * jnp.exp(-0.5 * expanded * expanded) * (1.0 / math.sqrt(2.0 * math.pi))
    return (expanded * cumulative).astype(BF16), slope


def natural_mixed(mixed):
    eye_w = eye(WIN)
    return jnp.concatenate([mm_nt(eye_w, part) for part in mixed], axis=0).astype(BF16)


def pack(packed_ref, start, value):
    height = value.shape[0]
    for part in range(value.shape[1] // 128):
        rows = slice(start + part * height, start + (part + 1) * height)
        packed_ref[rows] = value[:, part * 128 : (part + 1) * 128].astype(BF16)


def backward(
    grad,
    active,
    slope,
    second_hat,
    second_inverse,
    second_norm,
    mixed,
    attended,
    weights_ref,
    first_hat,
    first_inverse,
    first_norm,
    gain_one,
    gain_two,
    in_weight,
    out_weight,
    up_weight,
    down_weight,
    scaled_ref,
    packed_ref,
):
    eye_c = eye(C)
    grad_half = grad.astype(BF16)
    pack(packed_ref, 2304, mm(turned(grad_half), active))
    grad_expanded = (mm(grad_half, down_weight) * slope).astype(BF16)
    normed_t = turned(second_norm)
    pack(packed_ref, 1152, mm(normed_t, grad_expanded))
    grad_second = mm_nt(grad_expanded, up_weight)
    gain_two_grad = jnp.sum(grad_second * second_hat, axis=0, keepdims=True)
    grad_hidden = (grad + norm_backward(grad_second * gain_two, second_hat, second_inverse)).astype(BF16)
    grad_out = mm(mixed[0], grad_hidden[:WIN]) + mm(mixed[1], grad_hidden[WIN:])
    packed_ref[960:1152] = grad_out[:, :128].astype(BF16)
    grad_mixed = mm_nt(grad_hidden, out_weight).astype(BF16)
    projected = []
    for window in range(2):
        queries_t, keys_t, values = attended[window]
        upstream_t = mm_nt(eye_c, grad_mixed[window * WIN : (window + 1) * WIN]).astype(BF16)
        grad_q, grad_k, grad_v = [], [], []
        for head in range(HEADS):
            lanes = slice(head * HEAD, (head + 1) * HEAD)
            half = weights_ref[window * HEADS + head]
            weights = half.astype(F32)
            own = values * head_lanes(head)
            grad_weights = mm(own, upstream_t)
            inner = jnp.sum(grad_weights * weights, axis=0, keepdims=True)
            grad_scores = weights * (grad_weights - inner)
            scaled = (grad_scores * SCALE).astype(BF16)
            scaled_ref[window * HEADS + head] = scaled
            grad_v.append(mm_nt(upstream_t[lanes], half))
            grad_q.append(mm(keys_t[lanes], scaled))
            grad_k.append(mm_nt(queries_t[lanes], scaled))
        projected_t = jnp.concatenate(grad_q + grad_k + grad_v, axis=0).astype(BF16)
        projected.append(mm_nt(eye(WIN), projected_t))
    projected = jnp.concatenate(projected, axis=0).astype(BF16)
    first_t = turned(first_norm)
    grad_in = mm(first_t, projected)
    pack(packed_ref, 0, grad_in[:, :512])
    packed_ref[768:960] = jnp.concatenate([grad_in[:, 512:], grad_out[:, 128:]], axis=1).astype(BF16)
    grad_first = mm_nt(projected, in_weight)
    gain_one_grad = jnp.sum(grad_first * first_hat, axis=0, keepdims=True)
    gain_rows = jnp.concatenate(
        [
            gain_one_grad[:, :128],
            jnp.concatenate([gain_one_grad[:, 128:], gain_two_grad[:, 128:]], axis=1),
            gain_two_grad[:, :128],
            jnp.zeros((ROWS - GAIN_ROWS - 3, 128), F32),
        ],
        axis=0,
    )
    packed_ref[GAIN_ROWS:ROWS] = gain_rows.astype(BF16)
    return (
        grad_hidden.astype(F32) + norm_backward(grad_first * gain_one, first_hat, first_inverse)
    ).astype(BF16)


def load_grid(grid_ref, rows_ref):
    for row in range(6):
        for col in range(12):
            piece = grid_ref[row, col].astype(F32)
            target = pl.ds(row * 12 + col, 4, stride=72)
            rows_ref[0, target, :] = piece[:, :128]
            rows_ref[1, target, :] = jnp.concatenate([piece[:, 128:], jnp.zeros((4, 64), F32)], axis=1)
    return jnp.concatenate([rows_ref[0], rows_ref[1][:, :64]], axis=1)


def store_grid(rows, rows_ref, grid_ref):
    rows_ref[0] = rows[:, :128]
    rows_ref[1] = jnp.concatenate([rows[:, 128:], jnp.zeros((TOKENS, 64), F32)], axis=1)
    for row in range(6):
        for col in range(12):
            source = pl.ds(row * 12 + col, 4, stride=72)
            piece = jnp.concatenate([rows_ref[0, source, :], rows_ref[1, source, :][:, :64]], axis=1)
            grid_ref[row, col] = piece.astype(BF16)


def block_weights(gains_ref, in_ref, out_ref, up_ref, down_ref):
    gains = gains_ref[...]
    return gains[0:1], gains[1:2], in_ref[...], out_ref[...], up_ref[...], down_ref[...]


def write_halves(upper_ref, packed_ref, keep_ref, send_ref):
    half = ROWS // 2
    is_upper = upper_ref[0] == 1

    @pl.when(is_upper)
    def _():
        keep_ref[...] = packed_ref[half:]
        send_ref[...] = packed_ref[:half]

    @pl.when(jnp.logical_not(is_upper))
    def _():
        keep_ref[...] = packed_ref[:half]
        send_ref[...] = packed_ref[half:]


def first_kernel(
    levels_ref,
    inputs_ref,
    grad_ref,
    gains_ref,
    in_ref,
    out_ref,
    up_ref,
    down_ref,
    table_ref,
    quad_0,
    quad_1,
    quad_2,
    quad_3,
    weights_out,
    turned_out,
    flat_out,
    rows_ref,
    row_ref,
    shaped_ref,
    bias_ref,
):
    levels = [levels_ref[0, 0], levels_ref[0, 1]]
    gain_one, gain_two, in_weight, out_weight, up_weight, down_weight = block_weights(
        gains_ref, in_ref, out_ref, up_ref, down_ref
    )
    order = places(quad_of_row(0))
    grad_quads = mm(order, load_grid(grad_ref, rows_ref).astype(BF16))
    flat = load_grid(inputs_ref, rows_ref)
    flat_out[0] = flat.astype(BF16)
    spread_bias(table_ref, row_ref, shaped_ref, bias_ref)
    hat, _ = norm_stats(flat)
    normed = (hat * gain_one).astype(BF16)
    attended, mixed = attention(
        normed, in_weight, lambda window, head: load_tiles(bias_ref, levels[window], head), weights_out
    )
    for window in range(2):
        turned_out[window, 0] = attended[window][0]
        turned_out[window, 1] = attended[window][1]
        turned_out[window, 2] = mixed[window]
        flat_out[2, window * WIN : (window + 1) * WIN] = attended[window][2]
    hidden = (flat + mm(natural_mixed(mixed), out_weight)).astype(BF16)
    flat_out[1] = hidden
    hidden = hidden.astype(F32)
    _, _, _, expanded = feed_forward(hidden, gain_two, up_weight)
    active = (expanded * 0.5 * (1.0 + lax.erf(expanded * (1.0 / math.sqrt(2.0))))).astype(BF16)
    result = (hidden + mm_nt(active, down_weight)).astype(BF16)
    result_quads = mm(order, result)
    for index, quad in enumerate((quad_0, quad_1, quad_2, quad_3)):
        rows = slice(index * QUAD, (index + 1) * QUAD)
        quad[...] = jnp.concatenate([result_quads[rows], grad_quads[rows]], axis=0).astype(BF16)


def region_row(region_ref, window):
    pieces = [region_ref[row, window * 2 + level : window * 2 + level + 1, :] for level in range(2) for row in range(6)]
    return jnp.concatenate(pieces, axis=1)


def prepare_kernel(
    levels_ref, region_ref, table_ref, bias_out, row_ref, shaped_ref, bias_ref
):
    levels = [levels_ref[0, 0], levels_ref[0, 1]]
    spread_bias(table_ref, row_ref, shaped_ref, bias_ref)
    diagonal = lax.broadcasted_iota(jnp.int32, (WIN, WIN), 0) == lax.broadcasted_iota(jnp.int32, (WIN, WIN), 1)
    for window in range(2):
        across = region_row(region_ref, window).astype(F32)
        down = jnp.sum(jnp.where(diagonal, across, 0.0), axis=1, keepdims=True)
        same = across == down
        for head in range(HEADS):
            bias = jnp.where(same, load_tiles(bias_ref, levels[window], head), NEGATIVE)
            bias_out[window * HEADS + head] = bias.astype(BF16)


def second_kernel(
    upper_ref,
    quad_0,
    quad_1,
    quad_2,
    quad_3,
    bias_ref,
    gains_ref,
    in_ref,
    out_ref,
    up_ref,
    down_ref,
    back_0,
    back_1,
    back_2,
    back_3,
    keep_ref,
    send_ref,
    scaled_ref,
    weights_ref,
    packed_ref,
):
    quads = [quad[...].astype(F32) for quad in (quad_0, quad_1, quad_2, quad_3)]
    ahead = places(row_of_quad(1))
    flat = mm(ahead, jnp.concatenate([quad[:QUAD] for quad in quads], axis=0).astype(BF16))
    grad = mm(ahead, jnp.concatenate([quad[QUAD:] for quad in quads], axis=0).astype(BF16))
    gain_one, gain_two, in_weight, out_weight, up_weight, down_weight = block_weights(
        gains_ref, in_ref, out_ref, up_ref, down_ref
    )
    first_hat, first_inverse = norm_stats(flat)
    first_norm = (first_hat * gain_one).astype(BF16)
    attended, mixed = attention(
        first_norm, in_weight, lambda window, head: bias_ref[window * HEADS + head].astype(F32), weights_ref
    )
    hidden = (flat + mm(natural_mixed(mixed), out_weight)).astype(BF16).astype(F32)
    second_hat, second_inverse, second_norm, expanded = feed_forward(hidden, gain_two, up_weight)
    active, slope = gelu_parts(expanded)
    result = (hidden + mm_nt(active, down_weight)).astype(BF16)
    grad_in = backward(
        grad, active, slope, second_hat, second_inverse, second_norm, mixed, attended, weights_ref,
        first_hat, first_inverse, first_norm, gain_one, gain_two, in_weight, out_weight, up_weight,
        down_weight, scaled_ref, packed_ref,
    )
    back = places(quad_of_row(1))
    result_quads, grad_quads = mm(back, result), mm(back, grad_in)
    for index, quad in enumerate((back_0, back_1, back_2, back_3)):
        rows = slice(index * QUAD, (index + 1) * QUAD)
        quad[...] = jnp.concatenate([result_quads[rows], grad_quads[rows]], axis=0).astype(BF16)
    write_halves(upper_ref, packed_ref, keep_ref, send_ref)


def collect_kernel(levels_ref, scaled_ref, tables_out, row_ref, shaped_ref, grads_ref):
    levels = [levels_ref[0, 0], levels_ref[0, 1]]
    collect_bias(scaled_ref, levels, row_ref, shaped_ref, grads_ref, tables_out)


def finish_kernel(
    levels_ref, scaled_ref, second_tables_ref, tables_out, row_ref, shaped_ref, grads_ref
):
    levels = [levels_ref[0, 0], levels_ref[0, 1]]
    collect_bias(scaled_ref, levels, row_ref, shaped_ref, grads_ref, tables_out.at[:TABLE_ROWS])
    tables_out[TABLE_ROWS:] = second_tables_ref[...]


def activation_kernel(flat_ref, gains_ref, up_ref, active_out, slope_out):
    _, _, _, expanded = feed_forward(flat_ref[1].astype(F32), gains_ref[1:2], up_ref[...])
    active, slope = gelu_parts(expanded)
    active_out[...] = active
    slope_out[...] = slope.astype(BF16)


def third_kernel(
    upper_ref,
    quad_0,
    quad_1,
    quad_2,
    quad_3,
    weights_ref,
    turned_ref,
    flat_ref,
    active_ref,
    slope_ref,
    gains_ref,
    in_ref,
    out_ref,
    up_ref,
    down_ref,
    keep_ref,
    send_ref,
    rows_out,
    scaled_ref,
    packed_ref,
):
    quads = [quad[...].astype(F32) for quad in (quad_0, quad_1, quad_2, quad_3)]
    grad = mm(places(row_of_quad(0)), jnp.concatenate([quad[QUAD:] for quad in quads], axis=0).astype(BF16))
    gain_one, gain_two, in_weight, out_weight, up_weight, down_weight = block_weights(
        gains_ref, in_ref, out_ref, up_ref, down_ref
    )
    first_hat, first_inverse = norm_stats(flat_ref[0].astype(F32))
    first_norm = (first_hat * gain_one).astype(BF16)
    second_hat, second_inverse = norm_stats(flat_ref[1].astype(F32))
    second_norm = (second_hat * gain_two).astype(BF16)
    attended = [
        (turned_ref[window, 0], turned_ref[window, 1], flat_ref[2, window * WIN : (window + 1) * WIN])
        for window in range(2)
    ]
    mixed = [turned_ref[0, 2], turned_ref[1, 2]]
    rows_out[...] = backward(
        grad, active_ref[...], slope_ref[...].astype(F32), second_hat, second_inverse, second_norm, mixed,
        attended, weights_ref, first_hat, first_inverse, first_norm, gain_one, gain_two, in_weight,
        out_weight, up_weight, down_weight, scaled_ref, packed_ref,
    )
    write_halves(upper_ref, packed_ref, keep_ref, send_ref)


def grids_kernel(quad_0, quad_1, quad_2, quad_3, grad_rows_ref, blocks_out, grad_out, rows_ref):
    quads = [quad[:QUAD].astype(F32) for quad in (quad_0, quad_1, quad_2, quad_3)]
    blocks = mm(places(row_of_quad(0)), jnp.concatenate(quads, axis=0).astype(BF16))
    store_grid(blocks, rows_ref, blocks_out)
    store_grid(grad_rows_ref[...].astype(F32), rows_ref, grad_out)


SMEM = pl.BlockSpec(memory_space=pltpu.SMEM)
VMEM = pl.BlockSpec(memory_space=pltpu.VMEM)
ANY = pl.BlockSpec(memory_space=pl.ANY)
FAR_LIMIT = 60 * 1024 * 1024
NEAR_LIMIT = 28 * 1024 * 1024


class Part:
    def __init__(self, array, block):
        self.array, self.block = array, block
        self.lead = sum(size == 1 for size in array.shape[1:]) + 1
        self.shape, self.dtype = array.shape[self.lead :], array.dtype

    def spec(self):
        return pl.BlockSpec(
            (None,) * self.lead + self.shape, lambda *_: (self.block,) + (0,) * (self.lead - 1 + len(self.shape))
        )

    def of(self, ref):
        return ref.at[(self.block,) + (0,) * (self.lead - 1)]


class Near:
    def __init__(self, array):
        self.array = array


def whole(array):
    return pl.BlockSpec(array.shape, lambda *_: (0,) * len(array.shape))


def call(kernel, scalars, operands, out_shapes, scratch, flops):
    specs = [operand.spec() if isinstance(operand, Part) else whole(operand) for operand in operands]
    arrays = [operand.array if isinstance(operand, Part) else operand for operand in operands]
    return pl.pallas_call(
        kernel,
        grid=(1,),
        in_specs=[SMEM] * len(scalars) + specs,
        out_specs=[whole(shape) for shape in out_shapes],
        out_shape=out_shapes,
        scratch_shapes=scratch,
        compiler_params=pltpu.CompilerParams(vmem_limit_bytes=FAR_LIMIT),
        cost_estimate=pl.CostEstimate(flops=flops, bytes_accessed=4_000_000, transcendentals=1_000_000),
    )(*scalars, *arrays)


def near_call(kernel, scalars, operands, out_shapes, scratch, flops, near_outs=(), carried=()):
    def is_near(operand):
        return isinstance(operand, Near)

    def plain_array(operand):
        return operand.array if isinstance(operand, (Near, Part)) else operand

    def source_of(operand, ref):
        return operand.of(ref) if isinstance(operand, Part) else ref

    far = [operand for operand in operands if not is_near(operand)]
    far_outs = [shape for place, shape in enumerate(out_shapes) if place not in near_outs]

    def body(*refs):
        refs = list(refs)

        def take(count):
            taken = refs[:count]
            del refs[:count]
            return taken

        scalar_refs, operand_refs, carried_refs = take(len(scalars)), take(len(operands)), take(len(carried))
        out_refs, carried_outs = take(len(out_shapes)), take(len(carried))
        scratch_refs, buffers, out_buffers = take(len(scratch)), take(len(far)), take(len(far_outs))
        sems, carried_sems, out_sems = refs
        inputs, arriving = [], []
        for operand, ref in zip(operands, operand_refs, strict=True):
            if is_near(operand):
                inputs.append(ref)
                continue
            place = len(arriving)
            arriving.append(pltpu.make_async_copy(source_of(operand, ref), buffers[place], sems.at[place]))
            inputs.append(buffers[place])
        for copy in arriving:
            copy.start()
        passing = [
            pltpu.make_async_copy(source_of(operand, ref), target, carried_sems.at[place])
            for place, (operand, ref, target) in enumerate(zip(carried, carried_refs, carried_outs, strict=True))
        ]
        for copy in passing:
            copy.start()
        for copy in arriving:
            copy.wait()
        outputs, leaving = [], []
        for place, ref in enumerate(out_refs):
            if place in near_outs:
                outputs.append(ref)
                continue
            outputs.append(out_buffers[len(leaving)])
            leaving.append(pltpu.make_async_copy(outputs[-1], ref, out_sems.at[len(leaving)]))
        kernel(*scalar_refs, *inputs, *outputs, *scratch_refs)
        for copy in leaving:
            copy.start()
        for copy in passing + leaving:
            copy.wait()

    return pl.pallas_call(
        body,
        in_specs=[SMEM] * len(scalars)
        + [VMEM if is_near(operand) else ANY for operand in operands]
        + [ANY] * len(carried),
        out_specs=[VMEM if place in near_outs else ANY for place in range(len(out_shapes))] + [VMEM] * len(carried),
        out_shape=[*out_shapes, *[shape_of(operand.shape, operand.dtype) for operand in carried]],
        scratch_shapes=[
            *scratch,
            *[pltpu.VMEM(operand.shape, operand.dtype) for operand in far],
            *[pltpu.VMEM(shape.shape, shape.dtype) for shape in far_outs],
            pltpu.SemaphoreType.DMA((max(len(far), 1),)),
            pltpu.SemaphoreType.DMA((max(len(carried), 1),)),
            pltpu.SemaphoreType.DMA((max(len(far_outs), 1),)),
        ],
        compiler_params=pltpu.CompilerParams(vmem_limit_bytes=NEAR_LIMIT),
        cost_estimate=pl.CostEstimate(flops=flops, bytes_accessed=4_000_000, transcendentals=1_000_000),
    )(*scalars, *[plain_array(operand) for operand in operands], *[plain_array(operand) for operand in carried])


def shape_of(shape, dtype):
    return jax.ShapeDtypeStruct(shape, dtype)


def shifted(value, lat_steps, lon_steps):
    lon_count, lat_count = lax.axis_size("lon"), lax.axis_size("lat")
    pairs = []
    for lon in range(lon_count):
        for lat in range(lat_count):
            source = ((lon + lon_steps) % lon_count) * lat_count + (lat + lat_steps) % lat_count
            pairs.append((source, lon * lat_count + lat))
    return lax.ppermute(value, ("lon", "lat"), pairs)


def per_device(
    inputs,
    grad_out,
    region,
    bias_level,
    norm_gains,
    in_weight,
    out_weight,
    up_weight,
    down_weight,
    bias_tables,
):
    weights = (norm_gains, in_weight, out_weight, up_weight, down_weight.transpose(0, 2, 1))
    first_weights = [Part(array, 0) for array in weights]
    second_weights = [Part(array, 1) for array in weights]
    inputs, grad_out = inputs.transpose(1, 2, 0, 3), grad_out.transpose(1, 2, 0, 3)
    bias_tables = bias_tables.transpose(0, 1, 3, 2, 4)
    bias_level = bias_level.T
    is_upper = odd(core_step()[1]).reshape(1)

    quad_shape = shape_of((2 * QUAD, C), BF16)
    grid_shape = shape_of((6, 12, 4, C), BF16)
    half_shape = shape_of((ROWS // 2, 128), BF16)
    table_shape = shape_of((TABLE_ROWS, 128), BF16)
    weights_shape = (2 * HEADS, WIN, WIN)
    grads_scratch = pltpu.VMEM((2, 2 * HEADS * WIN, 128), F32)
    row_scratch = pltpu.VMEM((16, 26 * 128), F32)
    shaped_scratch = pltpu.VMEM((4, 2 * 72 + 16, 128), F32)
    bias_scratch = pltpu.VMEM((2, 2 * HEADS * WIN, 128), F32)
    rows_scratch = pltpu.VMEM((2, TOKENS, 128), F32)
    packed_scratch = pltpu.VMEM((ROWS, 128), BF16)

    quads = call(
        first_kernel,
        (bias_level,),
        (inputs, grad_out, *first_weights, Part(bias_tables, 0)),
        [quad_shape] * 4
        + [
            shape_of(weights_shape, BF16),
            shape_of((2, 3, C, WIN), BF16),
            shape_of((3, TOKENS, C), BF16),
        ],
        [rows_scratch, row_scratch, shaped_scratch, bias_scratch],
        1_000_000_000,
    )
    stored = list(quads[4:])
    ahead = (
        quads[3],
        shifted(quads[2], 0, 1),
        shifted(quads[1], 1, 0),
        shifted(quads[0], 1, 1),
    )
    (bias,) = call(
        prepare_kernel,
        (bias_level,),
        (region.transpose(1, 0, 2), Part(bias_tables, 1)),
        [shape_of(weights_shape, BF16)],
        [row_scratch, shaped_scratch, bias_scratch],
        500_000_000,
    )
    *back, second_keep, second_send, second_scaled = call(
        second_kernel,
        (is_upper,),
        (*ahead, bias, *second_weights),
        [quad_shape] * 4 + [half_shape, half_shape, shape_of(weights_shape, BF16)],
        [pltpu.VMEM(weights_shape, BF16), packed_scratch],
        3_000_000_000,
    )
    home = [
        shifted(back[3], -1, -1),
        shifted(back[2], -1, 0),
        shifted(back[1], 0, -1),
        back[0],
    ]
    active, slope, *first_near = near_call(
        activation_kernel,
        (),
        (stored[2], first_weights[0], first_weights[3]),
        [shape_of((TOKENS, FFN), BF16), shape_of((TOKENS, FFN), BF16)],
        [],
        300_000_000,
        (0, 1),
        (home[3], *stored, *first_weights),
    )
    second_got = exchanged(second_send, core_step()[0])
    first_keep, first_send, grad_rows, first_scaled = near_call(
        third_kernel,
        (is_upper,),
        tuple(map(Near, (*home[:3], *first_near[:4], active, slope, *first_near[4:]))),
        [half_shape, half_shape, shape_of((TOKENS, C), BF16), shape_of(weights_shape, BF16)],
        [packed_scratch],
        2_000_000_000,
    )
    blocks_out, grad_inputs = near_call(
        grids_kernel,
        (),
        (*home, grad_rows),
        [grid_shape, grid_shape],
        [rows_scratch],
        100_000_000,
    )

    def collect(kernel, rows, *operands):
        return near_call(
            kernel,
            (bias_level,),
            operands,
            [shape_of((rows, 128), BF16)],
            [row_scratch, shaped_scratch, grads_scratch],
            500_000_000,
        )[0]

    first_got = exchanged(first_send, core_step()[0])
    second = added(second_keep, second_got)
    first = added(first_keep, first_got)
    first, second, first_scaled, second_scaled = tie((first, second, first_scaled, second_scaled))
    second_tables = collect(collect_kernel, TABLE_ROWS, second_scaled)
    tables = collect(finish_kernel, 2 * TABLE_ROWS, first_scaled, second_tables)
    totals = unpack(is_upper, *sum_all(first, second, tables, second_tables))
    gains, grad_in, grad_out_weight, grad_up, grad_down, grad_tables = totals
    return (
        blocks_out.transpose(2, 0, 1, 3),
        grad_inputs.transpose(2, 0, 1, 3),
        gains,
        grad_in,
        grad_out_weight,
        grad_up,
        grad_down.transpose(0, 2, 1),
        grad_tables.transpose(0, 1, 3, 2, 4),
    )


def exchanged(value, mask):
    lon_count, lat_count = lax.axis_size("lon"), lax.axis_size("lat")
    pairs = []
    for lon in range(lon_count):
        for lat in range(lat_count):
            pairs.append(((lon ^ mask[1]) * lat_count + (lat ^ mask[0]), lon * lat_count + lat))
    return lax.ppermute(value, ("lon", "lat"), pairs)


def added(left, right):
    return (left.astype(F32) + right.astype(F32)).astype(BF16)


def odd(mask):
    lat, lon = lax.axis_index("lat") & mask[0], lax.axis_index("lon") & mask[1]
    parity = jnp.int32(0)
    for place in range(5):
        parity = parity ^ (lat >> place) ^ (lon >> place)
    return parity & 1


def split(value, owner):
    half = value.shape[0] // 2
    up = odd(owner) != 0
    return jnp.where(up, value[half:], value[:half]), jnp.where(up, value[:half], value[half:])


def halve(value, mask, owner):
    keep, send = split(value, owner)
    return added(keep, exchanged(send, mask))


def double(value, mask, owner):
    other = exchanged(value, mask)
    up = odd(owner) != 0
    return jnp.concatenate([jnp.where(up, other, value), jnp.where(up, value, other)], axis=0)


def tie(values):
    return lax.optimization_barrier(values)


def core_step():
    return (1, 0), (1, 0)


def sum_all(first, second, tables, second_tables):
    core = core_step()[0]
    if lax.axis_size("lat") != 16 or lax.axis_size("lon") != 16:
        return sum_small(first, second, tables)
    y_low, y_high = ((2, 0), (2, 0)), (0, 8)
    x_low, x_high = ((4, 0), (12, 0)), ((12, 0), (8, 0))
    z_low, z_mid, z_high = ((0, 1), (0, 5)), ((0, 2), (0, 6)), (0, 7)

    first, second = halve(first, *y_low), halve(second, *x_low)
    first, second, second_tables = tie((first, second, second_tables))
    first, second = halve(first, *x_low), halve(second, *y_low)
    first, second = tie((first, second))
    rows = first.shape[0]
    joined = halve(jnp.concatenate([first, second], axis=0), *x_high)
    joined, tables = tie((joined, tables))
    for mask, owner in (z_low, z_mid):
        keep, send = split(tables, owner)
        got = exchanged(jnp.concatenate([joined, send], axis=0), mask)
        joined, tables = added(joined, got[:rows]), added(keep, got[rows:])
    joined = jnp.concatenate([joined, tables], axis=0)
    for mask in (z_high, y_high):
        joined = added(joined, exchanged(joined, mask))
    joined, tables = tie((joined[:rows], joined[rows:]))
    joined, tables = double(joined, *x_high), double(tables, *z_mid)
    first, second, tables = tie((joined[:rows], joined[rows:], tables))
    first, second, tables = double(first, *x_low), double(second, *y_low), double(tables, *z_low)
    first, second, tables = tie((first, second, tables))
    first, second = double(first, *y_low), double(second, *x_low)
    first, second = tie((first, second))
    return first, exchanged(first, core), second, exchanged(second, core), tables


def sum_small(first, second, tables):
    def over(value, axis):
        for place in range(lax.axis_size(axis).bit_length() - 1):
            if axis == "lon" or place:
                value = added(value, exchanged(value, (1 << place, 0) if axis == "lat" else (0, 1 << place)))
        return value

    core = core_step()[0]
    first, second = over(over(first, "lat"), "lon"), over(over(second, "lat"), "lon")
    return first, exchanged(first, core), second, exchanged(second, core), over(tables, "lon")


def unpack_kernel(upper_ref, first_own, first_other, second_own, second_other, tables_ref, *refs):
    results, (rows_ref, *buffers, sems) = refs[:6], refs[6:]
    gains_ref, in_ref, out_ref, up_ref, down_ref, grads_ref = buffers
    half = ROWS // 2
    is_upper = jnp.broadcast_to(upper_ref[0] == 1, (1, 128))
    copies = []

    def leave(index, block):
        copy = pltpu.make_async_copy(buffers[index].at[block], results[index].at[block], sems.at[index, block])
        copy.start()
        copies.append(copy)

    for block, (own, other) in enumerate(((first_own, first_other), (second_own, second_other))):

        def rows(start, stop, own=own, other=other):
            if start < half < stop:
                return jnp.concatenate([rows(start, half), rows(half, stop)], axis=0)
            lower = start < half
            start, stop = (start, stop) if lower else (start - half, stop - half)
            mine, theirs = own[start:stop].astype(F32), other[start:stop].astype(F32)
            return jnp.where(is_upper, theirs, mine) if lower else jnp.where(is_upper, mine, theirs)

        for index, (ref, start) in enumerate(((up_ref, 1152), (down_ref, 2304))):
            for part in range(6):
                lanes = slice(part * 128, (part + 1) * 128)
                ref[block, :, lanes] = rows(start + part * C, start + (part + 1) * C)
            leave(3 + index, block)
        for part in range(4):
            in_ref[block, :, part * 128 : (part + 1) * 128] = rows(part * C, (part + 1) * C)
        shared = rows(768, 960)
        in_ref[block, :, 512:] = shared[:, :64]
        leave(1, block)
        out_ref[block, :, :128] = rows(960, 1152)
        out_ref[block, :, 128:] = shared[:, 64:]
        leave(2, block)
        rows_ref[...] = tables_ref[block * TABLE_ROWS : (block + 1) * TABLE_ROWS].astype(F32)
        for slab in range(26):
            width = min(128, RELPOS - slab * 128)
            for level in range(2):
                start = slab * 12 + level * HEADS
                grads_ref[block, 0, :, level, slab * 128 : slab * 128 + width] = rows_ref[start : start + HEADS, :width]
        leave(5, block)
        gains = rows(GAIN_ROWS, GAIN_ROWS + 16)
        gains_ref[block, 0:1, :128] = gains[0:1]
        gains_ref[block, 0:1, 128:] = gains[1:2, :64]
        gains_ref[block, 1:2, :128] = gains[2:3]
        gains_ref[block, 1:2, 128:] = gains[1:2, 64:]
        leave(0, block)
    for copy in copies:
        copy.wait()


def unpack(is_upper, *values):
    shapes = [
        (2, 2, C),
        (2, C, 3 * C),
        (2, C, C),
        (2, C, FFN),
        (2, C, FFN),
        (2, 1, HEADS, 2, RELPOS),
    ]
    return pl.pallas_call(
        unpack_kernel,
        in_specs=[SMEM] + [pl.BlockSpec(memory_space=pltpu.VMEM)] * len(values),
        out_specs=[pl.BlockSpec(memory_space=pl.ANY)] * len(shapes),
        out_shape=[shape_of(shape, F32) for shape in shapes],
        scratch_shapes=[pltpu.VMEM((TABLE_ROWS, 128), F32)]
        + [pltpu.VMEM(shape, F32) for shape in shapes]
        + [pltpu.SemaphoreType.DMA((len(shapes), 2))],
        compiler_params=pltpu.CompilerParams(vmem_limit_bytes=NEAR_LIMIT),
    )(is_upper, *values)


def solution(mesh):
    placed = (
        P(None, "lat", "lon", None),
        P(None, "lat", "lon", None),
        P(None, "lat", "lon"),
        P(None, "lat"),
        P(),
        P(),
        P(),
        P(),
        P(),
        P(None, "lat", None, None, None),
    )
    return jax.shard_map(
        per_device,
        mesh=mesh,
        in_specs=placed,
        out_specs=(
            P(None, "lat", "lon", None),
            P(None, "lat", "lon", None),
            P(),
            P(),
            P(),
            P(),
            P(),
            P(None, "lat", None, None, None),
        ),
        check_vma=False,
    )
```

```python
import functools
import math

import jax
import jax.numpy as jnp
from jax import lax
from jax.experimental import pallas as pl
from jax.experimental.pallas import tpu as pltpu
from jax.sharding import PartitionSpec as P

C = 192
HEADS = 6
HEAD = 32
FFN = 768
WIN_Z = 2
WIN_LAT = 6
WIN_LON = 12
WIN = 144
TOKENS = 2 * WIN
QUAD = 72
RELPOS = 3312
SPAN = 2 * WIN_LON - 1
ROWS = 3584
GAIN_ROWS = 3456
TABLE_ROWS = 320

EPSILON = 1e-05
NEGATIVE = -1000000000.0
SCALE = 1.0 / math.sqrt(HEAD)

F32 = jnp.float32
BF16 = jnp.bfloat16


def mm(left, right):
    return lax.dot_general(left, right, (((1,), (0,)), ((), ())), preferred_element_type=F32)


def mm_nt(left, right):
    return lax.dot_general(left, right, (((1,), (1,)), ((), ())), preferred_element_type=F32)


def eye(size):
    return (
        lax.broadcasted_iota(jnp.int32, (size, size), 0) == lax.broadcasted_iota(jnp.int32, (size, size), 1)
    ).astype(F32).astype(BF16)


def divided(value, divisor, count):
    quotient = jnp.zeros_like(value)
    for number in range(1, count):
        quotient = quotient + (value >= number * divisor).astype(jnp.int32)
    return quotient, value - quotient * divisor


def lanes_of_tokens():
    return lax.broadcasted_iota(jnp.int32, (1, TOKENS), 1)


def row_of_quad(roll):
    lat_half, rest = divided(lanes_of_tokens(), 2 * QUAD, 2)
    lon_half, rest = divided(rest, QUAD, 2)
    level, rest = divided(rest, 18, 4)
    row, col = divided(rest, 6, 3)
    level = (level + 4 - roll) & 3
    return (level * 6 + lat_half * 3 + row) * 12 + lon_half * 6 + col


def quad_of_row(roll):
    level, rest = divided(lanes_of_tokens(), QUAD, 4)
    row, col = divided(rest, 12, 6)
    lat_half, row = divided(row, 3, 2)
    lon_half, col = divided(col, 6, 2)
    level = (level + roll) & 3
    return lat_half * 2 * QUAD + lon_half * QUAD + level * 18 + row * 6 + col


def places(rows):
    return (lax.broadcasted_iota(jnp.int32, (TOKENS, TOKENS), 0) == rows).astype(F32).astype(BF16)


def turned(value):
    return mm_nt(eye(value.shape[1]), value).astype(BF16)


def norm_stats(values):
    centre = values - jnp.mean(values, axis=-1, keepdims=True)
    inverse = lax.rsqrt(jnp.mean(centre * centre, axis=-1, keepdims=True) + EPSILON)
    return centre * inverse, inverse


def norm_backward(upstream, normal_hat, inverse):
    upstream_mean = jnp.mean(upstream, axis=-1, keepdims=True)
    cross_mean = jnp.mean(upstream * normal_hat, axis=-1, keepdims=True)
    return inverse * (upstream - upstream_mean - normal_hat * cross_mean)


def head_lanes(head):
    lane = lax.broadcasted_iota(jnp.int32, (1, C), 1)
    return ((lane >= head * HEAD) & (lane < (head + 1) * HEAD)).astype(F32).astype(BF16)


def pair_keys():
    row = lax.broadcasted_iota(jnp.int32, (512, 1), 0)
    within = row & 127
    third = (within >= SPAN).astype(jnp.int32) + (within >= 2 * SPAN).astype(jnp.int32)
    row_group = (row >> 7) * 3 + third
    row_offset = within - third * SPAN
    col = lax.broadcasted_iota(jnp.int32, (1, 256), 1)
    col_group = jnp.zeros_like(col)
    for group in range(1, 12):
        col_group = col_group + (col >= group * 12).astype(jnp.int32)
    col_place = col - col_group * 12
    usable = (row_group == col_group) & (within < 3 * SPAN) & (col < WIN)
    return jnp.where(usable, col_place + 11 - row_offset, -1).astype(F32).astype(BF16)


def pairs_of(keys, place):
    return jnp.where(keys == jnp.asarray(place, BF16), jnp.asarray(1, BF16), jnp.asarray(0, BF16))


def table_start(zs, zt, hs, ht):
    return (((zs * 2 + zt) * 6 + hs) * 6 + ht) * SPAN


def spread_bias(table_ref, row_ref, shaped_ref, bias_ref):
    for head in range(HEADS):
        row_ref[head * 2 : head * 2 + 2, :RELPOS] = table_ref[head].astype(F32)
    row = row_ref[: 2 * HEADS]
    for zs in range(2):
        for zt in range(2):
            for group in range(2):
                for ht in range(6):
                    pieces = []
                    for hs in range(group * 3, group * 3 + 3):
                        start = table_start(zs, zt, hs, ht)
                        pieces.append(row[:, start : start + SPAN])
                    pieces.append(jnp.zeros((2 * HEADS, 128 - 3 * SPAN), F32))
                    target = pl.ds(zt * 6 + ht, 2 * HEADS, stride=12)
                    shaped_ref[zs * 2 + group, target, :] = jnp.concatenate(pieces, axis=1)
    keys = pair_keys()
    shaped = jnp.concatenate([shaped_ref[part, :WIN].astype(BF16) for part in range(4)], axis=1)
    for col in range(WIN_LON):
        spread = mm(shaped, pairs_of(keys, col))
        bias_ref[0, pl.ds(col, WIN, stride=12), :] = spread[:, :128]
        bias_ref[1, pl.ds(col, WIN, stride=12), :] = spread[:, 128:]


def collect_bias(scaled_ref, levels, row_ref, shaped_ref, grads_ref, out_ref):
    for place in range(2 * HEADS):
        rows = slice(place * WIN, (place + 1) * WIN)
        piece = scaled_ref[place].astype(F32)
        grads_ref[0, rows] = piece[:, :128]
        grads_ref[1, rows] = jnp.concatenate([piece[:, 128:], jnp.zeros((WIN, 256 - WIN), F32)], axis=1)
    keys = pair_keys()
    total = jnp.zeros((WIN, 512), F32)
    for col in range(WIN_LON):
        left = grads_ref[0, pl.ds(col, WIN, stride=12), :]
        right = grads_ref[1, pl.ds(col, WIN, stride=12), :]
        piece = jnp.concatenate([left, right], axis=1).astype(BF16)
        total = total + mm_nt(piece, pairs_of(keys, col))
    total = total * (1.0 / SCALE)
    for part in range(4):
        shaped_ref[part, :WIN] = total[:, part * 128 : (part + 1) * 128]
    row_ref[...] = jnp.zeros_like(row_ref)
    for zs in range(2):
        for zt in range(2):
            for group in range(2):
                for ht in range(6):
                    pieces = [
                        shaped_ref[zs * 2 + group, pl.ds(window * 72 + zt * 6 + ht, HEADS, stride=12), :]
                        for window in range(2)
                    ]
                    for level in range(2):
                        chosen = jnp.zeros((HEADS, 128), F32)
                        for window in range(2):
                            chosen = chosen + jnp.where(levels[window] == level, pieces[window], 0.0)
                        for index in range(3):
                            start = table_start(zs, zt, group * 3 + index, ht)
                            row_ref[level * 8 : level * 8 + HEADS, start : start + SPAN] = chosen[
                                :, index * SPAN : (index + 1) * SPAN
                            ]
    for slab in range(26):
        lanes = slice(slab * 128, (slab + 1) * 128)
        rows = jnp.concatenate([row_ref[:HEADS, lanes], row_ref[8 : 8 + HEADS, lanes]], axis=0)
        shaped_ref[slab // 13, slab % 13 * 12 : slab % 13 * 12 + 12] = rows
    out_ref[...] = jnp.concatenate(
        [shaped_ref[0, :156], shaped_ref[1, :156], jnp.zeros((TABLE_ROWS - 312, 128), F32)], axis=0
    ).astype(BF16)


def load_tiles(bias_ref, level, head):
    rows = pl.ds(pl.multiple_of((head * 2 + level) * WIN, 8), WIN)
    return jnp.concatenate([bias_ref[0, rows, :], bias_ref[1, rows, : WIN - 128]], axis=1)


def attention(normed, in_weight, bias_of, weights_ref):
    eye_c = eye(C)
    weight_q, weight_k, weight_v = in_weight[:, :C], in_weight[:, C : 2 * C], in_weight[:, 2 * C :]
    kept = []
    mixed = []
    for window in range(2):
        rows = normed[window * WIN : (window + 1) * WIN]
        keys = mm(rows, weight_k).astype(BF16)
        values = mm(rows, weight_v).astype(BF16)
        queries = mm(rows, weight_q).astype(BF16)
        queries_t = mm_nt(eye_c, queries).astype(BF16)
        keys_t = mm_nt(eye_c, keys).astype(BF16)
        values_t = mm_nt(eye_c, values).astype(BF16)
        parts = []
        for head in range(HEADS):
            own = keys * head_lanes(head)
            scores = mm(own, queries_t) * SCALE + bias_of(window, head)
            weights = jnp.exp(scores - jnp.max(scores, axis=0, keepdims=True))
            weights = weights * (1.0 / jnp.sum(weights, axis=0, keepdims=True))
            weights = weights.astype(BF16)
            weights_ref[window * HEADS + head] = weights
            parts.append(mm(values_t[head * HEAD : (head + 1) * HEAD], weights))
        mixed.append(jnp.concatenate(parts, axis=0).astype(BF16))
        kept.append((queries_t, keys_t, values))
    return kept, mixed


def feed_forward(hidden, gain, up_weight):
    hat, inverse = norm_stats(hidden)
    normed = (hat * gain).astype(BF16)
    return hat, inverse, normed, mm(normed, up_weight)


def gelu_parts(expanded):
    cumulative = 0.5 * (1.0 + lax.erf(expanded * (1.0 / math.sqrt(2.0))))
    slope = cumulative + expanded * jnp.exp(-0.5 * expanded * expanded) * (1.0 / math.sqrt(2.0 * math.pi))
    return (expanded * cumulative).astype(BF16), slope


def natural_mixed(mixed):
    eye_w = eye(WIN)
    return jnp.concatenate([mm_nt(eye_w, part) for part in mixed], axis=0).astype(BF16)


def pack(packed_ref, start, value):
    height = value.shape[0]
    for part in range(value.shape[1] // 128):
        rows = slice(start + part * height, start + (part + 1) * height)
        packed_ref[rows] = value[:, part * 128 : (part + 1) * 128].astype(BF16)


def backward(
    grad,
    active,
    slope,
    second_hat,
    second_inverse,
    second_norm,
    mixed,
    attended,
    weights_ref,
    first_hat,
    first_inverse,
    first_norm,
    gain_one,
    gain_two,
    in_weight,
    out_weight,
    up_weight,
    down_weight,
    scaled_ref,
    packed_ref,
):
    eye_c = eye(C)
    grad_half = grad.astype(BF16)
    pack(packed_ref, 2304, mm(turned(grad_half), active))
    grad_expanded = (mm(grad_half, down_weight) * slope).astype(BF16)
    normed_t = turned(second_norm)
    pack(packed_ref, 1152, mm(normed_t, grad_expanded))
    grad_second = mm_nt(grad_expanded, up_weight)
    gain_two_grad = jnp.sum(grad_second * second_hat, axis=0, keepdims=True)
    grad_hidden = (grad + norm_backward(grad_second * gain_two, second_hat, second_inverse)).astype(BF16)
    grad_out = mm(mixed[0], grad_hidden[:WIN]) + mm(mixed[1], grad_hidden[WIN:])
    packed_ref[960:1152] = grad_out[:, :128].astype(BF16)
    grad_mixed = mm_nt(grad_hidden, out_weight).astype(BF16)
    projected = []
    for window in range(2):
        queries_t, keys_t, values = attended[window]
        upstream_t = mm_nt(eye_c, grad_mixed[window * WIN : (window + 1) * WIN]).astype(BF16)
        grad_q, grad_k, grad_v = [], [], []
        for head in range(HEADS):
            lanes = slice(head * HEAD, (head + 1) * HEAD)
            half = weights_ref[window * HEADS + head]
            weights = half.astype(F32)
            own = values * head_lanes(head)
            grad_weights = mm(own, upstream_t)
            inner = jnp.sum(grad_weights * weights, axis=0, keepdims=True)
            grad_scores = weights * (grad_weights - inner)
            scaled = (grad_scores * SCALE).astype(BF16)
            scaled_ref[window * HEADS + head] = scaled
            grad_v.append(mm_nt(upstream_t[lanes], half))
            grad_q.append(mm(keys_t[lanes], scaled))
            grad_k.append(mm_nt(queries_t[lanes], scaled))
        projected_t = jnp.concatenate(grad_q + grad_k + grad_v, axis=0).astype(BF16)
        projected.append(mm_nt(eye(WIN), projected_t))
    projected = jnp.concatenate(projected, axis=0).astype(BF16)
    first_t = turned(first_norm)
    grad_in = mm(first_t, projected)
    pack(packed_ref, 0, grad_in[:, :512])
    packed_ref[768:960] = jnp.concatenate([grad_in[:, 512:], grad_out[:, 128:]], axis=1).astype(BF16)
    grad_first = mm_nt(projected, in_weight)
    gain_one_grad = jnp.sum(grad_first * first_hat, axis=0, keepdims=True)
    gain_rows = jnp.concatenate(
        [
            gain_one_grad[:, :128],
            jnp.concatenate([gain_one_grad[:, 128:], gain_two_grad[:, 128:]], axis=1),
            gain_two_grad[:, :128],
            jnp.zeros((ROWS - GAIN_ROWS - 3, 128), F32),
        ],
        axis=0,
    )
    packed_ref[GAIN_ROWS:ROWS] = gain_rows.astype(BF16)
    return (
        grad_hidden.astype(F32) + norm_backward(grad_first * gain_one, first_hat, first_inverse)
    ).astype(BF16)


def load_grid(grid_ref, rows_ref):
    for row in range(6):
        for col in range(12):
            piece = grid_ref[row, col].astype(F32)
            target = pl.ds(row * 12 + col, 4, stride=72)
            rows_ref[0, target, :] = piece[:, :128]
            rows_ref[1, target, :] = jnp.concatenate([piece[:, 128:], jnp.zeros((4, 64), F32)], axis=1)
    return jnp.concatenate([rows_ref[0], rows_ref[1][:, :64]], axis=1)


def store_grid(rows, rows_ref, grid_ref):
    rows_ref[0] = rows[:, :128]
    rows_ref[1] = jnp.concatenate([rows[:, 128:], jnp.zeros((TOKENS, 64), F32)], axis=1)
    for row in range(6):
        for col in range(12):
            source = pl.ds(row * 12 + col, 4, stride=72)
            piece = jnp.concatenate([rows_ref[0, source, :], rows_ref[1, source, :][:, :64]], axis=1)
            grid_ref[row, col] = piece.astype(BF16)


def block_weights(gains_ref, in_ref, out_ref, up_ref, down_ref):
    gains = gains_ref[...]
    return gains[0:1], gains[1:2], in_ref[...], out_ref[...], up_ref[...], down_ref[...]


def write_halves(upper_ref, packed_ref, keep_ref, send_ref):
    half = ROWS // 2
    is_upper = upper_ref[0] == 1

    @pl.when(is_upper)
    def _():
        keep_ref[...] = packed_ref[half:]
        send_ref[...] = packed_ref[:half]

    @pl.when(jnp.logical_not(is_upper))
    def _():
        keep_ref[...] = packed_ref[:half]
        send_ref[...] = packed_ref[half:]


def first_kernel(
    levels_ref,
    inputs_ref,
    grad_ref,
    gains_ref,
    in_ref,
    out_ref,
    up_ref,
    down_ref,
    table_ref,
    quad_0,
    quad_1,
    quad_2,
    quad_3,
    weights_out,
    turned_out,
    flat_out,
    rows_ref,
    row_ref,
    shaped_ref,
    bias_ref,
):
    levels = [levels_ref[0, 0], levels_ref[0, 1]]
    gain_one, gain_two, in_weight, out_weight, up_weight, down_weight = block_weights(
        gains_ref, in_ref, out_ref, up_ref, down_ref
    )
    order = places(quad_of_row(0))
    grad_quads = mm(order, load_grid(grad_ref, rows_ref).astype(BF16))
    flat = load_grid(inputs_ref, rows_ref)
    flat_out[0] = flat.astype(BF16)
    spread_bias(table_ref, row_ref, shaped_ref, bias_ref)
    hat, _ = norm_stats(flat)
    normed = (hat * gain_one).astype(BF16)
    attended, mixed = attention(
        normed, in_weight, lambda window, head: load_tiles(bias_ref, levels[window], head), weights_out
    )
    for window in range(2):
        turned_out[window, 0] = attended[window][0]
        turned_out[window, 1] = attended[window][1]
        turned_out[window, 2] = mixed[window]
        flat_out[2, window * WIN : (window + 1) * WIN] = attended[window][2]
    hidden = (flat + mm(natural_mixed(mixed), out_weight)).astype(BF16)
    flat_out[1] = hidden
    hidden = hidden.astype(F32)
    _, _, _, expanded = feed_forward(hidden, gain_two, up_weight)
    active = (expanded * 0.5 * (1.0 + lax.erf(expanded * (1.0 / math.sqrt(2.0))))).astype(BF16)
    result = (hidden + mm_nt(active, down_weight)).astype(BF16)
    result_quads = mm(order, result)
    for index, quad in enumerate((quad_0, quad_1, quad_2, quad_3)):
        rows = slice(index * QUAD, (index + 1) * QUAD)
        quad[...] = jnp.concatenate([result_quads[rows], grad_quads[rows]], axis=0).astype(BF16)


def region_row(region_ref, window):
    pieces = [region_ref[row, window * 2 + level : window * 2 + level + 1, :] for level in range(2) for row in range(6)]
    return jnp.concatenate(pieces, axis=1)


def prepare_kernel(
    levels_ref, region_ref, table_ref, bias_out, row_ref, shaped_ref, bias_ref
):
    levels = [levels_ref[0, 0], levels_ref[0, 1]]
    spread_bias(table_ref, row_ref, shaped_ref, bias_ref)
    diagonal = lax.broadcasted_iota(jnp.int32, (WIN, WIN), 0) == lax.broadcasted_iota(jnp.int32, (WIN, WIN), 1)
    for window in range(2):
        across = region_row(region_ref, window).astype(F32)
        down = jnp.sum(jnp.where(diagonal, across, 0.0), axis=1, keepdims=True)
        same = across == down
        for head in range(HEADS):
            bias = jnp.where(same, load_tiles(bias_ref, levels[window], head), NEGATIVE)
            bias_out[window * HEADS + head] = bias.astype(BF16)


def second_kernel(
    upper_ref,
    quad_0,
    quad_1,
    quad_2,
    quad_3,
    bias_ref,
    gains_ref,
    in_ref,
    out_ref,
    up_ref,
    down_ref,
    back_0,
    back_1,
    back_2,
    back_3,
    keep_ref,
    send_ref,
    scaled_ref,
    weights_ref,
    packed_ref,
):
    quads = [quad[...].astype(F32) for quad in (quad_0, quad_1, quad_2, quad_3)]
    ahead = places(row_of_quad(1))
    flat = mm(ahead, jnp.concatenate([quad[:QUAD] for quad in quads], axis=0).astype(BF16))
    grad = mm(ahead, jnp.concatenate([quad[QUAD:] for quad in quads], axis=0).astype(BF16))
    gain_one, gain_two, in_weight, out_weight, up_weight, down_weight = block_weights(
        gains_ref, in_ref, out_ref, up_ref, down_ref
    )
    first_hat, first_inverse = norm_stats(flat)
    first_norm = (first_hat * gain_one).astype(BF16)
    attended, mixed = attention(
        first_norm, in_weight, lambda window, head: bias_ref[window * HEADS + head].astype(F32), weights_ref
    )
    hidden = (flat + mm(natural_mixed(mixed), out_weight)).astype(BF16).astype(F32)
    second_hat, second_inverse, second_norm, expanded = feed_forward(hidden, gain_two, up_weight)
    active, slope = gelu_parts(expanded)
    result = (hidden + mm_nt(active, down_weight)).astype(BF16)
    grad_in = backward(
        grad, active, slope, second_hat, second_inverse, second_norm, mixed, attended, weights_ref,
        first_hat, first_inverse, first_norm, gain_one, gain_two, in_weight, out_weight, up_weight,
        down_weight, scaled_ref, packed_ref,
    )
    back = places(quad_of_row(1))
    result_quads, grad_quads = mm(back, result), mm(back, grad_in)
    for index, quad in enumerate((back_0, back_1, back_2, back_3)):
        rows = slice(index * QUAD, (index + 1) * QUAD)
        quad[...] = jnp.concatenate([result_quads[rows], grad_quads[rows]], axis=0).astype(BF16)
    write_halves(upper_ref, packed_ref, keep_ref, send_ref)


def collect_kernel(levels_ref, scaled_ref, tables_out, row_ref, shaped_ref, grads_ref):
    levels = [levels_ref[0, 0], levels_ref[0, 1]]
    collect_bias(scaled_ref, levels, row_ref, shaped_ref, grads_ref, tables_out)


def finish_kernel(
    levels_ref, scaled_ref, second_tables_ref, tables_out, row_ref, shaped_ref, grads_ref
):
    levels = [levels_ref[0, 0], levels_ref[0, 1]]
    collect_bias(scaled_ref, levels, row_ref, shaped_ref, grads_ref, tables_out.at[:TABLE_ROWS])
    tables_out[TABLE_ROWS:] = second_tables_ref[...]


def activation_kernel(_, flat_ref, gains_ref, up_ref, active_out, slope_out):
    _, _, _, expanded = feed_forward(flat_ref[1].astype(F32), gains_ref[1:2], up_ref[...])
    active, slope = gelu_parts(expanded)
    active_out[...] = active
    slope_out[...] = slope.astype(BF16)


def third_kernel(
    upper_ref,
    quad_0,
    quad_1,
    quad_2,
    quad_3,
    weights_ref,
    turned_ref,
    flat_ref,
    active_ref,
    slope_ref,
    gains_ref,
    in_ref,
    out_ref,
    up_ref,
    down_ref,
    keep_ref,
    send_ref,
    rows_out,
    scaled_ref,
    packed_ref,
):
    quads = [quad[...].astype(F32) for quad in (quad_0, quad_1, quad_2, quad_3)]
    grad = mm(places(row_of_quad(0)), jnp.concatenate([quad[QUAD:] for quad in quads], axis=0).astype(BF16))
    gain_one, gain_two, in_weight, out_weight, up_weight, down_weight = block_weights(
        gains_ref, in_ref.at[0], out_ref, up_ref, down_ref
    )
    first_hat, first_inverse = norm_stats(flat_ref[0].astype(F32))
    first_norm = (first_hat * gain_one).astype(BF16)
    second_hat, second_inverse = norm_stats(flat_ref[1].astype(F32))
    second_norm = (second_hat * gain_two).astype(BF16)
    attended = [
        (turned_ref[window, 0], turned_ref[window, 1], flat_ref[2, window * WIN : (window + 1) * WIN])
        for window in range(2)
    ]
    mixed = [turned_ref[0, 2], turned_ref[1, 2]]
    rows_out[...] = backward(
        grad, active_ref[...], slope_ref[...].astype(F32), second_hat, second_inverse, second_norm, mixed,
        attended, weights_ref, first_hat, first_inverse, first_norm, gain_one, gain_two, in_weight,
        out_weight, up_weight, down_weight, scaled_ref, packed_ref,
    )
    write_halves(upper_ref, packed_ref, keep_ref, send_ref)


def grids_kernel(quad_0, quad_1, quad_2, quad_3, grad_rows_ref, blocks_out, grad_out, rows_ref):
    quads = [quad[:QUAD].astype(F32) for quad in (quad_0, quad_1, quad_2, quad_3)]
    blocks = mm(places(row_of_quad(0)), jnp.concatenate(quads, axis=0).astype(BF16))
    store_grid(blocks, rows_ref, blocks_out)
    store_grid(grad_rows_ref[...].astype(F32), rows_ref, grad_out)


SMEM = pl.BlockSpec(memory_space=pltpu.SMEM)
VMEM = pl.BlockSpec(memory_space=pltpu.VMEM)
ANY = pl.BlockSpec(memory_space=pl.ANY)
FAR_LIMIT = 60 * 1024 * 1024
NEAR_LIMIT = 28 * 1024 * 1024


class Part:
    def __init__(self, array, block):
        self.array, self.block = array, block
        self.lead = sum(size == 1 for size in array.shape[1:]) + 1
        self.shape, self.dtype = array.shape[self.lead :], array.dtype

    def spec(self):
        return pl.BlockSpec(
            (None,) * self.lead + self.shape, lambda *_: (self.block,) + (0,) * (self.lead - 1 + len(self.shape))
        )

    def of(self, ref):
        return ref.at[(self.block,) + (0,) * (self.lead - 1)]


class Near:
    def __init__(self, array):
        self.array = array


def whole(array):
    return pl.BlockSpec(array.shape, lambda *_: (0,) * len(array.shape))


def call(kernel, scalars, operands, out_shapes, scratch, flops):
    specs = [operand.spec() if isinstance(operand, Part) else whole(operand) for operand in operands]
    arrays = [operand.array if isinstance(operand, Part) else operand for operand in operands]
    return pl.pallas_call(
        kernel,
        grid=(1,),
        in_specs=[SMEM] * len(scalars) + specs,
        out_specs=[whole(shape) for shape in out_shapes],
        out_shape=out_shapes,
        scratch_shapes=scratch,
        compiler_params=pltpu.CompilerParams(vmem_limit_bytes=FAR_LIMIT),
        cost_estimate=pl.CostEstimate(flops=flops, bytes_accessed=4_000_000, transcendentals=1_000_000),
    )(*scalars, *arrays)


def near_call(kernel, scalars, operands, out_shapes, scratch, flops, near_outs=(), carried=()):
    def is_near(operand):
        return isinstance(operand, Near)

    def plain_array(operand):
        return operand.array if isinstance(operand, (Near, Part)) else operand

    def source_of(operand, ref):
        return operand.of(ref) if isinstance(operand, Part) else ref

    far = [operand for operand in operands if not is_near(operand)]
    far_outs = [shape for place, shape in enumerate(out_shapes) if place not in near_outs]

    def body(*refs):
        refs = list(refs)

        def take(count):
            taken = refs[:count]
            del refs[:count]
            return taken

        scalar_refs, operand_refs, carried_refs = take(len(scalars)), take(len(operands)), take(len(carried))
        out_refs, carried_outs = take(len(out_shapes)), take(len(carried))
        scratch_refs, buffers, out_buffers = take(len(scratch)), take(len(far)), take(len(far_outs))
        sems, carried_sems, out_sems = refs
        inputs, arriving = [], []
        for operand, ref in zip(operands, operand_refs, strict=True):
            if is_near(operand):
                inputs.append(ref)
                continue
            place = len(arriving)
            arriving.append(pltpu.make_async_copy(source_of(operand, ref), buffers[place], sems.at[place]))
            inputs.append(buffers[place])
        for copy in arriving:
            copy.start()
        passing = [
            pltpu.make_async_copy(source_of(operand, ref), target, carried_sems.at[place])
            for place, (operand, ref, target) in enumerate(zip(carried, carried_refs, carried_outs, strict=True))
        ]
        for copy in passing:
            copy.start()
        for copy in arriving:
            copy.wait()
        outputs, leaving = [], []
        for place, ref in enumerate(out_refs):
            if place in near_outs:
                outputs.append(ref)
                continue
            outputs.append(out_buffers[len(leaving)])
            leaving.append(pltpu.make_async_copy(outputs[-1], ref, out_sems.at[len(leaving)]))
        kernel(*scalar_refs, *inputs, *outputs, *scratch_refs)
        for copy in leaving:
            copy.start()
        for copy in passing + leaving:
            copy.wait()

    return pl.pallas_call(
        body,
        in_specs=[SMEM] * len(scalars)
        + [VMEM if is_near(operand) else ANY for operand in operands]
        + [ANY] * len(carried),
        out_specs=[VMEM if place in near_outs else ANY for place in range(len(out_shapes))] + [VMEM] * len(carried),
        out_shape=[*out_shapes, *[shape_of(operand.shape, operand.dtype) for operand in carried]],
        scratch_shapes=[
            *scratch,
            *[pltpu.VMEM(operand.shape, operand.dtype) for operand in far],
            *[pltpu.VMEM(shape.shape, shape.dtype) for shape in far_outs],
            pltpu.SemaphoreType.DMA((max(len(far), 1),)),
            pltpu.SemaphoreType.DMA((max(len(carried), 1),)),
            pltpu.SemaphoreType.DMA((max(len(far_outs), 1),)),
        ],
        compiler_params=pltpu.CompilerParams(vmem_limit_bytes=NEAR_LIMIT),
        cost_estimate=pl.CostEstimate(flops=flops, bytes_accessed=4_000_000, transcendentals=1_000_000),
    )(*scalars, *[plain_array(operand) for operand in operands], *[plain_array(operand) for operand in carried])


def shape_of(shape, dtype):
    return jax.ShapeDtypeStruct(shape, dtype)


def shifted(value, lat_steps, lon_steps):
    lon_count, lat_count = lax.axis_size("lon"), lax.axis_size("lat")
    pairs = []
    for lon in range(lon_count):
        for lat in range(lat_count):
            source = ((lon + lon_steps) % lon_count) * lat_count + (lat + lat_steps) % lat_count
            pairs.append((source, lon * lat_count + lat))
    return lax.ppermute(value, ("lon", "lat"), pairs)


def per_device(
    inputs,
    grad_out,
    region,
    bias_level,
    norm_gains,
    in_weight,
    out_weight,
    up_weight,
    down_weight,
    bias_tables,
):
    weights = (norm_gains, in_weight, out_weight, up_weight, down_weight.transpose(0, 2, 1))
    first_weights = [Part(array, 0) for array in weights]
    second_weights = [Part(array, 1) for array in weights]
    inputs, grad_out = inputs.transpose(1, 2, 0, 3), grad_out.transpose(1, 2, 0, 3)
    bias_tables = bias_tables.transpose(0, 1, 3, 2, 4)
    bias_level = bias_level.T
    is_upper = odd(core_step()[1]).reshape(1)

    quad_shape = shape_of((2 * QUAD, C), BF16)
    grid_shape = shape_of((6, 12, 4, C), BF16)
    half_shape = shape_of((ROWS // 2, 128), BF16)
    table_shape = shape_of((TABLE_ROWS, 128), BF16)
    weights_shape = (2 * HEADS, WIN, WIN)
    grads_scratch = pltpu.VMEM((2, 2 * HEADS * WIN, 128), F32)
    row_scratch = pltpu.VMEM((16, 26 * 128), F32)
    shaped_scratch = pltpu.VMEM((4, 2 * 72 + 16, 128), F32)
    bias_scratch = pltpu.VMEM((2, 2 * HEADS * WIN, 128), F32)
    rows_scratch = pltpu.VMEM((2, TOKENS, 128), F32)
    packed_scratch = pltpu.VMEM((ROWS, 128), BF16)

    quads = call(
        first_kernel,
        (bias_level,),
        (inputs, grad_out, *first_weights, Part(bias_tables, 0)),
        [quad_shape] * 4
        + [
            shape_of(weights_shape, BF16),
            shape_of((2, 3, C, WIN), BF16),
            shape_of((3, TOKENS, C), BF16),
        ],
        [rows_scratch, row_scratch, shaped_scratch, bias_scratch],
        1_000_000_000,
    )
    stored = list(quads[4:])
    ahead = (
        quads[3],
        shifted(quads[2], 0, 1),
        shifted(quads[1], 1, 0),
        shifted(quads[0], 1, 1),
    )
    (bias,) = call(
        prepare_kernel,
        (bias_level,),
        (region.transpose(1, 0, 2), Part(bias_tables, 1)),
        [shape_of(weights_shape, BF16)],
        [row_scratch, shaped_scratch, bias_scratch],
        500_000_000,
    )
    *back, second_keep, second_send, second_scaled = call(
        second_kernel,
        (is_upper,),
        (*ahead, bias, *second_weights),
        [quad_shape] * 4 + [half_shape, half_shape, shape_of(weights_shape, BF16)],
        [pltpu.VMEM(weights_shape, BF16), packed_scratch],
        3_000_000_000,
    )
    home = [
        shifted(back[3], -1, -1),
        shifted(back[2], -1, 0),
        shifted(back[1], 0, -1),
        back[0],
    ]
    home[3], after_second = tie((home[3], is_upper))
    active, slope, *first_near = near_call(
        activation_kernel,
        (after_second,),
        (stored[2], first_weights[0], first_weights[3]),
        [shape_of((TOKENS, FFN), BF16), shape_of((TOKENS, FFN), BF16)],
        [],
        300_000_000,
        (0, 1),
        (*stored, first_weights[0], *first_weights[2:]),
    )
    second_got = exchanged(second_send, core_step()[0])
    first_keep, first_send, grad_rows, first_scaled = near_call(
        third_kernel,
        (is_upper,),
        tuple(map(Near, (*home, *first_near[:3], active, slope, first_near[3], in_weight, *first_near[4:]))),
        [half_shape, half_shape, shape_of((TOKENS, C), BF16), shape_of(weights_shape, BF16)],
        [packed_scratch],
        2_000_000_000,
    )
    blocks_out, grad_inputs = near_call(
        grids_kernel,
        (),
        (*home, grad_rows),
        [grid_shape, grid_shape],
        [rows_scratch],
        100_000_000,
    )

    def collect(kernel, rows, *operands):
        return near_call(
            kernel,
            (bias_level,),
            operands,
            [shape_of((rows, 128), BF16)],
            [row_scratch, shaped_scratch, grads_scratch],
            500_000_000,
        )[0]

    first_got = exchanged(first_send, core_step()[0])
    second = added(second_keep, second_got)
    first = added(first_keep, first_got)
    first, second, first_scaled, second_scaled = tie((first, second, first_scaled, second_scaled))
    second_tables = collect(collect_kernel, TABLE_ROWS, second_scaled)
    tables = collect(finish_kernel, 2 * TABLE_ROWS, first_scaled, second_tables)
    totals = unpack(is_upper, *sum_all(first, second, tables, second_tables))
    gains, grad_in, grad_out_weight, grad_up, grad_down, grad_tables = totals
    return (
        blocks_out.transpose(2, 0, 1, 3),
        grad_inputs.transpose(2, 0, 1, 3),
        gains,
        grad_in,
        grad_out_weight,
        grad_up,
        grad_down.transpose(0, 2, 1),
        grad_tables.transpose(0, 1, 3, 2, 4),
    )


def exchanged(value, mask):
    lon_count, lat_count = lax.axis_size("lon"), lax.axis_size("lat")
    pairs = []
    for lon in range(lon_count):
        for lat in range(lat_count):
            pairs.append(((lon ^ mask[1]) * lat_count + (lat ^ mask[0]), lon * lat_count + lat))
    return lax.ppermute(value, ("lon", "lat"), pairs)


def added(left, right):
    return (left.astype(F32) + right.astype(F32)).astype(BF16)


def odd(mask):
    lat, lon = lax.axis_index("lat") & mask[0], lax.axis_index("lon") & mask[1]
    parity = jnp.int32(0)
    for place in range(5):
        parity = parity ^ (lat >> place) ^ (lon >> place)
    return parity & 1


def split(value, owner):
    half = value.shape[0] // 2
    up = odd(owner) != 0
    return jnp.where(up, value[half:], value[:half]), jnp.where(up, value[:half], value[half:])


def halve(value, mask, owner):
    keep, send = split(value, owner)
    return added(keep, exchanged(send, mask))


def double(value, mask, owner):
    other = exchanged(value, mask)
    up = odd(owner) != 0
    return jnp.concatenate([jnp.where(up, other, value), jnp.where(up, value, other)], axis=0)


def tie(values):
    return lax.optimization_barrier(values)


def core_step():
    return (1, 0), (1, 0)


def sum_all(first, second, tables, second_tables):
    core = core_step()[0]
    if lax.axis_size("lat") != 16 or lax.axis_size("lon") != 16:
        return sum_small(first, second, tables)
    y_low, y_high = ((2, 0), (2, 0)), (0, 8)
    x_low, x_high = ((4, 0), (12, 0)), ((12, 0), (8, 0))
    z_low, z_mid, z_high = ((0, 1), (0, 5)), ((0, 2), (0, 6)), (0, 7)

    first, second = halve(first, *y_low), halve(second, *x_low)
    first, second, second_tables = tie((first, second, second_tables))
    first, second = halve(first, *x_low), halve(second, *y_low)
    first, second = tie((first, second))
    rows = first.shape[0]
    joined = halve(jnp.concatenate([first, second], axis=0), *x_high)
    joined, tables = tie((joined, tables))
    for mask, owner in (z_low, z_mid):
        keep, send = split(tables, owner)
        got = exchanged(jnp.concatenate([joined, send], axis=0), mask)
        joined, tables = added(joined, got[:rows]), added(keep, got[rows:])
    joined = jnp.concatenate([joined, tables], axis=0)
    for mask in (z_high, y_high):
        joined = added(joined, exchanged(joined, mask))
    joined, tables = tie((joined[:rows], joined[rows:]))
    tables = double(tables, *z_mid)
    joined = double(joined, *x_high)
    first, second = tie((joined[:rows], joined[rows:]))
    first, second = double(first, *x_low), double(second, *y_low)
    first, second, tables = tie((first, second, tables))
    first, second = double(first, *y_low), double(second, *x_low)
    tables = double(tables, *z_low)
    first, second, tables = tie((first, second, tables))
    return first, exchanged(first, core), second, exchanged(second, core), tables


def sum_small(first, second, tables):
    def over(value, axis):
        for place in range(lax.axis_size(axis).bit_length() - 1):
            if axis == "lon" or place:
                value = added(value, exchanged(value, (1 << place, 0) if axis == "lat" else (0, 1 << place)))
        return value

    core = core_step()[0]
    first, second = over(over(first, "lat"), "lon"), over(over(second, "lat"), "lon")
    return first, exchanged(first, core), second, exchanged(second, core), over(tables, "lon")


def unpack_kernel(upper_ref, first_own, first_other, second_own, second_other, tables_ref, *refs):
    results, (rows_ref, *buffers, sems) = refs[:6], refs[6:]
    gains_ref, in_ref, out_ref, up_ref, down_ref, grads_ref = buffers
    half = ROWS // 2
    is_upper = jnp.broadcast_to(upper_ref[0] == 1, (1, 128))
    copies = []

    def leave(index, block):
        copy = pltpu.make_async_copy(buffers[index].at[block], results[index].at[block], sems.at[index, block])
        copy.start()
        copies.append(copy)

    for block, (own, other) in enumerate(((first_own, first_other), (second_own, second_other))):

        def rows(start, stop, own=own, other=other):
            if start < half < stop:
                return jnp.concatenate([rows(start, half), rows(half, stop)], axis=0)
            lower = start < half
            start, stop = (start, stop) if lower else (start - half, stop - half)
            mine, theirs = own[start:stop].astype(F32), other[start:stop].astype(F32)
            return jnp.where(is_upper, theirs, mine) if lower else jnp.where(is_upper, mine, theirs)

        for index, (ref, start) in enumerate(((up_ref, 1152), (down_ref, 2304))):
            for part in range(6):
                lanes = slice(part * 128, (part + 1) * 128)
                ref[block, :, lanes] = rows(start + part * C, start + (part + 1) * C)
            leave(3 + index, block)
        for part in range(4):
            in_ref[block, :, part * 128 : (part + 1) * 128] = rows(part * C, (part + 1) * C)
        shared = rows(768, 960)
        in_ref[block, :, 512:] = shared[:, :64]
        leave(1, block)
        out_ref[block, :, :128] = rows(960, 1152)
        out_ref[block, :, 128:] = shared[:, 64:]
        leave(2, block)
        rows_ref[...] = tables_ref[block * TABLE_ROWS : (block + 1) * TABLE_ROWS].astype(F32)
        for slab in range(26):
            width = min(128, RELPOS - slab * 128)
            for level in range(2):
                start = slab * 12 + level * HEADS
                grads_ref[block, 0, :, level, slab * 128 : slab * 128 + width] = rows_ref[start : start + HEADS, :width]
        leave(5, block)
        gains = rows(GAIN_ROWS, GAIN_ROWS + 16)
        gains_ref[block, 0:1, :128] = gains[0:1]
        gains_ref[block, 0:1, 128:] = gains[1:2, :64]
        gains_ref[block, 1:2, :128] = gains[2:3]
        gains_ref[block, 1:2, 128:] = gains[1:2, 64:]
        leave(0, block)
    for copy in copies:
        copy.wait()


def unpack(is_upper, *values):
    shapes = [
        (2, 2, C),
        (2, C, 3 * C),
        (2, C, C),
        (2, C, FFN),
        (2, C, FFN),
        (2, 1, HEADS, 2, RELPOS),
    ]
    return pl.pallas_call(
        unpack_kernel,
        in_specs=[SMEM] + [pl.BlockSpec(memory_space=pltpu.VMEM)] * len(values),
        out_specs=[pl.BlockSpec(memory_space=pl.ANY)] * len(shapes),
        out_shape=[shape_of(shape, F32) for shape in shapes],
        scratch_shapes=[pltpu.VMEM((TABLE_ROWS, 128), F32)]
        + [pltpu.VMEM(shape, F32) for shape in shapes]
        + [pltpu.SemaphoreType.DMA((len(shapes), 2))],
        compiler_params=pltpu.CompilerParams(vmem_limit_bytes=NEAR_LIMIT),
    )(is_upper, *values)


def solution(mesh):
    placed = (
        P(None, "lat", "lon", None),
        P(None, "lat", "lon", None),
        P(None, "lat", "lon"),
        P(None, "lat"),
        P(),
        P(),
        P(),
        P(),
        P(),
        P(None, "lat", None, None, None),
    )
    return jax.shard_map(
        per_device,
        mesh=mesh,
        in_specs=placed,
        out_specs=(
            P(None, "lat", "lon", None),
            P(None, "lat", "lon", None),
            P(),
            P(),
            P(),
            P(),
            P(),
            P(None, "lat", None, None, None),
        ),
        check_vma=False,
    )
```

```python
import functools
import math

import jax
import jax.numpy as jnp
from jax import lax
from jax.experimental import pallas as pl
from jax.experimental.pallas import tpu as pltpu
from jax.sharding import PartitionSpec as P

C = 192
HEADS = 6
HEAD = 32
FFN = 768
WIN_Z = 2
WIN_LAT = 6
WIN_LON = 12
WIN = 144
TOKENS = 2 * WIN
QUAD = 72
RELPOS = 3312
SPAN = 2 * WIN_LON - 1
ROWS = 3584
GAIN_ROWS = 3456
TABLE_ROWS = 320

EPSILON = 1e-05
NEGATIVE = -1000000000.0
SCALE = 1.0 / math.sqrt(HEAD)

F32 = jnp.float32
BF16 = jnp.bfloat16


def mm(left, right):
    return lax.dot_general(left, right, (((1,), (0,)), ((), ())), preferred_element_type=F32)


def mm_nt(left, right):
    return lax.dot_general(left, right, (((1,), (1,)), ((), ())), preferred_element_type=F32)


def eye(size):
    return (
        lax.broadcasted_iota(jnp.int32, (size, size), 0) == lax.broadcasted_iota(jnp.int32, (size, size), 1)
    ).astype(F32).astype(BF16)


def divided(value, divisor, count):
    quotient = jnp.zeros_like(value)
    for number in range(1, count):
        quotient = quotient + (value >= number * divisor).astype(jnp.int32)
    return quotient, value - quotient * divisor


def lanes_of_tokens():
    return lax.broadcasted_iota(jnp.int32, (1, TOKENS), 1)


def row_of_quad(roll):
    lat_half, rest = divided(lanes_of_tokens(), 2 * QUAD, 2)
    lon_half, rest = divided(rest, QUAD, 2)
    level, rest = divided(rest, 18, 4)
    row, col = divided(rest, 6, 3)
    level = (level + 4 - roll) & 3
    return (level * 6 + lat_half * 3 + row) * 12 + lon_half * 6 + col


def quad_of_row(roll):
    level, rest = divided(lanes_of_tokens(), QUAD, 4)
    row, col = divided(rest, 12, 6)
    lat_half, row = divided(row, 3, 2)
    lon_half, col = divided(col, 6, 2)
    level = (level + roll) & 3
    return lat_half * 2 * QUAD + lon_half * QUAD + level * 18 + row * 6 + col


def places(rows):
    return (lax.broadcasted_iota(jnp.int32, (TOKENS, TOKENS), 0) == rows).astype(F32).astype(BF16)


def turned(value):
    return mm_nt(eye(value.shape[1]), value).astype(BF16)


def norm_stats(values):
    centre = values - jnp.mean(values, axis=-1, keepdims=True)
    inverse = lax.rsqrt(jnp.mean(centre * centre, axis=-1, keepdims=True) + EPSILON)
    return centre * inverse, inverse


def norm_backward(upstream, normal_hat, inverse):
    upstream_mean = jnp.mean(upstream, axis=-1, keepdims=True)
    cross_mean = jnp.mean(upstream * normal_hat, axis=-1, keepdims=True)
    return inverse * (upstream - upstream_mean - normal_hat * cross_mean)


def head_lanes(head):
    lane = lax.broadcasted_iota(jnp.int32, (1, C), 1)
    return ((lane >= head * HEAD) & (lane < (head + 1) * HEAD)).astype(F32).astype(BF16)


def pair_keys():
    row = lax.broadcasted_iota(jnp.int32, (512, 1), 0)
    within = row & 127
    third = (within >= SPAN).astype(jnp.int32) + (within >= 2 * SPAN).astype(jnp.int32)
    row_group = (row >> 7) * 3 + third
    row_offset = within - third * SPAN
    col = lax.broadcasted_iota(jnp.int32, (1, 256), 1)
    col_group = jnp.zeros_like(col)
    for group in range(1, 12):
        col_group = col_group + (col >= group * 12).astype(jnp.int32)
    col_place = col - col_group * 12
    usable = (row_group == col_group) & (within < 3 * SPAN) & (col < WIN)
    return jnp.where(usable, col_place + 11 - row_offset, -1).astype(F32).astype(BF16)


def pairs_of(keys, place):
    return jnp.where(keys == jnp.asarray(place, BF16), jnp.asarray(1, BF16), jnp.asarray(0, BF16))


def table_start(zs, zt, hs, ht):
    return (((zs * 2 + zt) * 6 + hs) * 6 + ht) * SPAN


def spread_bias(table_ref, row_ref, shaped_ref, bias_ref):
    for head in range(HEADS):
        row_ref[head * 2 : head * 2 + 2, :RELPOS] = table_ref[head].astype(F32)
    row = row_ref[: 2 * HEADS]
    for zs in range(2):
        for zt in range(2):
            for group in range(2):
                for ht in range(6):
                    pieces = []
                    for hs in range(group * 3, group * 3 + 3):
                        start = table_start(zs, zt, hs, ht)
                        pieces.append(row[:, start : start + SPAN])
                    pieces.append(jnp.zeros((2 * HEADS, 128 - 3 * SPAN), F32))
                    target = pl.ds(zt * 6 + ht, 2 * HEADS, stride=12)
                    shaped_ref[zs * 2 + group, target, :] = jnp.concatenate(pieces, axis=1)
    keys = pair_keys()
    shaped = jnp.concatenate([shaped_ref[part, :WIN].astype(BF16) for part in range(4)], axis=1)
    for col in range(WIN_LON):
        spread = mm(shaped, pairs_of(keys, col))
        bias_ref[0, pl.ds(col, WIN, stride=12), :] = spread[:, :128]
        bias_ref[1, pl.ds(col, WIN, stride=12), :] = spread[:, 128:]


def collect_bias(scaled_ref, levels, row_ref, shaped_ref, grads_ref, out_ref):
    for place in range(2 * HEADS):
        rows = slice(place * WIN, (place + 1) * WIN)
        piece = scaled_ref[place].astype(F32)
        grads_ref[0, rows] = piece[:, :128]
        grads_ref[1, rows] = jnp.concatenate([piece[:, 128:], jnp.zeros((WIN, 256 - WIN), F32)], axis=1)
    keys = pair_keys()
    total = jnp.zeros((WIN, 512), F32)
    for col in range(WIN_LON):
        left = grads_ref[0, pl.ds(col, WIN, stride=12), :]
        right = grads_ref[1, pl.ds(col, WIN, stride=12), :]
        piece = jnp.concatenate([left, right], axis=1).astype(BF16)
        total = total + mm_nt(piece, pairs_of(keys, col))
    total = total * (1.0 / SCALE)
    for part in range(4):
        shaped_ref[part, :WIN] = total[:, part * 128 : (part + 1) * 128]
    row_ref[...] = jnp.zeros_like(row_ref)
    for zs in range(2):
        for zt in range(2):
            for group in range(2):
                for ht in range(6):
                    pieces = [
                        shaped_ref[zs * 2 + group, pl.ds(window * 72 + zt * 6 + ht, HEADS, stride=12), :]
                        for window in range(2)
                    ]
                    for level in range(2):
                        chosen = jnp.zeros((HEADS, 128), F32)
                        for window in range(2):
                            chosen = chosen + jnp.where(levels[window] == level, pieces[window], 0.0)
                        for index in range(3):
                            start = table_start(zs, zt, group * 3 + index, ht)
                            row_ref[level * 8 : level * 8 + HEADS, start : start + SPAN] = chosen[
                                :, index * SPAN : (index + 1) * SPAN
                            ]
    for slab in range(26):
        lanes = slice(slab * 128, (slab + 1) * 128)
        rows = jnp.concatenate([row_ref[:HEADS, lanes], row_ref[8 : 8 + HEADS, lanes]], axis=0)
        shaped_ref[slab // 13, slab % 13 * 12 : slab % 13 * 12 + 12] = rows
    out_ref[...] = jnp.concatenate(
        [shaped_ref[0, :156], shaped_ref[1, :156], jnp.zeros((TABLE_ROWS - 312, 128), F32)], axis=0
    ).astype(BF16)


def load_tiles(bias_ref, level, head):
    rows = pl.ds(pl.multiple_of((head * 2 + level) * WIN, 8), WIN)
    return jnp.concatenate([bias_ref[0, rows, :], bias_ref[1, rows, : WIN - 128]], axis=1)


def attention(normed, in_weight, bias_of, weights_ref):
    eye_c = eye(C)
    weight_q, weight_k, weight_v = in_weight[:, :C], in_weight[:, C : 2 * C], in_weight[:, 2 * C :]
    kept = []
    mixed = []
    for window in range(2):
        rows = normed[window * WIN : (window + 1) * WIN]
        keys = mm(rows, weight_k).astype(BF16)
        values = mm(rows, weight_v).astype(BF16)
        queries = mm(rows, weight_q).astype(BF16)
        queries_t = mm_nt(eye_c, queries).astype(BF16)
        keys_t = mm_nt(eye_c, keys).astype(BF16)
        values_t = mm_nt(eye_c, values).astype(BF16)
        parts = []
        for head in range(HEADS):
            own = keys * head_lanes(head)
            scores = mm(own, queries_t) * SCALE + bias_of(window, head)
            weights = jnp.exp(scores - jnp.max(scores, axis=0, keepdims=True))
            weights = weights * (1.0 / jnp.sum(weights, axis=0, keepdims=True))
            weights = weights.astype(BF16)
            weights_ref[window * HEADS + head] = weights
            parts.append(mm(values_t[head * HEAD : (head + 1) * HEAD], weights))
        mixed.append(jnp.concatenate(parts, axis=0).astype(BF16))
        kept.append((queries_t, keys_t, values))
    return kept, mixed


def feed_forward(hidden, gain, up_weight):
    hat, inverse = norm_stats(hidden)
    normed = (hat * gain).astype(BF16)
    return hat, inverse, normed, mm(normed, up_weight)


def gelu_parts(expanded):
    cumulative = 0.5 * (1.0 + lax.erf(expanded * (1.0 / math.sqrt(2.0))))
    slope = cumulative + expanded * jnp.exp(-0.5 * expanded * expanded) * (1.0 / math.sqrt(2.0 * math.pi))
    return (expanded * cumulative).astype(BF16), slope


def natural_mixed(mixed):
    eye_w = eye(WIN)
    return jnp.concatenate([mm_nt(eye_w, part) for part in mixed], axis=0).astype(BF16)


def pack(packed_ref, start, value):
    height = value.shape[0]
    for part in range(value.shape[1] // 128):
        rows = slice(start + part * height, start + (part + 1) * height)
        packed_ref[rows] = value[:, part * 128 : (part + 1) * 128].astype(BF16)


def backward(
    grad,
    active,
    slope,
    second_hat,
    second_inverse,
    second_norm,
    mixed,
    attended,
    weights_ref,
    first_hat,
    first_inverse,
    first_norm,
    gain_one,
    gain_two,
    in_weight,
    out_weight,
    up_weight,
    down_weight,
    scaled_ref,
    packed_ref,
):
    eye_c = eye(C)
    grad_half = grad.astype(BF16)
    pack(packed_ref, 2304, mm(turned(grad_half), active))
    grad_expanded = (mm(grad_half, down_weight) * slope).astype(BF16)
    normed_t = turned(second_norm)
    pack(packed_ref, 1152, mm(normed_t, grad_expanded))
    grad_second = mm_nt(grad_expanded, up_weight)
    gain_two_grad = jnp.sum(grad_second * second_hat, axis=0, keepdims=True)
    grad_hidden = (grad + norm_backward(grad_second * gain_two, second_hat, second_inverse)).astype(BF16)
    grad_out = mm(mixed[0], grad_hidden[:WIN]) + mm(mixed[1], grad_hidden[WIN:])
    packed_ref[960:1152] = grad_out[:, :128].astype(BF16)
    grad_mixed = mm_nt(grad_hidden, out_weight).astype(BF16)
    projected = []
    for window in range(2):
        queries_t, keys_t, values = attended[window]
        upstream_t = mm_nt(eye_c, grad_mixed[window * WIN : (window + 1) * WIN]).astype(BF16)
        grad_q, grad_k, grad_v = [], [], []
        for head in range(HEADS):
            lanes = slice(head * HEAD, (head + 1) * HEAD)
            half = weights_ref[window * HEADS + head]
            weights = half.astype(F32)
            own = values * head_lanes(head)
            grad_weights = mm(own, upstream_t)
            inner = jnp.sum(grad_weights * weights, axis=0, keepdims=True)
            grad_scores = weights * (grad_weights - inner)
            scaled = (grad_scores * SCALE).astype(BF16)
            scaled_ref[window * HEADS + head] = scaled
            grad_v.append(mm_nt(upstream_t[lanes], half))
            grad_q.append(mm(keys_t[lanes], scaled))
            grad_k.append(mm_nt(queries_t[lanes], scaled))
        projected_t = jnp.concatenate(grad_q + grad_k + grad_v, axis=0).astype(BF16)
        projected.append(mm_nt(eye(WIN), projected_t))
    projected = jnp.concatenate(projected, axis=0).astype(BF16)
    first_t = turned(first_norm)
    grad_in = mm(first_t, projected)
    pack(packed_ref, 0, grad_in[:, :512])
    packed_ref[768:960] = jnp.concatenate([grad_in[:, 512:], grad_out[:, 128:]], axis=1).astype(BF16)
    grad_first = mm_nt(projected, in_weight)
    gain_one_grad = jnp.sum(grad_first * first_hat, axis=0, keepdims=True)
    gain_rows = jnp.concatenate(
        [
            gain_one_grad[:, :128],
            jnp.concatenate([gain_one_grad[:, 128:], gain_two_grad[:, 128:]], axis=1),
            gain_two_grad[:, :128],
            jnp.zeros((ROWS - GAIN_ROWS - 3, 128), F32),
        ],
        axis=0,
    )
    packed_ref[GAIN_ROWS:ROWS] = gain_rows.astype(BF16)
    return (
        grad_hidden.astype(F32) + norm_backward(grad_first * gain_one, first_hat, first_inverse)
    ).astype(BF16)


def load_grid(grid_ref, rows_ref):
    for row in range(6):
        for col in range(12):
            piece = grid_ref[row, col].astype(F32)
            target = pl.ds(row * 12 + col, 4, stride=72)
            rows_ref[0, target, :] = piece[:, :128]
            rows_ref[1, target, :] = jnp.concatenate([piece[:, 128:], jnp.zeros((4, 64), F32)], axis=1)
    return jnp.concatenate([rows_ref[0], rows_ref[1][:, :64]], axis=1)


def store_grid(rows, rows_ref, grid_ref):
    rows_ref[0] = rows[:, :128]
    rows_ref[1] = jnp.concatenate([rows[:, 128:], jnp.zeros((TOKENS, 64), F32)], axis=1)
    for row in range(6):
        for col in range(12):
            source = pl.ds(row * 12 + col, 4, stride=72)
            piece = jnp.concatenate([rows_ref[0, source, :], rows_ref[1, source, :][:, :64]], axis=1)
            grid_ref[row, col] = piece.astype(BF16)


def block_weights(gains_ref, in_ref, out_ref, up_ref, down_ref):
    gains = gains_ref[...]
    return gains[0:1], gains[1:2], in_ref[...], out_ref[...], up_ref[...], down_ref[...]


def write_halves(upper_ref, packed_ref, keep_ref, send_ref):
    half = ROWS // 2
    is_upper = upper_ref[0] == 1

    @pl.when(is_upper)
    def _():
        keep_ref[...] = packed_ref[half:]
        send_ref[...] = packed_ref[:half]

    @pl.when(jnp.logical_not(is_upper))
    def _():
        keep_ref[...] = packed_ref[:half]
        send_ref[...] = packed_ref[half:]


def first_kernel(
    levels_ref,
    inputs_ref,
    grad_ref,
    gains_ref,
    in_ref,
    out_ref,
    up_ref,
    down_ref,
    table_ref,
    quad_0,
    quad_1,
    quad_2,
    quad_3,
    weights_out,
    turned_out,
    flat_out,
    rows_ref,
    row_ref,
    shaped_ref,
    bias_ref,
):
    levels = [levels_ref[0, 0], levels_ref[0, 1]]
    gain_one, gain_two, in_weight, out_weight, up_weight, down_weight = block_weights(
        gains_ref, in_ref, out_ref, up_ref, down_ref
    )
    order = places(quad_of_row(0))
    grad_quads = mm(order, load_grid(grad_ref, rows_ref).astype(BF16))
    flat = load_grid(inputs_ref, rows_ref)
    flat_out[0] = flat.astype(BF16)
    spread_bias(table_ref, row_ref, shaped_ref, bias_ref)
    hat, _ = norm_stats(flat)
    normed = (hat * gain_one).astype(BF16)
    attended, mixed = attention(
        normed, in_weight, lambda window, head: load_tiles(bias_ref, levels[window], head), weights_out
    )
    for window in range(2):
        turned_out[window, 0] = attended[window][0]
        turned_out[window, 1] = attended[window][1]
        turned_out[window, 2] = mixed[window]
        flat_out[2, window * WIN : (window + 1) * WIN] = attended[window][2]
    hidden = (flat + mm(natural_mixed(mixed), out_weight)).astype(BF16)
    flat_out[1] = hidden
    hidden = hidden.astype(F32)
    _, _, _, expanded = feed_forward(hidden, gain_two, up_weight)
    active = (expanded * 0.5 * (1.0 + lax.erf(expanded * (1.0 / math.sqrt(2.0))))).astype(BF16)
    result = (hidden + mm_nt(active, down_weight)).astype(BF16)
    result_quads = mm(order, result)
    for index, quad in enumerate((quad_0, quad_1, quad_2, quad_3)):
        rows = slice(index * QUAD, (index + 1) * QUAD)
        quad[...] = jnp.concatenate([result_quads[rows], grad_quads[rows]], axis=0).astype(BF16)


def region_row(region_ref, window):
    pieces = [region_ref[row, window * 2 + level : window * 2 + level + 1, :] for level in range(2) for row in range(6)]
    return jnp.concatenate(pieces, axis=1)


def prepare_kernel(
    levels_ref, region_ref, table_ref, bias_out, row_ref, shaped_ref, bias_ref
):
    levels = [levels_ref[0, 0], levels_ref[0, 1]]
    spread_bias(table_ref, row_ref, shaped_ref, bias_ref)
    diagonal = lax.broadcasted_iota(jnp.int32, (WIN, WIN), 0) == lax.broadcasted_iota(jnp.int32, (WIN, WIN), 1)
    for window in range(2):
        across = region_row(region_ref, window).astype(F32)
        down = jnp.sum(jnp.where(diagonal, across, 0.0), axis=1, keepdims=True)
        same = across == down
        for head in range(HEADS):
            bias = jnp.where(same, load_tiles(bias_ref, levels[window], head), NEGATIVE)
            bias_out[window * HEADS + head] = bias.astype(BF16)


def second_kernel(
    upper_ref,
    quad_0,
    quad_1,
    quad_2,
    quad_3,
    bias_ref,
    gains_ref,
    in_ref,
    out_ref,
    up_ref,
    down_ref,
    back_0,
    back_1,
    back_2,
    back_3,
    keep_ref,
    send_ref,
    scaled_ref,
    weights_ref,
    packed_ref,
):
    quads = [quad[...].astype(F32) for quad in (quad_0, quad_1, quad_2, quad_3)]
    ahead = places(row_of_quad(1))
    flat = mm(ahead, jnp.concatenate([quad[:QUAD] for quad in quads], axis=0).astype(BF16))
    grad = mm(ahead, jnp.concatenate([quad[QUAD:] for quad in quads], axis=0).astype(BF16))
    gain_one, gain_two, in_weight, out_weight, up_weight, down_weight = block_weights(
        gains_ref, in_ref, out_ref, up_ref, down_ref
    )
    first_hat, first_inverse = norm_stats(flat)
    first_norm = (first_hat * gain_one).astype(BF16)
    attended, mixed = attention(
        first_norm, in_weight, lambda window, head: bias_ref[window * HEADS + head].astype(F32), weights_ref
    )
    hidden = (flat + mm(natural_mixed(mixed), out_weight)).astype(BF16).astype(F32)
    second_hat, second_inverse, second_norm, expanded = feed_forward(hidden, gain_two, up_weight)
    active, slope = gelu_parts(expanded)
    result = (hidden + mm_nt(active, down_weight)).astype(BF16)
    grad_in = backward(
        grad, active, slope, second_hat, second_inverse, second_norm, mixed, attended, weights_ref,
        first_hat, first_inverse, first_norm, gain_one, gain_two, in_weight, out_weight, up_weight,
        down_weight, scaled_ref, packed_ref,
    )
    back = places(quad_of_row(1))
    result_quads, grad_quads = mm(back, result), mm(back, grad_in)
    for index, quad in enumerate((back_0, back_1, back_2, back_3)):
        rows = slice(index * QUAD, (index + 1) * QUAD)
        quad[...] = jnp.concatenate([result_quads[rows], grad_quads[rows]], axis=0).astype(BF16)
    write_halves(upper_ref, packed_ref, keep_ref, send_ref)


def collect_kernel(levels_ref, scaled_ref, tables_out, row_ref, shaped_ref, grads_ref):
    levels = [levels_ref[0, 0], levels_ref[0, 1]]
    collect_bias(scaled_ref, levels, row_ref, shaped_ref, grads_ref, tables_out)


def finish_kernel(
    levels_ref, scaled_ref, second_tables_ref, tables_out, row_ref, shaped_ref, grads_ref
):
    levels = [levels_ref[0, 0], levels_ref[0, 1]]
    collect_bias(scaled_ref, levels, row_ref, shaped_ref, grads_ref, tables_out.at[:TABLE_ROWS])
    tables_out[TABLE_ROWS:] = second_tables_ref[...]


def activation_kernel(_, flat_ref, gains_ref, up_ref, active_out, slope_out):
    _, _, _, expanded = feed_forward(flat_ref[1].astype(F32), gains_ref[1:2], up_ref[...])
    active, slope = gelu_parts(expanded)
    active_out[...] = active
    slope_out[...] = slope.astype(BF16)


def third_kernel(
    upper_ref,
    quad_0,
    quad_1,
    quad_2,
    quad_3,
    weights_ref,
    turned_ref,
    flat_ref,
    active_ref,
    slope_ref,
    gains_ref,
    in_ref,
    out_ref,
    up_ref,
    down_ref,
    keep_ref,
    send_ref,
    rows_out,
    scaled_ref,
    packed_ref,
):
    quads = [quad[...].astype(F32) for quad in (quad_0, quad_1, quad_2, quad_3)]
    grad = mm(places(row_of_quad(0)), jnp.concatenate([quad[QUAD:] for quad in quads], axis=0).astype(BF16))
    gain_one, gain_two, in_weight, out_weight, up_weight, down_weight = block_weights(
        gains_ref, in_ref.at[0], out_ref, up_ref, down_ref
    )
    first_hat, first_inverse = norm_stats(flat_ref[0].astype(F32))
    first_norm = (first_hat * gain_one).astype(BF16)
    second_hat, second_inverse = norm_stats(flat_ref[1].astype(F32))
    second_norm = (second_hat * gain_two).astype(BF16)
    attended = [
        (turned_ref[window, 0], turned_ref[window, 1], flat_ref[2, window * WIN : (window + 1) * WIN])
        for window in range(2)
    ]
    mixed = [turned_ref[0, 2], turned_ref[1, 2]]
    rows_out[...] = backward(
        grad, active_ref[...], slope_ref[...].astype(F32), second_hat, second_inverse, second_norm, mixed,
        attended, weights_ref, first_hat, first_inverse, first_norm, gain_one, gain_two, in_weight,
        out_weight, up_weight, down_weight, scaled_ref, packed_ref,
    )
    write_halves(upper_ref, packed_ref, keep_ref, send_ref)


def grids_kernel(quad_0, quad_1, quad_2, quad_3, grad_rows_ref, blocks_out, grad_out, rows_ref):
    quads = [quad[:QUAD].astype(F32) for quad in (quad_0, quad_1, quad_2, quad_3)]
    blocks = mm(places(row_of_quad(0)), jnp.concatenate(quads, axis=0).astype(BF16))
    store_grid(blocks, rows_ref, blocks_out)
    store_grid(grad_rows_ref[...].astype(F32), rows_ref, grad_out)


SMEM = pl.BlockSpec(memory_space=pltpu.SMEM)
VMEM = pl.BlockSpec(memory_space=pltpu.VMEM)
ANY = pl.BlockSpec(memory_space=pl.ANY)
FAR_LIMIT = 60 * 1024 * 1024
NEAR_LIMIT = 28 * 1024 * 1024


class Part:
    def __init__(self, array, block):
        self.array, self.block = array, block
        self.lead = sum(size == 1 for size in array.shape[1:]) + 1
        self.shape, self.dtype = array.shape[self.lead :], array.dtype

    def spec(self):
        return pl.BlockSpec(
            (None,) * self.lead + self.shape, lambda *_: (self.block,) + (0,) * (self.lead - 1 + len(self.shape))
        )

    def of(self, ref):
        return ref.at[(self.block,) + (0,) * (self.lead - 1)]


class Near:
    def __init__(self, array):
        self.array = array


def whole(array):
    return pl.BlockSpec(array.shape, lambda *_: (0,) * len(array.shape))


def call(kernel, scalars, operands, out_shapes, scratch, flops):
    specs = [operand.spec() if isinstance(operand, Part) else whole(operand) for operand in operands]
    arrays = [operand.array if isinstance(operand, Part) else operand for operand in operands]
    return pl.pallas_call(
        kernel,
        grid=(1,),
        in_specs=[SMEM] * len(scalars) + specs,
        out_specs=[whole(shape) for shape in out_shapes],
        out_shape=out_shapes,
        scratch_shapes=scratch,
        compiler_params=pltpu.CompilerParams(vmem_limit_bytes=FAR_LIMIT),
        cost_estimate=pl.CostEstimate(flops=flops, bytes_accessed=4_000_000, transcendentals=1_000_000),
    )(*scalars, *arrays)


def near_call(kernel, scalars, operands, out_shapes, scratch, flops, near_outs=(), carried=()):
    def is_near(operand):
        return isinstance(operand, Near)

    def plain_array(operand):
        return operand.array if isinstance(operand, (Near, Part)) else operand

    def source_of(operand, ref):
        return operand.of(ref) if isinstance(operand, Part) else ref

    far = [operand for operand in operands if not is_near(operand)]
    far_outs = [shape for place, shape in enumerate(out_shapes) if place not in near_outs]

    def body(*refs):
        refs = list(refs)

        def take(count):
            taken = refs[:count]
            del refs[:count]
            return taken

        scalar_refs, operand_refs, carried_refs = take(len(scalars)), take(len(operands)), take(len(carried))
        out_refs, carried_outs = take(len(out_shapes)), take(len(carried))
        scratch_refs, buffers, out_buffers = take(len(scratch)), take(len(far)), take(len(far_outs))
        sems, carried_sems, out_sems = refs
        inputs, arriving = [], []
        for operand, ref in zip(operands, operand_refs, strict=True):
            if is_near(operand):
                inputs.append(ref)
                continue
            place = len(arriving)
            arriving.append(pltpu.make_async_copy(source_of(operand, ref), buffers[place], sems.at[place]))
            inputs.append(buffers[place])
        for copy in arriving:
            copy.start()
        passing = [
            pltpu.make_async_copy(source_of(operand, ref), target, carried_sems.at[place])
            for place, (operand, ref, target) in enumerate(zip(carried, carried_refs, carried_outs, strict=True))
        ]
        for copy in passing:
            copy.start()
        for copy in arriving:
            copy.wait()
        outputs, leaving = [], []
        for place, ref in enumerate(out_refs):
            if place in near_outs:
                outputs.append(ref)
                continue
            outputs.append(out_buffers[len(leaving)])
            leaving.append(pltpu.make_async_copy(outputs[-1], ref, out_sems.at[len(leaving)]))
        kernel(*scalar_refs, *inputs, *outputs, *scratch_refs)
        for copy in leaving:
            copy.start()
        for copy in passing + leaving:
            copy.wait()

    return pl.pallas_call(
        body,
        in_specs=[SMEM] * len(scalars)
        + [VMEM if is_near(operand) else ANY for operand in operands]
        + [ANY] * len(carried),
        out_specs=[VMEM if place in near_outs else ANY for place in range(len(out_shapes))] + [VMEM] * len(carried),
        out_shape=[*out_shapes, *[shape_of(operand.shape, operand.dtype) for operand in carried]],
        scratch_shapes=[
            *scratch,
            *[pltpu.VMEM(operand.shape, operand.dtype) for operand in far],
            *[pltpu.VMEM(shape.shape, shape.dtype) for shape in far_outs],
            pltpu.SemaphoreType.DMA((max(len(far), 1),)),
            pltpu.SemaphoreType.DMA((max(len(carried), 1),)),
            pltpu.SemaphoreType.DMA((max(len(far_outs), 1),)),
        ],
        compiler_params=pltpu.CompilerParams(vmem_limit_bytes=NEAR_LIMIT),
        cost_estimate=pl.CostEstimate(flops=flops, bytes_accessed=4_000_000, transcendentals=1_000_000),
    )(*scalars, *[plain_array(operand) for operand in operands], *[plain_array(operand) for operand in carried])


def shape_of(shape, dtype):
    return jax.ShapeDtypeStruct(shape, dtype)


def shifted(value, lat_steps, lon_steps):
    lon_count, lat_count = lax.axis_size("lon"), lax.axis_size("lat")
    pairs = []
    for lon in range(lon_count):
        for lat in range(lat_count):
            source = ((lon + lon_steps) % lon_count) * lat_count + (lat + lat_steps) % lat_count
            pairs.append((source, lon * lat_count + lat))
    return lax.ppermute(value, ("lon", "lat"), pairs)


def per_device(
    inputs,
    grad_out,
    region,
    bias_level,
    norm_gains,
    in_weight,
    out_weight,
    up_weight,
    down_weight,
    bias_tables,
):
    weights = (norm_gains, in_weight, out_weight, up_weight, down_weight.transpose(0, 2, 1))
    first_weights = [Part(array, 0) for array in weights]
    second_weights = [Part(array, 1) for array in weights]
    inputs, grad_out = inputs.transpose(1, 2, 0, 3), grad_out.transpose(1, 2, 0, 3)
    bias_tables = bias_tables.transpose(0, 1, 3, 2, 4)
    bias_level = bias_level.T
    is_upper = odd(core_step()[1]).reshape(1)

    quad_shape = shape_of((2 * QUAD, C), BF16)
    grid_shape = shape_of((6, 12, 4, C), BF16)
    half_shape = shape_of((ROWS // 2, 128), BF16)
    table_shape = shape_of((TABLE_ROWS, 128), BF16)
    weights_shape = (2 * HEADS, WIN, WIN)
    grads_scratch = pltpu.VMEM((2, 2 * HEADS * WIN, 128), F32)
    row_scratch = pltpu.VMEM((16, 26 * 128), F32)
    shaped_scratch = pltpu.VMEM((4, 2 * 72 + 16, 128), F32)
    bias_scratch = pltpu.VMEM((2, 2 * HEADS * WIN, 128), F32)
    rows_scratch = pltpu.VMEM((2, TOKENS, 128), F32)
    packed_scratch = pltpu.VMEM((ROWS, 128), BF16)

    quads = call(
        first_kernel,
        (bias_level,),
        (inputs, grad_out, *first_weights, Part(bias_tables, 0)),
        [quad_shape] * 4
        + [
            shape_of(weights_shape, BF16),
            shape_of((2, 3, C, WIN), BF16),
            shape_of((3, TOKENS, C), BF16),
        ],
        [rows_scratch, row_scratch, shaped_scratch, bias_scratch],
        1_000_000_000,
    )
    stored = list(quads[4:])
    ahead = (
        quads[3],
        shifted(quads[2], 0, 1),
        shifted(quads[1], 1, 0),
        shifted(quads[0], 1, 1),
    )
    (bias,) = call(
        prepare_kernel,
        (bias_level,),
        (region.transpose(1, 0, 2), Part(bias_tables, 1)),
        [shape_of(weights_shape, BF16)],
        [row_scratch, shaped_scratch, bias_scratch],
        500_000_000,
    )
    *back, second_keep, second_send, second_scaled = call(
        second_kernel,
        (is_upper,),
        (*ahead, bias, *second_weights),
        [quad_shape] * 4 + [half_shape, half_shape, shape_of(weights_shape, BF16)],
        [pltpu.VMEM(weights_shape, BF16), packed_scratch],
        3_000_000_000,
    )
    home = [
        shifted(back[3], -1, -1),
        shifted(back[2], -1, 0),
        shifted(back[1], 0, -1),
        back[0],
    ]
    home[3], after_second = tie((home[3], is_upper))
    active, slope, *first_near = near_call(
        activation_kernel,
        (after_second,),
        (stored[2], first_weights[0], first_weights[3]),
        [shape_of((TOKENS, FFN), BF16), shape_of((TOKENS, FFN), BF16)],
        [],
        300_000_000,
        (0, 1),
        (*stored, first_weights[0], *first_weights[2:]),
    )
    second_got = exchanged(second_send, core_step()[0])
    first_keep, first_send, grad_rows, first_scaled = near_call(
        third_kernel,
        (is_upper,),
        tuple(map(Near, (*home, *first_near[:3], active, slope, first_near[3], in_weight, *first_near[4:]))),
        [half_shape, half_shape, shape_of((TOKENS, C), BF16), shape_of(weights_shape, BF16)],
        [packed_scratch],
        2_000_000_000,
    )
    blocks_out, grad_inputs = near_call(
        grids_kernel,
        (),
        (*home, grad_rows),
        [grid_shape, grid_shape],
        [rows_scratch],
        100_000_000,
    )

    def collect(kernel, rows, *operands):
        return near_call(
            kernel,
            (bias_level,),
            operands,
            [shape_of((rows, 128), BF16)],
            [row_scratch, shaped_scratch, grads_scratch],
            500_000_000,
        )[0]

    first_got = exchanged(first_send, core_step()[0])
    second = added(second_keep, second_got)
    first = added(first_keep, first_got)
    first, second, first_scaled, second_scaled = tie((first, second, first_scaled, second_scaled))
    second_tables = collect(collect_kernel, TABLE_ROWS, second_scaled)
    tables = collect(finish_kernel, 2 * TABLE_ROWS, first_scaled, second_tables)
    totals = unpack(is_upper, *sum_all(first, second, tables, second_tables))
    gains, grad_in, grad_out_weight, grad_up, grad_down, grad_tables = totals
    return (
        blocks_out.transpose(2, 0, 1, 3),
        grad_inputs.transpose(2, 0, 1, 3),
        gains,
        grad_in,
        grad_out_weight,
        grad_up,
        grad_down.transpose(0, 2, 1),
        grad_tables.transpose(0, 1, 3, 2, 4),
    )


def exchanged(value, mask):
    lon_count, lat_count = lax.axis_size("lon"), lax.axis_size("lat")
    pairs = []
    for lon in range(lon_count):
        for lat in range(lat_count):
            pairs.append(((lon ^ mask[1]) * lat_count + (lat ^ mask[0]), lon * lat_count + lat))
    return lax.ppermute(value, ("lon", "lat"), pairs)


def added(left, right):
    return (left.astype(F32) + right.astype(F32)).astype(BF16)


def odd(mask):
    lat, lon = lax.axis_index("lat") & mask[0], lax.axis_index("lon") & mask[1]
    parity = jnp.int32(0)
    for place in range(5):
        parity = parity ^ (lat >> place) ^ (lon >> place)
    return parity & 1


def split(value, owner):
    half = value.shape[0] // 2
    up = odd(owner) != 0
    return jnp.where(up, value[half:], value[:half]), jnp.where(up, value[:half], value[half:])


def halve(value, mask, owner):
    keep, send = split(value, owner)
    return added(keep, exchanged(send, mask))


def double(value, mask, owner):
    other = exchanged(value, mask)
    up = odd(owner) != 0
    return jnp.concatenate([jnp.where(up, other, value), jnp.where(up, value, other)], axis=0)


def tie(values):
    return lax.optimization_barrier(values)


def core_step():
    return (1, 0), (1, 0)


def sum_all(first, second, tables, second_tables):
    core = core_step()[0]
    if lax.axis_size("lat") != 16 or lax.axis_size("lon") != 16:
        return sum_small(first, second, tables)
    y_low, y_high = ((2, 0), (2, 0)), (0, 8)
    x_low, x_high = ((4, 0), (12, 0)), ((12, 0), (8, 0))
    z_low, z_mid, z_high = ((0, 1), (0, 5)), ((0, 2), (0, 6)), (0, 7)

    first, second = halve(first, *y_low), halve(second, *x_low)
    first, second_tables = tie((first, second_tables))
    first, second = halve(first, *x_low), halve(second, *y_low)
    rows = first.shape[0]
    joined = halve(jnp.concatenate([first, second], axis=0), *x_high)
    joined, tables = tie((joined, tables))
    for mask, owner in (z_low, z_mid):
        keep, send = split(tables, owner)
        got = exchanged(jnp.concatenate([joined, send], axis=0), mask)
        joined, tables = added(joined, got[:rows]), added(keep, got[rows:])
    joined = jnp.concatenate([joined, tables], axis=0)
    for mask in (z_high, y_high):
        joined = added(joined, exchanged(joined, mask))
    joined, tables = tie((joined[:rows], joined[rows:]))
    tables = double(tables, *z_mid)
    joined = double(joined, *x_high)
    first, second = tie((joined[:rows], joined[rows:]))
    first, second = double(first, *x_low), double(second, *y_low)
    first, tables = tie((first, tables))
    first, second = double(first, *y_low), double(second, *x_low)
    tables = double(tables, *z_low)
    first, second, tables = tie((first, second, tables))
    return first, exchanged(first, core), second, exchanged(second, core), tables


def sum_small(first, second, tables):
    def over(value, axis):
        for place in range(lax.axis_size(axis).bit_length() - 1):
            if axis == "lon" or place:
                value = added(value, exchanged(value, (1 << place, 0) if axis == "lat" else (0, 1 << place)))
        return value

    core = core_step()[0]
    first, second = over(over(first, "lat"), "lon"), over(over(second, "lat"), "lon")
    return first, exchanged(first, core), second, exchanged(second, core), over(tables, "lon")


def unpack_kernel(upper_ref, first_own, first_other, second_own, second_other, tables_ref, *refs):
    results, (rows_ref, *buffers, sems) = refs[:6], refs[6:]
    gains_ref, in_ref, out_ref, up_ref, down_ref, grads_ref = buffers
    half = ROWS // 2
    is_upper = jnp.broadcast_to(upper_ref[0] == 1, (1, 128))
    copies = []

    def leave(index, block):
        copy = pltpu.make_async_copy(buffers[index].at[block], results[index].at[block], sems.at[index, block])
        copy.start()
        copies.append(copy)

    for block, (own, other) in enumerate(((first_own, first_other), (second_own, second_other))):

        def rows(start, stop, own=own, other=other):
            if start < half < stop:
                return jnp.concatenate([rows(start, half), rows(half, stop)], axis=0)
            lower = start < half
            start, stop = (start, stop) if lower else (start - half, stop - half)
            mine, theirs = own[start:stop].astype(F32), other[start:stop].astype(F32)
            return jnp.where(is_upper, theirs, mine) if lower else jnp.where(is_upper, mine, theirs)

        for index, (ref, start) in enumerate(((up_ref, 1152), (down_ref, 2304))):
            for part in range(6):
                lanes = slice(part * 128, (part + 1) * 128)
                ref[block, :, lanes] = rows(start + part * C, start + (part + 1) * C)
            leave(3 + index, block)
        for part in range(4):
            in_ref[block, :, part * 128 : (part + 1) * 128] = rows(part * C, (part + 1) * C)
        shared = rows(768, 960)
        in_ref[block, :, 512:] = shared[:, :64]
        leave(1, block)
        out_ref[block, :, :128] = rows(960, 1152)
        out_ref[block, :, 128:] = shared[:, 64:]
        leave(2, block)
        rows_ref[...] = tables_ref[block * TABLE_ROWS : (block + 1) * TABLE_ROWS].astype(F32)
        for slab in range(26):
            width = min(128, RELPOS - slab * 128)
            for level in range(2):
                start = slab * 12 + level * HEADS
                grads_ref[block, 0, :, level, slab * 128 : slab * 128 + width] = rows_ref[start : start + HEADS, :width]
        leave(5, block)
        gains = rows(GAIN_ROWS, GAIN_ROWS + 16)
        gains_ref[block, 0:1, :128] = gains[0:1]
        gains_ref[block, 0:1, 128:] = gains[1:2, :64]
        gains_ref[block, 1:2, :128] = gains[2:3]
        gains_ref[block, 1:2, 128:] = gains[1:2, 64:]
        leave(0, block)
    for copy in copies:
        copy.wait()


def unpack(is_upper, *values):
    shapes = [
        (2, 2, C),
        (2, C, 3 * C),
        (2, C, C),
        (2, C, FFN),
        (2, C, FFN),
        (2, 1, HEADS, 2, RELPOS),
    ]
    return pl.pallas_call(
        unpack_kernel,
        in_specs=[SMEM] + [pl.BlockSpec(memory_space=pltpu.VMEM)] * len(values),
        out_specs=[pl.BlockSpec(memory_space=pl.ANY)] * len(shapes),
        out_shape=[shape_of(shape, F32) for shape in shapes],
        scratch_shapes=[pltpu.VMEM((TABLE_ROWS, 128), F32)]
        + [pltpu.VMEM(shape, F32) for shape in shapes]
        + [pltpu.SemaphoreType.DMA((len(shapes), 2))],
        compiler_params=pltpu.CompilerParams(vmem_limit_bytes=NEAR_LIMIT),
    )(is_upper, *values)


def solution(mesh):
    placed = (
        P(None, "lat", "lon", None),
        P(None, "lat", "lon", None),
        P(None, "lat", "lon"),
        P(None, "lat"),
        P(),
        P(),
        P(),
        P(),
        P(),
        P(None, "lat", None, None, None),
    )
    return jax.shard_map(
        per_device,
        mesh=mesh,
        in_specs=placed,
        out_specs=(
            P(None, "lat", "lon", None),
            P(None, "lat", "lon", None),
            P(),
            P(),
            P(),
            P(),
            P(),
            P(None, "lat", None, None, None),
        ),
        check_vma=False,
    )
```

```python
import functools
import math

import jax
import jax.numpy as jnp
from jax import lax
from jax.experimental import pallas as pl
from jax.experimental.pallas import tpu as pltpu
from jax.sharding import PartitionSpec as P

C = 192
HEADS = 6
HEAD = 32
FFN = 768
WIN_Z = 2
WIN_LAT = 6
WIN_LON = 12
WIN = 144
TOKENS = 2 * WIN
QUAD = 72
RELPOS = 3312
SPAN = 2 * WIN_LON - 1
ROWS = 3520
GAIN_ROWS = 3456
TABLE_ROWS = 320

EPSILON = 1e-05
NEGATIVE = -1000000000.0
SCALE = 1.0 / math.sqrt(HEAD)

F32 = jnp.float32
BF16 = jnp.bfloat16


def mm(left, right):
    return lax.dot_general(left, right, (((1,), (0,)), ((), ())), preferred_element_type=F32)


def mm_nt(left, right):
    return lax.dot_general(left, right, (((1,), (1,)), ((), ())), preferred_element_type=F32)


def eye(size):
    return (
        lax.broadcasted_iota(jnp.int32, (size, size), 0) == lax.broadcasted_iota(jnp.int32, (size, size), 1)
    ).astype(F32).astype(BF16)


def divided(value, divisor, count):
    quotient = jnp.zeros_like(value)
    for number in range(1, count):
        quotient = quotient + (value >= number * divisor).astype(jnp.int32)
    return quotient, value - quotient * divisor


def lanes_of_tokens():
    return lax.broadcasted_iota(jnp.int32, (1, TOKENS), 1)


def row_of_quad(roll):
    lat_half, rest = divided(lanes_of_tokens(), 2 * QUAD, 2)
    lon_half, rest = divided(rest, QUAD, 2)
    level, rest = divided(rest, 18, 4)
    row, col = divided(rest, 6, 3)
    level = (level + 4 - roll) & 3
    return (level * 6 + lat_half * 3 + row) * 12 + lon_half * 6 + col


def quad_of_row(roll):
    level, rest = divided(lanes_of_tokens(), QUAD, 4)
    row, col = divided(rest, 12, 6)
    lat_half, row = divided(row, 3, 2)
    lon_half, col = divided(col, 6, 2)
    level = (level + roll) & 3
    return lat_half * 2 * QUAD + lon_half * QUAD + level * 18 + row * 6 + col


def places(rows):
    return (lax.broadcasted_iota(jnp.int32, (TOKENS, TOKENS), 0) == rows).astype(F32).astype(BF16)


def turned(value):
    return mm_nt(eye(value.shape[1]), value).astype(BF16)


def norm_stats(values):
    centre = values - jnp.mean(values, axis=-1, keepdims=True)
    inverse = lax.rsqrt(jnp.mean(centre * centre, axis=-1, keepdims=True) + EPSILON)
    return centre * inverse, inverse


def norm_backward(upstream, normal_hat, inverse):
    upstream_mean = jnp.mean(upstream, axis=-1, keepdims=True)
    cross_mean = jnp.mean(upstream * normal_hat, axis=-1, keepdims=True)
    return inverse * (upstream - upstream_mean - normal_hat * cross_mean)


def head_lanes(head):
    lane = lax.broadcasted_iota(jnp.int32, (1, C), 1)
    return ((lane >= head * HEAD) & (lane < (head + 1) * HEAD)).astype(F32).astype(BF16)


def pair_keys():
    row = lax.broadcasted_iota(jnp.int32, (512, 1), 0)
    within = row & 127
    third = (within >= SPAN).astype(jnp.int32) + (within >= 2 * SPAN).astype(jnp.int32)
    row_group = (row >> 7) * 3 + third
    row_offset = within - third * SPAN
    col = lax.broadcasted_iota(jnp.int32, (1, 256), 1)
    col_group = jnp.zeros_like(col)
    for group in range(1, 12):
        col_group = col_group + (col >= group * 12).astype(jnp.int32)
    col_place = col - col_group * 12
    usable = (row_group == col_group) & (within < 3 * SPAN) & (col < WIN)
    return jnp.where(usable, col_place + 11 - row_offset, -1).astype(F32).astype(BF16)


def pairs_of(keys, place):
    return jnp.where(keys == jnp.asarray(place, BF16), jnp.asarray(1, BF16), jnp.asarray(0, BF16))


def table_start(zs, zt, hs, ht):
    return (((zs * 2 + zt) * 6 + hs) * 6 + ht) * SPAN


def spread_bias(table_ref, row_ref, shaped_ref, bias_ref):
    for head in range(HEADS):
        row_ref[head * 2 : head * 2 + 2, :RELPOS] = table_ref[head].astype(F32)
    row = row_ref[: 2 * HEADS]
    for zs in range(2):
        for zt in range(2):
            for group in range(2):
                for ht in range(6):
                    pieces = []
                    for hs in range(group * 3, group * 3 + 3):
                        start = table_start(zs, zt, hs, ht)
                        pieces.append(row[:, start : start + SPAN])
                    pieces.append(jnp.zeros((2 * HEADS, 128 - 3 * SPAN), F32))
                    target = pl.ds(zt * 6 + ht, 2 * HEADS, stride=12)
                    shaped_ref[zs * 2 + group, target, :] = jnp.concatenate(pieces, axis=1)
    keys = pair_keys()
    shaped = jnp.concatenate([shaped_ref[part, :WIN].astype(BF16) for part in range(4)], axis=1)
    for col in range(WIN_LON):
        spread = mm(shaped, pairs_of(keys, col))
        bias_ref[0, pl.ds(col, WIN, stride=12), :] = spread[:, :128]
        bias_ref[1, pl.ds(col, WIN, stride=12), :] = spread[:, 128:]


def collect_bias(scaled_ref, levels, row_ref, shaped_ref, grads_ref, out_ref):
    for place in range(2 * HEADS):
        rows = slice(place * WIN, (place + 1) * WIN)
        piece = scaled_ref[place].astype(F32)
        grads_ref[0, rows] = piece[:, :128]
        grads_ref[1, rows] = jnp.concatenate([piece[:, 128:], jnp.zeros((WIN, 256 - WIN), F32)], axis=1)
    keys = pair_keys()
    total = jnp.zeros((WIN, 512), F32)
    for col in range(WIN_LON):
        left = grads_ref[0, pl.ds(col, WIN, stride=12), :]
        right = grads_ref[1, pl.ds(col, WIN, stride=12), :]
        piece = jnp.concatenate([left, right], axis=1).astype(BF16)
        total = total + mm_nt(piece, pairs_of(keys, col))
    total = total * (1.0 / SCALE)
    for part in range(4):
        shaped_ref[part, :WIN] = total[:, part * 128 : (part + 1) * 128]
    row_ref[...] = jnp.zeros_like(row_ref)
    for zs in range(2):
        for zt in range(2):
            for group in range(2):
                for ht in range(6):
                    pieces = [
                        shaped_ref[zs * 2 + group, pl.ds(window * 72 + zt * 6 + ht, HEADS, stride=12), :]
                        for window in range(2)
                    ]
                    for level in range(2):
                        chosen = jnp.zeros((HEADS, 128), F32)
                        for window in range(2):
                            chosen = chosen + jnp.where(levels[window] == level, pieces[window], 0.0)
                        for index in range(3):
                            start = table_start(zs, zt, group * 3 + index, ht)
                            row_ref[level * 8 : level * 8 + HEADS, start : start + SPAN] = chosen[
                                :, index * SPAN : (index + 1) * SPAN
                            ]
    for slab in range(26):
        lanes = slice(slab * 128, (slab + 1) * 128)
        rows = jnp.concatenate([row_ref[:HEADS, lanes], row_ref[8 : 8 + HEADS, lanes]], axis=0)
        shaped_ref[slab // 13, slab % 13 * 12 : slab % 13 * 12 + 12] = rows
    out_ref[...] = jnp.concatenate(
        [shaped_ref[0, :156], shaped_ref[1, :156], jnp.zeros((TABLE_ROWS - 312, 128), F32)], axis=0
    ).astype(BF16)


def load_tiles(bias_ref, level, head):
    rows = pl.ds(pl.multiple_of((head * 2 + level) * WIN, 8), WIN)
    return jnp.concatenate([bias_ref[0, rows, :], bias_ref[1, rows, : WIN - 128]], axis=1)


def attention(normed, in_weight, bias_of, weights_ref):
    eye_c = eye(C)
    weight_q, weight_k, weight_v = in_weight[:, :C], in_weight[:, C : 2 * C], in_weight[:, 2 * C :]
    kept = []
    mixed = []
    for window in range(2):
        rows = normed[window * WIN : (window + 1) * WIN]
        keys = mm(rows, weight_k).astype(BF16)
        values = mm(rows, weight_v).astype(BF16)
        queries = mm(rows, weight_q).astype(BF16)
        queries_t = mm_nt(eye_c, queries).astype(BF16)
        keys_t = mm_nt(eye_c, keys).astype(BF16)
        values_t = mm_nt(eye_c, values).astype(BF16)
        parts = []
        for head in range(HEADS):
            own = keys * head_lanes(head)
            scores = mm(own, queries_t) * SCALE + bias_of(window, head)
            weights = jnp.exp(scores - jnp.max(scores, axis=0, keepdims=True))
            weights = weights * (1.0 / jnp.sum(weights, axis=0, keepdims=True))
            weights = weights.astype(BF16)
            weights_ref[window * HEADS + head] = weights
            parts.append(mm(values_t[head * HEAD : (head + 1) * HEAD], weights))
        mixed.append(jnp.concatenate(parts, axis=0).astype(BF16))
        kept.append((queries_t, keys_t, values))
    return kept, mixed


def feed_forward(hidden, gain, up_weight):
    hat, inverse = norm_stats(hidden)
    normed = (hat * gain).astype(BF16)
    return hat, inverse, normed, mm(normed, up_weight)


def gelu_parts(expanded):
    cumulative = 0.5 * (1.0 + lax.erf(expanded * (1.0 / math.sqrt(2.0))))
    slope = cumulative + expanded * jnp.exp(-0.5 * expanded * expanded) * (1.0 / math.sqrt(2.0 * math.pi))
    return (expanded * cumulative).astype(BF16), slope


def natural_mixed(mixed):
    eye_w = eye(WIN)
    return jnp.concatenate([mm_nt(eye_w, part) for part in mixed], axis=0).astype(BF16)


def pack(packed_ref, start, value):
    height = value.shape[0]
    for part in range(value.shape[1] // 128):
        rows = slice(start + part * height, start + (part + 1) * height)
        packed_ref[rows] = value[:, part * 128 : (part + 1) * 128].astype(BF16)


def backward(
    grad,
    active,
    slope,
    second_hat,
    second_inverse,
    second_norm,
    mixed,
    attended,
    weights_ref,
    first_hat,
    first_inverse,
    first_norm,
    gain_one,
    gain_two,
    in_weight,
    out_weight,
    up_weight,
    down_weight,
    scaled_ref,
    packed_ref,
):
    eye_c = eye(C)
    grad_half = grad.astype(BF16)
    pack(packed_ref, 2304, mm(turned(grad_half), active))
    grad_expanded = (mm(grad_half, down_weight) * slope).astype(BF16)
    normed_t = turned(second_norm)
    pack(packed_ref, 1152, mm(normed_t, grad_expanded))
    grad_second = mm_nt(grad_expanded, up_weight)
    gain_two_grad = jnp.sum(grad_second * second_hat, axis=0, keepdims=True)
    grad_hidden = (grad + norm_backward(grad_second * gain_two, second_hat, second_inverse)).astype(BF16)
    grad_out = mm(mixed[0], grad_hidden[:WIN]) + mm(mixed[1], grad_hidden[WIN:])
    packed_ref[960:1152] = grad_out[:, :128].astype(BF16)
    grad_mixed = mm_nt(grad_hidden, out_weight).astype(BF16)
    projected = []
    for window in range(2):
        queries_t, keys_t, values = attended[window]
        upstream_t = mm_nt(eye_c, grad_mixed[window * WIN : (window + 1) * WIN]).astype(BF16)
        grad_q, grad_k, grad_v = [], [], []
        for head in range(HEADS):
            lanes = slice(head * HEAD, (head + 1) * HEAD)
            half = weights_ref[window * HEADS + head]
            weights = half.astype(F32)
            own = values * head_lanes(head)
            grad_weights = mm(own, upstream_t)
            inner = jnp.sum(grad_weights * weights, axis=0, keepdims=True)
            grad_scores = weights * (grad_weights - inner)
            scaled = (grad_scores * SCALE).astype(BF16)
            scaled_ref[window * HEADS + head] = scaled
            grad_v.append(mm_nt(upstream_t[lanes], half))
            grad_q.append(mm(keys_t[lanes], scaled))
            grad_k.append(mm_nt(queries_t[lanes], scaled))
        projected_t = jnp.concatenate(grad_q + grad_k + grad_v, axis=0).astype(BF16)
        projected.append(mm_nt(eye(WIN), projected_t))
    projected = jnp.concatenate(projected, axis=0).astype(BF16)
    first_t = turned(first_norm)
    grad_in = mm(first_t, projected)
    pack(packed_ref, 0, grad_in[:, :512])
    packed_ref[768:960] = jnp.concatenate([grad_in[:, 512:], grad_out[:, 128:]], axis=1).astype(BF16)
    grad_first = mm_nt(projected, in_weight)
    gain_one_grad = jnp.sum(grad_first * first_hat, axis=0, keepdims=True)
    gain_rows = jnp.concatenate(
        [
            gain_one_grad[:, :128],
            jnp.concatenate([gain_one_grad[:, 128:], gain_two_grad[:, 128:]], axis=1),
            gain_two_grad[:, :128],
            jnp.zeros((ROWS - GAIN_ROWS - 3, 128), F32),
        ],
        axis=0,
    )
    packed_ref[GAIN_ROWS:ROWS] = gain_rows.astype(BF16)
    return (
        grad_hidden.astype(F32) + norm_backward(grad_first * gain_one, first_hat, first_inverse)
    ).astype(BF16)


def load_grid(grid_ref, rows_ref):
    for row in range(6):
        for col in range(12):
            piece = grid_ref[row, col].astype(F32)
            target = pl.ds(row * 12 + col, 4, stride=72)
            rows_ref[0, target, :] = piece[:, :128]
            rows_ref[1, target, :] = jnp.concatenate([piece[:, 128:], jnp.zeros((4, 64), F32)], axis=1)
    return jnp.concatenate([rows_ref[0], rows_ref[1][:, :64]], axis=1)


def store_grid(rows, rows_ref, grid_ref):
    rows_ref[0] = rows[:, :128]
    rows_ref[1] = jnp.concatenate([rows[:, 128:], jnp.zeros((TOKENS, 64), F32)], axis=1)
    for row in range(6):
        for col in range(12):
            source = pl.ds(row * 12 + col, 4, stride=72)
            piece = jnp.concatenate([rows_ref[0, source, :], rows_ref[1, source, :][:, :64]], axis=1)
            grid_ref[row, col] = piece.astype(BF16)


def block_weights(gains_ref, in_ref, out_ref, up_ref, down_ref):
    gains = gains_ref[...]
    return gains[0:1], gains[1:2], in_ref[...], out_ref[...], up_ref[...], down_ref[...]


def write_halves(upper_ref, packed_ref, keep_ref, send_ref):
    half = ROWS // 2
    is_upper = upper_ref[0] == 1

    @pl.when(is_upper)
    def _():
        keep_ref[...] = packed_ref[half:]
        send_ref[...] = packed_ref[:half]

    @pl.when(jnp.logical_not(is_upper))
    def _():
        keep_ref[...] = packed_ref[:half]
        send_ref[...] = packed_ref[half:]


def first_kernel(
    levels_ref,
    inputs_ref,
    grad_ref,
    gains_ref,
    in_ref,
    out_ref,
    up_ref,
    down_ref,
    table_ref,
    quad_0,
    quad_1,
    quad_2,
    quad_3,
    weights_out,
    turned_out,
    flat_out,
    rows_ref,
    row_ref,
    shaped_ref,
    bias_ref,
):
    levels = [levels_ref[0, 0], levels_ref[0, 1]]
    gain_one, gain_two, in_weight, out_weight, up_weight, down_weight = block_weights(
        gains_ref, in_ref, out_ref, up_ref, down_ref
    )
    order = places(quad_of_row(0))
    grad_quads = mm(order, load_grid(grad_ref, rows_ref).astype(BF16))
    flat = load_grid(inputs_ref, rows_ref)
    flat_out[0] = flat.astype(BF16)
    spread_bias(table_ref, row_ref, shaped_ref, bias_ref)
    hat, _ = norm_stats(flat)
    normed = (hat * gain_one).astype(BF16)
    attended, mixed = attention(
        normed, in_weight, lambda window, head: load_tiles(bias_ref, levels[window], head), weights_out
    )
    for window in range(2):
        turned_out[window, 0] = attended[window][0]
        turned_out[window, 1] = attended[window][1]
        turned_out[window, 2] = mixed[window]
        flat_out[2, window * WIN : (window + 1) * WIN] = attended[window][2]
    hidden = (flat + mm(natural_mixed(mixed), out_weight)).astype(BF16)
    flat_out[1] = hidden
    hidden = hidden.astype(F32)
    _, _, _, expanded = feed_forward(hidden, gain_two, up_weight)
    active = (expanded * 0.5 * (1.0 + lax.erf(expanded * (1.0 / math.sqrt(2.0))))).astype(BF16)
    result = (hidden + mm_nt(active, down_weight)).astype(BF16)
    result_quads = mm(order, result)
    for index, quad in enumerate((quad_0, quad_1, quad_2, quad_3)):
        rows = slice(index * QUAD, (index + 1) * QUAD)
        quad[...] = jnp.concatenate([result_quads[rows], grad_quads[rows]], axis=0).astype(BF16)


def region_row(region_ref, window):
    pieces = [region_ref[row, window * 2 + level : window * 2 + level + 1, :] for level in range(2) for row in range(6)]
    return jnp.concatenate(pieces, axis=1)


def prepare_kernel(
    levels_ref, region_ref, table_ref, bias_out, row_ref, shaped_ref, bias_ref
):
    levels = [levels_ref[0, 0], levels_ref[0, 1]]
    spread_bias(table_ref, row_ref, shaped_ref, bias_ref)
    diagonal = lax.broadcasted_iota(jnp.int32, (WIN, WIN), 0) == lax.broadcasted_iota(jnp.int32, (WIN, WIN), 1)
    for window in range(2):
        across = region_row(region_ref, window).astype(F32)
        down = jnp.sum(jnp.where(diagonal, across, 0.0), axis=1, keepdims=True)
        same = across == down
        for head in range(HEADS):
            bias = jnp.where(same, load_tiles(bias_ref, levels[window], head), NEGATIVE)
            bias_out[window * HEADS + head] = bias.astype(BF16)


def second_kernel(
    upper_ref,
    quad_0,
    quad_1,
    quad_2,
    quad_3,
    bias_ref,
    gains_ref,
    in_ref,
    out_ref,
    up_ref,
    down_ref,
    back_0,
    back_1,
    back_2,
    back_3,
    keep_ref,
    send_ref,
    scaled_ref,
    weights_ref,
    packed_ref,
):
    quads = [quad[...].astype(F32) for quad in (quad_0, quad_1, quad_2, quad_3)]
    ahead = places(row_of_quad(1))
    flat = mm(ahead, jnp.concatenate([quad[:QUAD] for quad in quads], axis=0).astype(BF16))
    grad = mm(ahead, jnp.concatenate([quad[QUAD:] for quad in quads], axis=0).astype(BF16))
    gain_one, gain_two, in_weight, out_weight, up_weight, down_weight = block_weights(
        gains_ref, in_ref, out_ref, up_ref, down_ref
    )
    first_hat, first_inverse = norm_stats(flat)
    first_norm = (first_hat * gain_one).astype(BF16)
    attended, mixed = attention(
        first_norm, in_weight, lambda window, head: bias_ref[window * HEADS + head].astype(F32), weights_ref
    )
    hidden = (flat + mm(natural_mixed(mixed), out_weight)).astype(BF16).astype(F32)
    second_hat, second_inverse, second_norm, expanded = feed_forward(hidden, gain_two, up_weight)
    active, slope = gelu_parts(expanded)
    result = (hidden + mm_nt(active, down_weight)).astype(BF16)
    grad_in = backward(
        grad, active, slope, second_hat, second_inverse, second_norm, mixed, attended, weights_ref,
        first_hat, first_inverse, first_norm, gain_one, gain_two, in_weight, out_weight, up_weight,
        down_weight, scaled_ref, packed_ref,
    )
    back = places(quad_of_row(1))
    result_quads, grad_quads = mm(back, result), mm(back, grad_in)
    for index, quad in enumerate((back_0, back_1, back_2, back_3)):
        rows = slice(index * QUAD, (index + 1) * QUAD)
        quad[...] = jnp.concatenate([result_quads[rows], grad_quads[rows]], axis=0).astype(BF16)
    write_halves(upper_ref, packed_ref, keep_ref, send_ref)


def collect_kernel(levels_ref, scaled_ref, tables_out, row_ref, shaped_ref, grads_ref):
    levels = [levels_ref[0, 0], levels_ref[0, 1]]
    collect_bias(scaled_ref, levels, row_ref, shaped_ref, grads_ref, tables_out)


def finish_kernel(
    levels_ref, scaled_ref, second_tables_ref, tables_out, row_ref, shaped_ref, grads_ref
):
    levels = [levels_ref[0, 0], levels_ref[0, 1]]
    collect_bias(scaled_ref, levels, row_ref, shaped_ref, grads_ref, tables_out.at[:TABLE_ROWS])
    tables_out[TABLE_ROWS:] = second_tables_ref[...]


def activation_kernel(_, flat_ref, gains_ref, up_ref, active_out, slope_out):
    _, _, _, expanded = feed_forward(flat_ref[1].astype(F32), gains_ref[1:2], up_ref[...])
    active, slope = gelu_parts(expanded)
    active_out[...] = active
    slope_out[...] = slope.astype(BF16)


def third_kernel(
    upper_ref,
    quad_0,
    quad_1,
    quad_2,
    quad_3,
    weights_ref,
    turned_ref,
    flat_ref,
    active_ref,
    slope_ref,
    gains_ref,
    in_ref,
    out_ref,
    up_ref,
    down_ref,
    keep_ref,
    send_ref,
    rows_out,
    scaled_ref,
    packed_ref,
):
    quads = [quad[...].astype(F32) for quad in (quad_0, quad_1, quad_2, quad_3)]
    grad = mm(places(row_of_quad(0)), jnp.concatenate([quad[QUAD:] for quad in quads], axis=0).astype(BF16))
    gain_one, gain_two, in_weight, out_weight, up_weight, down_weight = block_weights(
        gains_ref, in_ref.at[0], out_ref, up_ref, down_ref
    )
    first_hat, first_inverse = norm_stats(flat_ref[0].astype(F32))
    first_norm = (first_hat * gain_one).astype(BF16)
    second_hat, second_inverse = norm_stats(flat_ref[1].astype(F32))
    second_norm = (second_hat * gain_two).astype(BF16)
    attended = [
        (turned_ref[window, 0], turned_ref[window, 1], flat_ref[2, window * WIN : (window + 1) * WIN])
        for window in range(2)
    ]
    mixed = [turned_ref[0, 2], turned_ref[1, 2]]
    rows_out[...] = backward(
        grad, active_ref[...], slope_ref[...].astype(F32), second_hat, second_inverse, second_norm, mixed,
        attended, weights_ref, first_hat, first_inverse, first_norm, gain_one, gain_two, in_weight,
        out_weight, up_weight, down_weight, scaled_ref, packed_ref,
    )
    write_halves(upper_ref, packed_ref, keep_ref, send_ref)


def grids_kernel(quad_0, quad_1, quad_2, quad_3, grad_rows_ref, blocks_out, grad_out, rows_ref):
    quads = [quad[:QUAD].astype(F32) for quad in (quad_0, quad_1, quad_2, quad_3)]
    blocks = mm(places(row_of_quad(0)), jnp.concatenate(quads, axis=0).astype(BF16))
    store_grid(blocks, rows_ref, blocks_out)
    store_grid(grad_rows_ref[...].astype(F32), rows_ref, grad_out)


SMEM = pl.BlockSpec(memory_space=pltpu.SMEM)
VMEM = pl.BlockSpec(memory_space=pltpu.VMEM)
ANY = pl.BlockSpec(memory_space=pl.ANY)
FAR_LIMIT = 60 * 1024 * 1024
NEAR_LIMIT = 28 * 1024 * 1024


class Part:
    def __init__(self, array, block):
        self.array, self.block = array, block
        self.lead = sum(size == 1 for size in array.shape[1:]) + 1
        self.shape, self.dtype = array.shape[self.lead :], array.dtype

    def spec(self):
        return pl.BlockSpec(
            (None,) * self.lead + self.shape, lambda *_: (self.block,) + (0,) * (self.lead - 1 + len(self.shape))
        )

    def of(self, ref):
        return ref.at[(self.block,) + (0,) * (self.lead - 1)]


class Near:
    def __init__(self, array):
        self.array = array


def whole(array):
    return pl.BlockSpec(array.shape, lambda *_: (0,) * len(array.shape))


def call(kernel, scalars, operands, out_shapes, scratch, flops):
    specs = [operand.spec() if isinstance(operand, Part) else whole(operand) for operand in operands]
    arrays = [operand.array if isinstance(operand, Part) else operand for operand in operands]
    return pl.pallas_call(
        kernel,
        grid=(1,),
        in_specs=[SMEM] * len(scalars) + specs,
        out_specs=[whole(shape) for shape in out_shapes],
        out_shape=out_shapes,
        scratch_shapes=scratch,
        compiler_params=pltpu.CompilerParams(vmem_limit_bytes=FAR_LIMIT),
        cost_estimate=pl.CostEstimate(flops=flops, bytes_accessed=4_000_000, transcendentals=1_000_000),
    )(*scalars, *arrays)


def near_call(kernel, scalars, operands, out_shapes, scratch, flops, near_outs=(), carried=()):
    def is_near(operand):
        return isinstance(operand, Near)

    def plain_array(operand):
        return operand.array if isinstance(operand, (Near, Part)) else operand

    def source_of(operand, ref):
        return operand.of(ref) if isinstance(operand, Part) else ref

    far = [operand for operand in operands if not is_near(operand)]
    far_outs = [shape for place, shape in enumerate(out_shapes) if place not in near_outs]

    def body(*refs):
        refs = list(refs)

        def take(count):
            taken = refs[:count]
            del refs[:count]
            return taken

        scalar_refs, operand_refs, carried_refs = take(len(scalars)), take(len(operands)), take(len(carried))
        out_refs, carried_outs = take(len(out_shapes)), take(len(carried))
        scratch_refs, buffers, out_buffers = take(len(scratch)), take(len(far)), take(len(far_outs))
        sems, carried_sems, out_sems = refs
        inputs, arriving = [], []
        for operand, ref in zip(operands, operand_refs, strict=True):
            if is_near(operand):
                inputs.append(ref)
                continue
            place = len(arriving)
            arriving.append(pltpu.make_async_copy(source_of(operand, ref), buffers[place], sems.at[place]))
            inputs.append(buffers[place])
        for copy in arriving:
            copy.start()
        passing = [
            pltpu.make_async_copy(source_of(operand, ref), target, carried_sems.at[place])
            for place, (operand, ref, target) in enumerate(zip(carried, carried_refs, carried_outs, strict=True))
        ]
        for copy in passing:
            copy.start()
        for copy in arriving:
            copy.wait()
        outputs, leaving = [], []
        for place, ref in enumerate(out_refs):
            if place in near_outs:
                outputs.append(ref)
                continue
            outputs.append(out_buffers[len(leaving)])
            leaving.append(pltpu.make_async_copy(outputs[-1], ref, out_sems.at[len(leaving)]))
        kernel(*scalar_refs, *inputs, *outputs, *scratch_refs)
        for copy in leaving:
            copy.start()
        for copy in passing + leaving:
            copy.wait()

    return pl.pallas_call(
        body,
        in_specs=[SMEM] * len(scalars)
        + [VMEM if is_near(operand) else ANY for operand in operands]
        + [ANY] * len(carried),
        out_specs=[VMEM if place in near_outs else ANY for place in range(len(out_shapes))] + [VMEM] * len(carried),
        out_shape=[*out_shapes, *[shape_of(operand.shape, operand.dtype) for operand in carried]],
        scratch_shapes=[
            *scratch,
            *[pltpu.VMEM(operand.shape, operand.dtype) for operand in far],
            *[pltpu.VMEM(shape.shape, shape.dtype) for shape in far_outs],
            pltpu.SemaphoreType.DMA((max(len(far), 1),)),
            pltpu.SemaphoreType.DMA((max(len(carried), 1),)),
            pltpu.SemaphoreType.DMA((max(len(far_outs), 1),)),
        ],
        compiler_params=pltpu.CompilerParams(vmem_limit_bytes=NEAR_LIMIT),
        cost_estimate=pl.CostEstimate(flops=flops, bytes_accessed=4_000_000, transcendentals=1_000_000),
    )(*scalars, *[plain_array(operand) for operand in operands], *[plain_array(operand) for operand in carried])


def shape_of(shape, dtype):
    return jax.ShapeDtypeStruct(shape, dtype)


def shifted(value, lat_steps, lon_steps):
    lon_count, lat_count = lax.axis_size("lon"), lax.axis_size("lat")
    pairs = []
    for lon in range(lon_count):
        for lat in range(lat_count):
            source = ((lon + lon_steps) % lon_count) * lat_count + (lat + lat_steps) % lat_count
            pairs.append((source, lon * lat_count + lat))
    return lax.ppermute(value, ("lon", "lat"), pairs)


def per_device(
    inputs,
    grad_out,
    region,
    bias_level,
    norm_gains,
    in_weight,
    out_weight,
    up_weight,
    down_weight,
    bias_tables,
):
    weights = (norm_gains, in_weight, out_weight, up_weight, down_weight.transpose(0, 2, 1))
    first_weights = [Part(array, 0) for array in weights]
    second_weights = [Part(array, 1) for array in weights]
    inputs, grad_out = inputs.transpose(1, 2, 0, 3), grad_out.transpose(1, 2, 0, 3)
    bias_tables = bias_tables.transpose(0, 1, 3, 2, 4)
    bias_level = bias_level.T
    is_upper = odd(core_step()[1]).reshape(1)

    quad_shape = shape_of((2 * QUAD, C), BF16)
    grid_shape = shape_of((6, 12, 4, C), BF16)
    half_shape = shape_of((ROWS // 2, 128), BF16)
    table_shape = shape_of((TABLE_ROWS, 128), BF16)
    weights_shape = (2 * HEADS, WIN, WIN)
    grads_scratch = pltpu.VMEM((2, 2 * HEADS * WIN, 128), F32)
    row_scratch = pltpu.VMEM((16, 26 * 128), F32)
    shaped_scratch = pltpu.VMEM((4, 2 * 72 + 16, 128), F32)
    bias_scratch = pltpu.VMEM((2, 2 * HEADS * WIN, 128), F32)
    rows_scratch = pltpu.VMEM((2, TOKENS, 128), F32)
    packed_scratch = pltpu.VMEM((ROWS, 128), BF16)

    quads = call(
        first_kernel,
        (bias_level,),
        (inputs, grad_out, *first_weights, Part(bias_tables, 0)),
        [quad_shape] * 4
        + [
            shape_of(weights_shape, BF16),
            shape_of((2, 3, C, WIN), BF16),
            shape_of((3, TOKENS, C), BF16),
        ],
        [rows_scratch, row_scratch, shaped_scratch, bias_scratch],
        1_000_000_000,
    )
    stored = list(quads[4:])
    ahead = (
        quads[3],
        shifted(quads[2], 0, 1),
        shifted(quads[1], 1, 0),
        shifted(quads[0], 1, 1),
    )
    (bias,) = call(
        prepare_kernel,
        (bias_level,),
        (region.transpose(1, 0, 2), Part(bias_tables, 1)),
        [shape_of(weights_shape, BF16)],
        [row_scratch, shaped_scratch, bias_scratch],
        500_000_000,
    )
    *back, second_keep, second_send, second_scaled = call(
        second_kernel,
        (is_upper,),
        (*ahead, bias, *second_weights),
        [quad_shape] * 4 + [half_shape, half_shape, shape_of(weights_shape, BF16)],
        [pltpu.VMEM(weights_shape, BF16), packed_scratch],
        3_000_000_000,
    )
    home = [
        shifted(back[3], -1, -1),
        shifted(back[2], -1, 0),
        shifted(back[1], 0, -1),
        back[0],
    ]
    home[3], after_second = tie((home[3], is_upper))
    active, slope, *first_near = near_call(
        activation_kernel,
        (after_second,),
        (stored[2], first_weights[0], first_weights[3]),
        [shape_of((TOKENS, FFN), BF16), shape_of((TOKENS, FFN), BF16)],
        [],
        300_000_000,
        (0, 1),
        (*stored, first_weights[0], *first_weights[2:]),
    )
    second_got = exchanged(second_send, core_step()[0])
    first_keep, first_send, grad_rows, first_scaled = near_call(
        third_kernel,
        (is_upper,),
        tuple(map(Near, (*home, *first_near[:3], active, slope, first_near[3], in_weight, *first_near[4:]))),
        [half_shape, half_shape, shape_of((TOKENS, C), BF16), shape_of(weights_shape, BF16)],
        [packed_scratch],
        2_000_000_000,
    )
    blocks_out, grad_inputs = near_call(
        grids_kernel,
        (),
        (*home, grad_rows),
        [grid_shape, grid_shape],
        [rows_scratch],
        100_000_000,
    )

    def collect(kernel, rows, *operands):
        return near_call(
            kernel,
            (bias_level,),
            operands,
            [shape_of((rows, 128), BF16)],
            [row_scratch, shaped_scratch, grads_scratch],
            500_000_000,
        )[0]

    first_got = exchanged(first_send, core_step()[0])
    second = added(second_keep, second_got)
    first = added(first_keep, first_got)
    first, second, first_scaled, second_scaled = tie((first, second, first_scaled, second_scaled))
    second_tables = collect(collect_kernel, TABLE_ROWS, second_scaled)
    tables = collect(finish_kernel, 2 * TABLE_ROWS, first_scaled, second_tables)
    totals = unpack(is_upper, *sum_all(first, second, tables, second_tables))
    gains, grad_in, grad_out_weight, grad_up, grad_down, grad_tables = totals
    return (
        blocks_out.transpose(2, 0, 1, 3),
        grad_inputs.transpose(2, 0, 1, 3),
        gains,
        grad_in,
        grad_out_weight,
        grad_up,
        grad_down.transpose(0, 2, 1),
        grad_tables.transpose(0, 1, 3, 2, 4),
    )


def exchanged(value, mask):
    lon_count, lat_count = lax.axis_size("lon"), lax.axis_size("lat")
    pairs = []
    for lon in range(lon_count):
        for lat in range(lat_count):
            pairs.append(((lon ^ mask[1]) * lat_count + (lat ^ mask[0]), lon * lat_count + lat))
    return lax.ppermute(value, ("lon", "lat"), pairs)


def added(left, right):
    return (left.astype(F32) + right.astype(F32)).astype(BF16)


def odd(mask):
    lat, lon = lax.axis_index("lat") & mask[0], lax.axis_index("lon") & mask[1]
    parity = jnp.int32(0)
    for place in range(5):
        parity = parity ^ (lat >> place) ^ (lon >> place)
    return parity & 1


def split(value, owner):
    half = value.shape[0] // 2
    up = odd(owner) != 0
    return jnp.where(up, value[half:], value[:half]), jnp.where(up, value[:half], value[half:])


def halve(value, mask, owner):
    keep, send = split(value, owner)
    return added(keep, exchanged(send, mask))


def double(value, mask, owner):
    other = exchanged(value, mask)
    up = odd(owner) != 0
    return jnp.concatenate([jnp.where(up, other, value), jnp.where(up, value, other)], axis=0)


def tie(values):
    return lax.optimization_barrier(values)


def core_step():
    return (1, 0), (1, 0)


def sum_all(first, second, tables, second_tables):
    core = core_step()[0]
    if lax.axis_size("lat") != 16 or lax.axis_size("lon") != 16:
        return sum_small(first, second, tables)
    y_low, y_high = ((2, 0), (2, 0)), (0, 8)
    x_low, x_high = ((4, 0), (12, 0)), ((12, 0), (8, 0))
    z_low, z_mid, z_high = ((0, 1), (0, 5)), ((0, 2), (0, 6)), (0, 7)

    first, second = halve(first, *y_low), halve(second, *x_low)
    first, second_tables = tie((first, second_tables))
    first, second = halve(first, *x_low), halve(second, *y_low)
    rows = first.shape[0]
    joined = halve(jnp.concatenate([first, second], axis=0), *x_high)
    joined, tables = tie((joined, tables))
    for mask, owner in (z_low, z_mid):
        keep, send = split(tables, owner)
        got = exchanged(jnp.concatenate([joined, send], axis=0), mask)
        joined, tables = added(joined, got[:rows]), added(keep, got[rows:])
    joined = jnp.concatenate([joined, tables], axis=0)
    for mask in (z_high, y_high):
        joined = added(joined, exchanged(joined, mask))
    joined, tables = tie((joined[:rows], joined[rows:]))
    tables = double(tables, *z_mid)
    joined = double(joined, *x_high)
    first, second = tie((joined[:rows], joined[rows:]))
    first, second = double(first, *x_low), double(second, *y_low)
    first, tables = tie((first, tables))
    first, second = double(first, *y_low), double(second, *x_low)
    tables = double(tables, *z_low)
    first, second, tables = tie((first, second, tables))
    return first, exchanged(first, core), second, exchanged(second, core), tables


def sum_small(first, second, tables):
    def over(value, axis):
        for place in range(lax.axis_size(axis).bit_length() - 1):
            if axis == "lon" or place:
                value = added(value, exchanged(value, (1 << place, 0) if axis == "lat" else (0, 1 << place)))
        return value

    core = core_step()[0]
    first, second = over(over(first, "lat"), "lon"), over(over(second, "lat"), "lon")
    return first, exchanged(first, core), second, exchanged(second, core), over(tables, "lon")


def unpack_kernel(upper_ref, first_own, first_other, second_own, second_other, tables_ref, *refs):
    results, (rows_ref, *buffers, sems) = refs[:6], refs[6:]
    gains_ref, in_ref, out_ref, up_ref, down_ref, grads_ref = buffers
    half = ROWS // 2
    is_upper = jnp.broadcast_to(upper_ref[0] == 1, (1, 128))
    copies = []

    def leave(index, block):
        copy = pltpu.make_async_copy(buffers[index].at[block], results[index].at[block], sems.at[index, block])
        copy.start()
        copies.append(copy)

    for block, (own, other) in enumerate(((first_own, first_other), (second_own, second_other))):

        def rows(start, stop, own=own, other=other):
            if start < half < stop:
                return jnp.concatenate([rows(start, half), rows(half, stop)], axis=0)
            lower = start < half
            start, stop = (start, stop) if lower else (start - half, stop - half)
            mine, theirs = own[start:stop].astype(F32), other[start:stop].astype(F32)
            return jnp.where(is_upper, theirs, mine) if lower else jnp.where(is_upper, mine, theirs)

        for index, (ref, start) in enumerate(((up_ref, 1152), (down_ref, 2304))):
            for part in range(6):
                lanes = slice(part * 128, (part + 1) * 128)
                ref[block, :, lanes] = rows(start + part * C, start + (part + 1) * C)
            leave(3 + index, block)
        for part in range(4):
            in_ref[block, :, part * 128 : (part + 1) * 128] = rows(part * C, (part + 1) * C)
        shared = rows(768, 960)
        in_ref[block, :, 512:] = shared[:, :64]
        leave(1, block)
        out_ref[block, :, :128] = rows(960, 1152)
        out_ref[block, :, 128:] = shared[:, 64:]
        leave(2, block)
        rows_ref[...] = tables_ref[block * TABLE_ROWS : (block + 1) * TABLE_ROWS].astype(F32)
        for slab in range(26):
            width = min(128, RELPOS - slab * 128)
            for level in range(2):
                start = slab * 12 + level * HEADS
                grads_ref[block, 0, :, level, slab * 128 : slab * 128 + width] = rows_ref[start : start + HEADS, :width]
        leave(5, block)
        gains = rows(GAIN_ROWS, GAIN_ROWS + 16)
        gains_ref[block, 0:1, :128] = gains[0:1]
        gains_ref[block, 0:1, 128:] = gains[1:2, :64]
        gains_ref[block, 1:2, :128] = gains[2:3]
        gains_ref[block, 1:2, 128:] = gains[1:2, 64:]
        leave(0, block)
    for copy in copies:
        copy.wait()


def unpack(is_upper, *values):
    shapes = [
        (2, 2, C),
        (2, C, 3 * C),
        (2, C, C),
        (2, C, FFN),
        (2, C, FFN),
        (2, 1, HEADS, 2, RELPOS),
    ]
    return pl.pallas_call(
        unpack_kernel,
        in_specs=[SMEM] + [pl.BlockSpec(memory_space=pltpu.VMEM)] * len(values),
        out_specs=[pl.BlockSpec(memory_space=pl.ANY)] * len(shapes),
        out_shape=[shape_of(shape, F32) for shape in shapes],
        scratch_shapes=[pltpu.VMEM((TABLE_ROWS, 128), F32)]
        + [pltpu.VMEM(shape, F32) for shape in shapes]
        + [pltpu.SemaphoreType.DMA((len(shapes), 2))],
        compiler_params=pltpu.CompilerParams(vmem_limit_bytes=NEAR_LIMIT),
    )(is_upper, *values)


def solution(mesh):
    placed = (
        P(None, "lat", "lon", None),
        P(None, "lat", "lon", None),
        P(None, "lat", "lon"),
        P(None, "lat"),
        P(),
        P(),
        P(),
        P(),
        P(),
        P(None, "lat", None, None, None),
    )
    return jax.shard_map(
        per_device,
        mesh=mesh,
        in_specs=placed,
        out_specs=(
            P(None, "lat", "lon", None),
            P(None, "lat", "lon", None),
            P(),
            P(),
            P(),
            P(),
            P(),
            P(None, "lat", None, None, None),
        ),
        check_vma=False,
    )
```
